256 devices in a mesh: bank: 16 (over z_hi, y, core), group: 16 (over x, z_lo).
Axes of the slice: x: 4, y: 4, z: 8 (z_hi: 2, z_lo: 4; z = z_hi * 4 + z_lo), core: 2. Of those that a mesh axis runs over, the one named last changes fastest.
Arguments:
- source: bfloat16 [32768, 768], P(('bank', 'group'))
- target: bfloat16 [32768, 768], P(('group', 'bank'))
- pairs: int32 [16, 16, 48, 2], P('bank', 'group'), may hold values from 0 to 7, as said below
- counts: int32 [16, 16], P('bank', 'group'), may hold values from 8 to 48, as said below
Outputs:
- row_margin: float32 [16, 16, 48, 256], P('bank', 'group')
- col_margin: float32 [16, 16, 48, 256], P('bank', 'group')
- source_scores: float32 [32768], P(('bank', 'group'))
- target_scores: float32 [32768], P(('group', 'bank'))
The draws below stay inside these ranges and needn't reach their ends.
Inputs may be any that keep to these rules, and one draw needn't show every extreme that they name: Each device's entries are distinct (source block, target block) pairs; source blocks index its bank's source slab, target blocks its group's target slab. Among the first 8 entries of every device each source block and each target block of those slabs appears. Entries beyond the device's count hold valid pairs that are not used. `counts`: some device has exactly 48 live entries in every draw.
All inputs are finite; a program needn't handle non-finite values.
Results may differ from the reference program's by a relative error of at most 0.00046.
Values may be sent and summed in bfloat16 or wider, within the bound.
No kernel may reach another device: no remote copies, remote signals or barrier semaphores. Data moves between devices by JAX's collectives and lax.ppermute only.
A program may use at most 64 MiB of HBM per device.

```python
import math
import jax
import jax.numpy as jnp
from jax import lax

D = 768
BLK = 256
SRC_SLAB = 2048
TGT_SLAB = 2048
SOURCES = 32768
TARGETS = 32768
SRC_BLOCKS = 8
TGT_BLOCKS = 8
CELLS = 64
COVER = 8
PAIRS = 48
N_BANK = 16
N_GROUP = 16


centers_count = 8


def cluster_centers(key):
    return jax.random.normal(jax.random.fold_in(key, 71), (centers_count, D), jnp.float32)


def clustered_rows(key, centers, rows, row_spread):
    k_label = jax.random.fold_in(key, 0)
    k_weight = jax.random.fold_in(key, 1)
    k_normal = jax.random.fold_in(key, 2)
    k_scale = jax.random.fold_in(key, 4)
    label = jax.random.randint(k_label, (rows,), 0, centers_count)
    weight = jnp.exp(jax.random.uniform(k_weight, (rows, 1), jnp.float32, math.log(0.3), math.log(3.0)))
    normal_part = jax.random.normal(k_normal, (rows, D), jnp.float32)
    noise = normal_part
    scale = jnp.exp(jax.random.uniform(k_scale, (rows, 1), jnp.float32, 0.0, math.log(row_spread)))
    return scale * (noise + weight * centers[label])


def draw_source(key, part):
    centers = cluster_centers(key)
    key = jax.random.fold_in(key, 3)
    return clustered_rows(key, centers, SOURCES, 1.0).astype(jnp.bfloat16)


def draw_target(key, part):
    centers = cluster_centers(key)
    key = jax.random.fold_in(key, 4)
    return clustered_rows(key, centers, TARGETS, 1.0).astype(jnp.bfloat16)


def device_pairs(key):
    k_src, k_tgt, k_rest = jax.random.split(key, 3)
    perm_src = jax.random.permutation(k_src, SRC_BLOCKS).astype(jnp.int32)
    perm_tgt = jax.random.permutation(k_tgt, TGT_BLOCKS).astype(jnp.int32)
    leading = jnp.arange(COVER, dtype=jnp.int32)
    cover_cells = perm_src[leading % SRC_BLOCKS] * TGT_BLOCKS + perm_tgt[leading % TGT_BLOCKS]
    ranking = jax.random.permutation(k_rest, CELLS).astype(jnp.int32) + CELLS
    ranking = ranking.at[cover_cells].set(leading)
    order = jnp.argsort(ranking, stable=True)[:PAIRS].astype(jnp.int32)
    return jnp.stack([order // TGT_BLOCKS, order % TGT_BLOCKS], axis=-1)


def draw_pairs(key, part):
    key = jax.random.fold_in(key, 5)
    keys = jax.random.split(key, N_BANK * N_GROUP)
    return jax.vmap(device_pairs)(keys).reshape(N_BANK, N_GROUP, PAIRS, 2)


def draw_counts(key, part):
    key = jax.random.fold_in(key, 7)
    k_load, k_top = jax.random.split(key)
    extra = PAIRS - COVER
    level = jax.random.randint(k_load, (N_BANK * N_GROUP,), 0, extra + 1)
    load = COVER + level * level * level // max(extra * extra, 1)
    busiest = jax.random.randint(k_top, (), 0, N_BANK * N_GROUP)
    load = jnp.where(jnp.arange(N_BANK * N_GROUP) == busiest, PAIRS, load)
    return load.reshape(N_BANK, N_GROUP).astype(jnp.int32)


def setup_inputs(seed: int = 0) -> dict:
    splits = jax.random.split(jax.random.key(seed), 5)
    return {
        "source": draw_source(jax.random.fold_in(splits[4], 71), 0),
        "target": draw_target(jax.random.fold_in(splits[4], 71), 0),
        "pairs": draw_pairs(jax.random.fold_in(splits[4], 71), 0),
        "counts": draw_counts(jax.random.fold_in(splits[4], 71), 0),
    }


TEMP_INV = 20.0

def unit_rows(rows):
    values = rows.astype(jnp.float32)
    width = values.shape[-1]
    scale = lax.rsqrt(lax.optimization_barrier(jnp.mean(values * values, axis=-1, keepdims=True)) + 1e-06)
    return (values * (scale * (1.0 / math.sqrt(width)))).astype(jnp.bfloat16)

def reference(source, target, pairs, counts):
    src = unit_rows(source).reshape(N_BANK, SRC_SLAB, D)
    tgt = unit_rows(target).reshape(N_GROUP, TGT_SLAB, D)
    n_slots = N_BANK * N_GROUP * PAIRS
    flat_pairs = pairs.reshape(n_slots, 2)
    flat_counts = counts.reshape(N_BANK * N_GROUP)
    zero = jnp.int32(0)

    def locate(index):
        device = index // PAIRS
        slot = index % PAIRS
        bank = device // N_GROUP
        group = device % N_GROUP
        return (bank, group, slot < flat_counts[device], flat_pairs[index, 0], flat_pairs[index, 1])

    def make_tile(bank, group, src_block, tgt_block):
        left = lax.dynamic_slice(src, (bank, src_block * BLK, zero), (1, BLK, D))[0]
        right = lax.dynamic_slice(tgt, (group, tgt_block * BLK, zero), (1, BLK, D))[0]
        return jnp.dot(left, right.T, preferred_element_type=jnp.float32)

    def sum_step(carry, index):
        bank, group, valid, src_block, tgt_block = locate(index)

        def add_tile(state):
            rows, cols = state
            weights = jnp.exp(make_tile(bank, group, src_block, tgt_block) * TEMP_INV)
            old_rows = lax.dynamic_slice(rows, (bank, src_block * BLK), (1, BLK))
            rows = lax.dynamic_update_slice(rows, old_rows + weights.sum(1)[None], (bank, src_block * BLK))
            old_cols = lax.dynamic_slice(cols, (group, tgt_block * BLK), (1, BLK))
            cols = lax.dynamic_update_slice(cols, old_cols + weights.sum(0)[None], (group, tgt_block * BLK))
            return (rows, cols)

        def keep_state(state):
            return state
        return (lax.cond(valid, add_tile, keep_state, carry), None)
    start = (jnp.zeros((N_BANK, SRC_SLAB), jnp.float32), jnp.zeros((N_GROUP, TGT_SLAB), jnp.float32))
    indices = jnp.arange(n_slots, dtype=jnp.int32)
    (src_total, tgt_total), _ = lax.scan(sum_step, start, indices)
    src_score = jnp.log(src_total)
    tgt_score = jnp.log(tgt_total)

    def margin_step(index):
        bank, group, valid, src_block, tgt_block = locate(index)

        def live(operand):
            scores = make_tile(bank, group, src_block, tgt_block)
            src_part = lax.dynamic_slice(src_score, (bank, src_block * BLK), (1, BLK))[0]
            tgt_part = lax.dynamic_slice(tgt_score, (group, tgt_block * BLK), (1, BLK))[0]
            margin = scores * TEMP_INV - 0.5 * (src_part[:, None] + tgt_part[None, :])
            return (margin.max(1), margin.max(0))

        def empty(operand):
            return (jnp.zeros((BLK,), jnp.float32), jnp.zeros((BLK,), jnp.float32))
        return lax.cond(valid, live, empty, 0)
    row_best, col_best = lax.map(margin_step, indices)
    return (row_best.reshape(N_BANK, N_GROUP, PAIRS, BLK), col_best.reshape(N_BANK, N_GROUP, PAIRS, BLK), src_score.reshape(SOURCES), tgt_score.reshape(TARGETS))
```

```python
import math

import jax
import jax.numpy as jnp
from jax import lax
from jax.experimental import pallas as pl
from jax.experimental.pallas import tpu as pltpu
from jax.sharding import Mesh
from jax.sharding import PartitionSpec as P

BLK = 256
HALF = 128
SLOTS = 48
BLOCKS = 8
SHARDS = 16
TEMP_INV = 20.0
EXP2_SCALE = TEMP_INV * math.log2(math.e)
HALF_TEMP = 0.5 / TEMP_INV
NT = (((1,), (1,)), ((), ()))
AXES = ("zh", "y", "c", "x", "zl")
BANK = ("zh", "y", "c")
GROUP = ("x", "zl")


def unit_rows(rows):
    values = rows.astype(jnp.float32)
    width = values.shape[-1]
    scale = lax.rsqrt(jnp.mean(values * values, axis=-1, keepdims=True) + 1e-06)
    return (values * (scale * (1.0 / math.sqrt(width)))).astype(jnp.bfloat16)


def ring(n, step):
    return [(i, (i + step) % n) for i in range(n)]


SRC_PLACE = {}
for dz in range(4):
    SRC_PLACE[(0, dz)] = (0, dz)
    SRC_PLACE[(1, dz)] = (1, dz)
    SRC_PLACE[(3, dz)] = (2, dz)
    SRC_PLACE[(2, dz)] = (3, dz) if dz < 2 else (4, dz - 2)
TGT_PLACE = {}
for dh in range(2):
    for dc in range(2):
        TGT_PLACE[(dh, 0, dc)] = (0, dc, dh)
        TGT_PLACE[(dh, 1, dc)] = (1, dc, dh)
        TGT_PLACE[(dh, 3, dc)] = (2, dc, dh)
        TGT_PLACE[(dh, 2, dc)] = (3, dc, dh)


def load_slabs(meta, src_parts, tgt_parts, src, tgt, sems):
    zh, y, c, x, zl = (meta[k] for k in range(1, 6))
    copies = []
    for (dx, dz), (part, row) in SRC_PLACE.items():
        shard = lax.rem(x - dx + 4, 4) * 4 + lax.rem(zl - dz + 4, 4)
        dst = src.at[pl.ds(pl.multiple_of(shard * HALF, HALF), HALF)]
        copies.append(
            pltpu.make_async_copy(src_parts[part].at[row], dst, sems.at[len(copies)])
        )
    for (dh, dy, dc), (part, core, row) in TGT_PLACE.items():
        shard = lax.rem(zh + dh, 2) * 8 + lax.rem(y - dy + 4, 4) * 2 + lax.rem(c + dc, 2)
        dst = tgt.at[pl.ds(pl.multiple_of(shard * HALF, HALF), HALF)]
        copies.append(
            pltpu.make_async_copy(
                tgt_parts[4 * core + part].at[row], dst, sems.at[len(copies)]
            )
        )
    for copy in copies:
        copy.start()
    for copy in copies:
        copy.wait()


def slot(pairs, p):
    q = jnp.minimum(p, SLOTS - 1)
    return pairs[2 * q], pairs[2 * q + 1]


def tile(pairs, p, src, tgt, out):
    i, j = slot(pairs, p)
    left = src[pl.ds(pl.multiple_of(i * BLK, BLK), BLK), :]
    right = tgt[pl.ds(pl.multiple_of(j * BLK, BLK), BLK), :]
    out[...] = lax.dot_general(left, right, NT, preferred_element_type=jnp.float32)


def each_tile(count, compute, use, b0, b1):
    compute(0, b0)

    def body(k, carry):
        compute(2 * k + 1, b1)
        use(2 * k, b0)
        compute(2 * k + 2, b0)
        use(2 * k + 1, b1)
        return carry

    lax.fori_loop(0, (count + 1) // 2, body, 0)


def sums_kernel(meta, pairs, *refs):
    src_parts, tgt_parts = refs[:5], refs[5:13]
    row_out, col_out, src, tgt, acc_row, acc_col, b0, b1, sems = refs[13:]
    count = meta[0]
    load_slabs(meta, src_parts, tgt_parts, src, tgt, sems)
    acc_row[...] = jnp.zeros_like(acc_row)
    acc_col[...] = jnp.zeros_like(acc_col)

    def use(p, buf):
        i, j = slot(pairs, p)
        i = jnp.where(p < count, i, BLOCKS)
        j = jnp.where(p < count, j, BLOCKS)
        w = jnp.exp2(buf[...] * EXP2_SCALE)
        rows = pl.ds(pl.multiple_of(i * BLK, BLK), BLK)
        acc_row[rows, :] += w[:, :HALF] + w[:, HALF:]
        acc_col[j] += w.reshape(BLK // 8, 8, BLK).sum(0)

    each_tile(count, lambda p, buf: tile(pairs, p, src, tgt, buf), use, b0, b1)
    rows = [
        jnp.sum(acc_row[h * HALF : (h + 1) * HALF, :].T, axis=0, keepdims=True)
        for h in range(SHARDS)
    ]
    row_out[...] = jnp.broadcast_to(jnp.concatenate(rows, 0)[None], row_out.shape)
    cols = []
    for j in range(BLOCKS):
        col = jnp.sum(acc_col[j], axis=0, keepdims=True)
        cols += [col[:, :HALF], col[:, HALF:]]
    col_out[...] = jnp.broadcast_to(jnp.concatenate(cols, 0)[None], col_out.shape)


def margin_kernel(meta, pairs, row_all, col_all, *refs):
    src_parts, tgt_parts = refs[:5], refs[5:13]
    (row_best, col_best, src_piece, tgt_piece,
     src, tgt, s16, t16, s_cols, b0, b1, sems) = refs[13:]
    count = meta[0]
    load_slabs(meta, src_parts, tgt_parts, src, tgt, sems)
    s16[...] = jnp.log(jnp.sum(row_all[...], axis=0)) * HALF_TEMP
    t16[...] = jnp.log(jnp.sum(col_all[...], axis=0)) * HALF_TEMP
    row_best[...] = jnp.zeros_like(row_best)
    col_best[...] = jnp.zeros_like(col_best)
    for h in range(SHARDS):
        s_cols[h * HALF : (h + 1) * HALF, :] = jnp.broadcast_to(
            s16[h : h + 1, :], (HALF, HALF)
        ).T
    src_piece[...] = s16[pl.ds(meta[6], 1), :] * (2 * TEMP_INV)
    tgt_piece[...] = t16[pl.ds(meta[7], 1), :] * (2 * TEMP_INV)

    def use(p, buf):
        i, j = slot(pairs, p)
        ta, tb = t16[pl.ds(2 * j, 1), :], t16[pl.ds(2 * j + 1, 1), :]
        sa, sb = s16[pl.ds(2 * i, 1), :], s16[pl.ds(2 * i + 1, 1), :]
        sc = s_cols[pl.ds(pl.multiple_of(i * BLK, BLK), BLK), :]
        ua, ub = buf[:, :HALF], buf[:, HALF:]
        best = jnp.maximum(ua - ta, ub - tb)
        ra = jnp.max(best[:HALF].T, axis=0, keepdims=True)
        rb = jnp.max(best[HALF:].T, axis=0, keepdims=True)
        ca = jnp.max(ua - sc, axis=0, keepdims=True)
        cb = jnp.max(ub - sc, axis=0, keepdims=True)
        dest = jnp.where(p < count, p, SLOTS)
        row_best[dest] = jnp.concatenate([ra - sa, rb - sb], 1) * TEMP_INV
        col_best[dest] = jnp.concatenate([ca - ta, cb - tb], 1) * TEMP_INV

    each_tile(count, lambda p, buf: tile(pairs, p, src, tgt, buf), use, b0, b1)


VMEM = pl.BlockSpec(memory_space=pltpu.VMEM)
SMEM = pl.BlockSpec(memory_space=pltpu.SMEM)
ANY = pl.BlockSpec(memory_space=pl.ANY)


def per_device(source, target, pairs, counts):
    zh, y, c, x, zl = (lax.axis_index(a) for a in AXES)
    my_pairs = pairs.reshape(-1)
    width = source.shape[1]

    own_t = unit_rows(target)
    own_s = unit_rows(source)
    pair_t = jnp.stack([own_t, lax.ppermute(own_t, "zh", ring(2, 1))])
    quad_s = jnp.stack([own_s] + [lax.ppermute(own_s, "zl", ring(4, k)) for k in (1, 2, 3)])
    t_up = lax.ppermute(pair_t, "y", ring(4, 1))
    t_down = lax.ppermute(pair_t, "y", ring(4, -1))
    s_up = lax.ppermute(quad_s, "x", ring(4, 1))
    s_down = lax.ppermute(quad_s, "x", ring(4, -1))
    t_far = jnp.concatenate(
        [
            lax.ppermute(t_up[:1], "y", ring(4, 1)),
            lax.ppermute(t_down[1:], "y", ring(4, -1)),
        ]
    )
    s_far_a = lax.ppermute(s_up[:2], "x", ring(4, 1))
    s_far_b = lax.ppermute(s_down[2:], "x", ring(4, -1))
    t_mine = [pair_t, t_up, t_down, t_far]
    t_other = [lax.ppermute(v, "c", ring(2, 1)) for v in t_mine]
    slabs = [quad_s, s_up, s_down, s_far_a, s_far_b] + t_mine + t_other

    meta = jnp.stack(
        [counts[0, 0], zh, y, c, x, zl, x * 4 + zl, zh * 8 + y * 2 + c]
    ).astype(jnp.int32)
    f32 = lambda *shape: jax.ShapeDtypeStruct(shape, jnp.float32)
    slab_scratch = [
        pltpu.VMEM((BLOCKS * BLK, width), jnp.bfloat16),
        pltpu.VMEM((BLOCKS * BLK, width), jnp.bfloat16),
    ]
    tile_scratch = [pltpu.VMEM((BLK, BLK), jnp.float32)] * 2 + [
        pltpu.SemaphoreType.DMA((2 * SHARDS,))
    ]
    row_sums, col_sums = pl.pallas_call(
        sums_kernel,
        out_shape=(f32(SHARDS, SHARDS, HALF), f32(SHARDS, SHARDS, HALF)),
        in_specs=[SMEM, SMEM] + [ANY] * 13,
        out_specs=(VMEM, VMEM),
        scratch_shapes=slab_scratch
        + [
            pltpu.VMEM(((BLOCKS + 1) * BLK, HALF), jnp.float32),
            pltpu.VMEM((BLOCKS + 1, 8, BLK), jnp.float32),
        ]
        + tile_scratch,
        compiler_params=pltpu.CompilerParams(vmem_limit_bytes=32 * 1024 * 1024),
        name="sums",
    )(meta, my_pairs, *slabs)
    row_all = lax.all_to_all(row_sums, GROUP, 0, 0, tiled=True)
    col_all = lax.all_to_all(col_sums, BANK, 0, 0, tiled=True)
    row_best, col_best, src_piece, tgt_piece = pl.pallas_call(
        margin_kernel,
        out_shape=(
            f32(SLOTS + 1, 1, BLK),
            f32(SLOTS + 1, 1, BLK),
            f32(1, HALF),
            f32(1, HALF),
        ),
        in_specs=[SMEM, SMEM, VMEM, VMEM] + [ANY] * 13,
        out_specs=(VMEM,) * 4,
        scratch_shapes=slab_scratch
        + [
            pltpu.VMEM((SHARDS, HALF), jnp.float32),
            pltpu.VMEM((SHARDS, HALF), jnp.float32),
            pltpu.VMEM((BLOCKS * BLK, HALF), jnp.float32),
        ]
        + tile_scratch,
        compiler_params=pltpu.CompilerParams(vmem_limit_bytes=32 * 1024 * 1024),
        name="margins",
    )(meta, my_pairs, row_all, col_all, *slabs)
    return (
        row_best[:SLOTS].reshape(1, 1, SLOTS, BLK),
        col_best[:SLOTS].reshape(1, 1, SLOTS, BLK),
        src_piece.reshape(HALF),
        tgt_piece.reshape(HALF),
    )


def solution(mesh):
    fine = Mesh(mesh.devices.reshape(2, 4, 2, 4, 4), AXES)
    src_axes, tgt_axes = AXES, GROUP + BANK
    return jax.shard_map(
        per_device,
        mesh=fine,
        in_specs=(
            P(src_axes, None),
            P(tgt_axes, None),
            P(BANK, GROUP, None, None),
            P(BANK, GROUP),
        ),
        out_specs=(
            P(BANK, GROUP, None, None),
            P(BANK, GROUP, None, None),
            P(src_axes),
            P(tgt_axes),
        ),
        check_vma=False,
    )
```

```python
import math

import jax
import jax.numpy as jnp
from jax import lax
from jax.experimental import pallas as pl
from jax.experimental.pallas import tpu as pltpu
from jax.sharding import Mesh
from jax.sharding import PartitionSpec as P

BLK = 256
HALF = 128
SLOTS = 48
BLOCKS = 8
SHARDS = 16
TEMP_INV = 20.0
EXP2_SCALE = TEMP_INV * math.log2(math.e)
HALF_TEMP = 0.5 / TEMP_INV
NT = (((1,), (1,)), ((), ()))
AXES = ("zh", "y", "c", "x", "zl")
BANK = ("zh", "y", "c")
GROUP = ("x", "zl")


def unit_rows(rows):
    values = rows.astype(jnp.float32)
    width = values.shape[-1]
    scale = lax.rsqrt(jnp.mean(values * values, axis=-1, keepdims=True) + 1e-06)
    return (values * (scale * (1.0 / math.sqrt(width)))).astype(jnp.bfloat16)


def ring(n, step):
    return [(i, (i + step) % n) for i in range(n)]


GROUP_TILES = 8

SRC_PLACE = {(0, 0, 0): (0, 0, 128), (1, 0, 0): (1, 0, 128), (3, 0, 0): (2, 0, 128), (2, 0, 0): (3, 0, 128)}
for dz in (1, 2, 3):
    SRC_PLACE[(0, dz, 0)] = (4, 128 * dz - 128, 128)
    SRC_PLACE[(1, dz, 0)] = (5, 128 * dz - 128, 128)
    SRC_PLACE[(3, dz, 0)] = (6, 128 * dz - 128, 128)
SRC_PLACE[(2, 1, 0)] = (7, 0, 128)
SRC_PLACE[(2, 2, 0)] = (7, 128, 64)
SRC_PLACE[(2, 2, 64)] = (8, 0, 64)
SRC_PLACE[(2, 3, 0)] = (8, 64, 128)
SRC_PARTS = 9
TGT_PLACE = {}
for dh in range(2):
    for dc in range(2):
        for slot_y, dy in enumerate((0, 1, 3, 2)):
            TGT_PLACE[(dh, dy, dc)] = (2 * dh + dc, 128 * slot_y)
TGT_PARTS = 4
PARTS = SRC_PARTS + TGT_PARTS
COPIES = len(SRC_PLACE) + len(TGT_PLACE)


def load_slabs(meta, parts, src, tgt, sems):
    zh, y, c, x, zl = (meta[k] for k in range(1, 6))
    copies = []

    def add(part, first, rows, slab, place):
        copies.append(
            pltpu.make_async_copy(
                parts[part].at[pl.ds(first, rows)],
                slab.at[pl.ds(pl.multiple_of(place, 64), rows)],
                sems.at[len(copies)],
            )
        )

    for (dx, dz, offset), (part, first, rows) in SRC_PLACE.items():
        shard = lax.rem(x - dx + 4, 4) * 4 + lax.rem(zl - dz + 4, 4)
        add(part, first, rows, src, shard * HALF + offset)
    for (dh, dy, dc), (part, first) in TGT_PLACE.items():
        shard = lax.rem(zh + dh, 2) * 8 + lax.rem(y - dy + 4, 4) * 2 + lax.rem(c + dc, 2)
        add(SRC_PARTS + part, first, HALF, tgt, shard * HALF)
    for copy in copies:
        copy.start()
    for copy in copies:
        copy.wait()


def sums_kernel(meta, pairs, *refs):
    row_out, col_out, tiles_out, src, tgt, acc_row, acc_col, tiles, sems, out_sems = refs[PARTS:]
    count = meta[0]
    load_slabs(meta, refs[:PARTS], src, tgt, sems)
    acc_row[...] = jnp.zeros_like(acc_row)
    acc_col[...] = jnp.zeros_like(acc_col)
    groups = (count + GROUP_TILES - 1) // GROUP_TILES

    def copy_out(k):
        some = pl.ds(k * GROUP_TILES, GROUP_TILES)
        return pltpu.make_async_copy(tiles.at[some], tiles_out.at[some], out_sems.at[k])

    def group(k, carry):
        for u in range(GROUP_TILES):
            p = k * GROUP_TILES + u
            i, j = pairs[2 * p], pairs[2 * p + 1]
            left = src[pl.ds(pl.multiple_of(i * BLK, BLK), BLK), :]
            right = tgt[pl.ds(pl.multiple_of(j * BLK, BLK), BLK), :]
            scores = lax.dot_general(left, right, NT, preferred_element_type=jnp.float32)
            tiles[p] = scores
            i = jnp.where(p < count, i, BLOCKS)
            j = jnp.where(p < count, j, BLOCKS)
            w = jnp.exp2(scores * EXP2_SCALE)
            rows = pl.ds(pl.multiple_of(i * BLK, BLK), BLK)
            acc_row[rows, :] += w[:, :HALF] + w[:, HALF:]
            acc_col[j] += w.reshape(BLK // 8, 8, BLK).sum(0)
        copy_out(k).start()
        return carry

    lax.fori_loop(0, groups, group, 0)
    rows = [
        jnp.sum(acc_row[h * HALF : (h + 1) * HALF, :].T, axis=0, keepdims=True)
        for h in range(SHARDS)
    ]
    row_out[...] = jnp.broadcast_to(jnp.concatenate(rows, 0)[None], row_out.shape)
    cols = []
    for j in range(BLOCKS):
        col = jnp.sum(acc_col[j], axis=0, keepdims=True)
        cols += [col[:, :HALF], col[:, HALF:]]
    col_out[...] = jnp.broadcast_to(jnp.concatenate(cols, 0)[None], col_out.shape)

    def finish(k, carry):
        copy_out(k).wait()
        return carry

    lax.fori_loop(0, groups, finish, 0)


def margin_kernel(meta, pairs, row_all, col_all, tiles_in, row_best, col_best, src_piece, tgt_piece,
                  s16, t16, s_cols, tiles, in_sems):
    count = meta[0]
    groups = (count + GROUP_TILES - 1) // GROUP_TILES

    def copy_in(k):
        some = pl.ds(k * GROUP_TILES, GROUP_TILES)
        return pltpu.make_async_copy(tiles_in.at[some], tiles.at[some], in_sems.at[k])

    def begin(k, carry):
        copy_in(k).start()
        return carry

    lax.fori_loop(0, groups, begin, 0)
    s16[...] = jnp.log(jnp.sum(row_all[...], axis=0)) * HALF_TEMP
    t16[...] = jnp.log(jnp.sum(col_all[...], axis=0)) * HALF_TEMP
    row_best[...] = jnp.zeros_like(row_best)
    col_best[...] = jnp.zeros_like(col_best)
    for h in range(SHARDS):
        s_cols[h * HALF : (h + 1) * HALF, :] = jnp.broadcast_to(
            s16[h : h + 1, :], (HALF, HALF)
        ).T
    src_piece[...] = s16[pl.ds(meta[6], 1), :] * (2 * TEMP_INV)
    tgt_piece[...] = t16[pl.ds(meta[7], 1), :] * (2 * TEMP_INV)

    def group(k, carry):
        copy_in(k).wait()
        for u in range(GROUP_TILES):
            p = k * GROUP_TILES + u
            i, j = pairs[2 * p], pairs[2 * p + 1]
            ta, tb = t16[pl.ds(2 * j, 1), :], t16[pl.ds(2 * j + 1, 1), :]
            sa, sb = s16[pl.ds(2 * i, 1), :], s16[pl.ds(2 * i + 1, 1), :]
            sc = s_cols[pl.ds(pl.multiple_of(i * BLK, BLK), BLK), :]
            scores = tiles[p]
            ua, ub = scores[:, :HALF], scores[:, HALF:]
            best = jnp.maximum(ua - ta, ub - tb)
            ra = jnp.max(best[:HALF].T, axis=0, keepdims=True)
            rb = jnp.max(best[HALF:].T, axis=0, keepdims=True)
            ca = jnp.max(ua - sc, axis=0, keepdims=True)
            cb = jnp.max(ub - sc, axis=0, keepdims=True)
            dest = jnp.where(p < count, p, SLOTS)
            row_best[dest] = jnp.concatenate([ra - sa, rb - sb], 1) * TEMP_INV
            col_best[dest] = jnp.concatenate([ca - ta, cb - tb], 1) * TEMP_INV
        return carry

    lax.fori_loop(0, groups, group, 0)


VMEM = pl.BlockSpec(memory_space=pltpu.VMEM)
SMEM = pl.BlockSpec(memory_space=pltpu.SMEM)
ANY = pl.BlockSpec(memory_space=pl.ANY)
HBM = pl.BlockSpec(memory_space=pltpu.HBM)


def per_device(source, target, pairs, counts):
    zh, y, c, x, zl = (lax.axis_index(a) for a in AXES)
    my_pairs = pairs.reshape(-1)
    width = source.shape[1]

    own_s = unit_rows(source)
    own_t = unit_rows(target)
    near = [lax.ppermute(own_s, "zl", ring(4, k)) for k in (1, 2, 3)]
    far_t = lax.ppermute(own_t, "zh", ring(2, 1))
    s_own = [own_s] + [lax.ppermute(own_s, "x", ring(4, k)) for k in (1, -1, 2)]
    t_own = jnp.concatenate([own_t] + [lax.ppermute(own_t, "y", ring(4, k)) for k in (1, -1, 2)])
    rest = jnp.concatenate(near)
    up = lax.ppermute(rest, "x", ring(4, 1))
    down = lax.ppermute(rest, "x", ring(4, -1))
    t_far = jnp.concatenate([far_t] + [lax.ppermute(far_t, "y", ring(4, k)) for k in (1, -1, 2)])
    up_far = lax.ppermute(up[:192], "x", ring(4, 1))
    down_far = lax.ppermute(down[192:], "x", ring(4, -1))
    parts = s_own + [rest, up, down, up_far, down_far]
    parts += [t_own, lax.ppermute(t_own, "c", ring(2, 1)), t_far, lax.ppermute(t_far, "c", ring(2, 1))]

    meta = jnp.stack(
        [counts[0, 0], zh, y, c, x, zl, x * 4 + zl, zh * 8 + y * 2 + c]
    ).astype(jnp.int32)
    f32 = lambda *shape: jax.ShapeDtypeStruct(shape, jnp.float32)
    params = pltpu.CompilerParams(vmem_limit_bytes=40 * 1024 * 1024)
    slab = pltpu.VMEM((BLOCKS * BLK, width), jnp.bfloat16)
    tile_store = pltpu.VMEM((SLOTS, BLK, BLK), jnp.float32)
    group_sems = pltpu.SemaphoreType.DMA((SLOTS // GROUP_TILES,))
    row_sums, col_sums, tiles = pl.pallas_call(
        sums_kernel,
        out_shape=(f32(SHARDS, SHARDS, HALF), f32(SHARDS, SHARDS, HALF), f32(SLOTS, BLK, BLK)),
        in_specs=[SMEM, SMEM] + [ANY] * PARTS,
        out_specs=(VMEM, VMEM, HBM),
        scratch_shapes=[
            slab,
            slab,
            pltpu.VMEM(((BLOCKS + 1) * BLK, HALF), jnp.float32),
            pltpu.VMEM((BLOCKS + 1, 8, BLK), jnp.float32),
            tile_store,
            pltpu.SemaphoreType.DMA((COPIES,)),
            group_sems,
        ],
        compiler_params=params,
        name="sums",
    )(meta, my_pairs, *parts)
    row_all = lax.all_to_all(row_sums, GROUP, 0, 0, tiled=True)
    col_all = lax.all_to_all(col_sums, BANK, 0, 0, tiled=True)
    row_best, col_best, src_piece, tgt_piece = pl.pallas_call(
        margin_kernel,
        out_shape=(f32(SLOTS + 1, 1, BLK), f32(SLOTS + 1, 1, BLK), f32(1, HALF), f32(1, HALF)),
        in_specs=[SMEM, SMEM, VMEM, VMEM, HBM],
        out_specs=(VMEM,) * 4,
        scratch_shapes=[
            pltpu.VMEM((SHARDS, HALF), jnp.float32),
            pltpu.VMEM((SHARDS, HALF), jnp.float32),
            pltpu.VMEM((BLOCKS * BLK, HALF), jnp.float32),
            tile_store,
            group_sems,
        ],
        compiler_params=params,
        name="margins",
    )(meta, my_pairs, row_all, col_all, tiles)
    return (
        row_best[:SLOTS].reshape(1, 1, SLOTS, BLK),
        col_best[:SLOTS].reshape(1, 1, SLOTS, BLK),
        src_piece.reshape(HALF),
        tgt_piece.reshape(HALF),
    )


def solution(mesh):
    fine = Mesh(mesh.devices.reshape(2, 4, 2, 4, 4), AXES)
    src_axes, tgt_axes = AXES, GROUP + BANK
    return jax.shard_map(
        per_device,
        mesh=fine,
        in_specs=(
            P(src_axes, None),
            P(tgt_axes, None),
            P(BANK, GROUP, None, None),
            P(BANK, GROUP),
        ),
        out_specs=(
            P(BANK, GROUP, None, None),
            P(BANK, GROUP, None, None),
            P(src_axes),
            P(tgt_axes),
        ),
        check_vma=False,
    )
```

```python
import math

import jax
import jax.numpy as jnp
from jax import lax
from jax.experimental import pallas as pl
from jax.experimental.pallas import tpu as pltpu
from jax.sharding import Mesh
from jax.sharding import PartitionSpec as P

BLK = 256
HALF = 128
SLOTS = 48
BLOCKS = 8
SHARDS = 16
TEMP_INV = 20.0
EXP2_SCALE = TEMP_INV * math.log2(math.e)
HALF_TEMP = 0.5 / TEMP_INV
NT = (((1,), (1,)), ((), ()))
AXES = ("zh", "y", "c", "x", "zl")
BANK = ("zh", "y", "c")
GROUP = ("x", "zl")


def unit_rows(rows):
    values = rows.astype(jnp.float32)
    width = values.shape[-1]
    scale = lax.rsqrt(jnp.mean(values * values, axis=-1, keepdims=True) + 1e-06)
    return (values * (scale * (1.0 / math.sqrt(width)))).astype(jnp.bfloat16)


def ring(n, step):
    return [(i, (i + step) % n) for i in range(n)]


GROUP_TILES = 8

SRC_PLACE = {(0, 0, 0): (0, 0, 128), (1, 0, 0): (1, 0, 128), (3, 0, 0): (2, 0, 128), (2, 0, 0): (3, 0, 128)}
for dz in (1, 2, 3):
    SRC_PLACE[(0, dz, 0)] = (4, 128 * dz - 128, 128)
    SRC_PLACE[(1, dz, 0)] = (5, 128 * dz - 128, 128)
    SRC_PLACE[(3, dz, 0)] = (6, 128 * dz - 128, 128)
SRC_PLACE[(2, 1, 0)] = (7, 0, 128)
SRC_PLACE[(2, 2, 0)] = (7, 128, 64)
SRC_PLACE[(2, 2, 64)] = (8, 0, 64)
SRC_PLACE[(2, 3, 0)] = (8, 64, 128)
SRC_PARTS = 9
TGT_PLACE = {}
for dh in range(2):
    for dc in range(2):
        for slot_y, dy in enumerate((0, 1, 3, 2)):
            TGT_PLACE[(dh, dy, dc)] = (2 * dh + dc, 128 * slot_y)
TGT_PARTS = 4
PARTS = SRC_PARTS + TGT_PARTS


def load_slabs(meta, parts, src, tgt):
    zh, y, c, x, zl = (meta[k] for k in range(1, 6))

    def add(part, first, rows, slab, place):
        slab[pl.ds(pl.multiple_of(place, 64), rows), :] = parts[part][first : first + rows, :]

    for (dx, dz, offset), (part, first, rows) in SRC_PLACE.items():
        shard = lax.rem(x - dx + 4, 4) * 4 + lax.rem(zl - dz + 4, 4)
        add(part, first, rows, src, shard * HALF + offset)
    for (dh, dy, dc), (part, first) in TGT_PLACE.items():
        shard = lax.rem(zh + dh, 2) * 8 + lax.rem(y - dy + 4, 4) * 2 + lax.rem(c + dc, 2)
        add(SRC_PARTS + part, first, HALF, tgt, shard * HALF)


def sums_kernel(meta, pairs, *refs):
    row_out, col_out, tiles, src, tgt, acc_row, acc_col = refs[PARTS:]
    count = meta[0]
    load_slabs(meta, refs[:PARTS], src, tgt)
    acc_row[...] = jnp.zeros_like(acc_row)
    acc_col[...] = jnp.zeros_like(acc_col)

    def group(k, carry):
        for u in range(GROUP_TILES):
            p = k * GROUP_TILES + u
            i, j = pairs[2 * p], pairs[2 * p + 1]
            left = src[pl.ds(pl.multiple_of(i * BLK, BLK), BLK), :]
            right = tgt[pl.ds(pl.multiple_of(j * BLK, BLK), BLK), :]
            scores = lax.dot_general(left, right, NT, preferred_element_type=jnp.float32)
            tiles[p] = scores
            i = jnp.where(p < count, i, BLOCKS)
            j = jnp.where(p < count, j, BLOCKS)
            w = jnp.exp2(scores * EXP2_SCALE)
            rows = pl.ds(pl.multiple_of(i * BLK, BLK), BLK)
            acc_row[rows, :] += w[:, :HALF] + w[:, HALF:]
            acc_col[j] += w.reshape(BLK // 8, 8, BLK).sum(0)
        return carry

    lax.fori_loop(0, (count + GROUP_TILES - 1) // GROUP_TILES, group, 0)
    rows = [
        jnp.sum(acc_row[h * HALF : (h + 1) * HALF, :].T, axis=0, keepdims=True)
        for h in range(SHARDS)
    ]
    row_out[...] = jnp.broadcast_to(jnp.concatenate(rows, 0)[None], row_out.shape)
    cols = []
    for j in range(BLOCKS):
        col = jnp.sum(acc_col[j], axis=0, keepdims=True)
        cols += [col[:, :HALF], col[:, HALF:]]
    col_out[...] = jnp.concatenate(cols, 0)


def margin_kernel(meta, pairs, row_all, col_all, tiles, row_best, col_best, src_piece, tgt_piece,
                  s16, t16, s_cols):
    count = meta[0]
    s16[...] = jnp.log(jnp.sum(row_all[...], axis=0)) * HALF_TEMP
    t16[...] = jnp.log(jnp.sum(col_all[...], axis=0)) * HALF_TEMP
    row_best[...] = jnp.zeros_like(row_best)
    col_best[...] = jnp.zeros_like(col_best)
    for h in range(SHARDS):
        s_cols[h * HALF : (h + 1) * HALF, :] = jnp.broadcast_to(
            s16[h : h + 1, :], (HALF, HALF)
        ).T
    src_piece[...] = s16[pl.ds(meta[6], 1), :] * (2 * TEMP_INV)
    tgt_piece[...] = t16[pl.ds(meta[7], 1), :] * (2 * TEMP_INV)

    def group(k, carry):
        row_rows, col_rows = [], []
        for u in range(GROUP_TILES):
            p = k * GROUP_TILES + u
            i, j = pairs[2 * p], pairs[2 * p + 1]
            ta, tb = t16[pl.ds(2 * j, 1), :], t16[pl.ds(2 * j + 1, 1), :]
            sa, sb = s16[pl.ds(2 * i, 1), :], s16[pl.ds(2 * i + 1, 1), :]
            sc = s_cols[pl.ds(pl.multiple_of(i * BLK, BLK), BLK), :]
            scores = tiles[p]
            ua, ub = scores[:, :HALF], scores[:, HALF:]
            best = jnp.maximum(ua - ta, ub - tb)
            ra = jnp.max(best[:HALF].T, axis=0, keepdims=True)
            rb = jnp.max(best[HALF:].T, axis=0, keepdims=True)
            ca = jnp.max(ua - sc, axis=0, keepdims=True)
            cb = jnp.max(ub - sc, axis=0, keepdims=True)
            live = p < count
            row_rows.append(jnp.where(live, jnp.concatenate([ra - sa, rb - sb], 1), 0.0))
            col_rows.append(jnp.where(live, jnp.concatenate([ca - ta, cb - tb], 1), 0.0))
        some = pl.ds(pl.multiple_of(k * GROUP_TILES, GROUP_TILES), GROUP_TILES)
        row_best[some, :] = jnp.concatenate(row_rows, 0) * TEMP_INV
        col_best[some, :] = jnp.concatenate(col_rows, 0) * TEMP_INV
        return carry

    lax.fori_loop(0, (count + GROUP_TILES - 1) // GROUP_TILES, group, 0)


VMEM = pl.BlockSpec(memory_space=pltpu.VMEM)
SMEM = pl.BlockSpec(memory_space=pltpu.SMEM)


F32 = lambda *shape: jax.ShapeDtypeStruct(shape, jnp.float32)
PARAMS = pltpu.CompilerParams(vmem_limit_bytes=20 * 1024 * 1024)


def sums(meta, pairs, parts):
    slab = pltpu.VMEM((BLOCKS * BLK, parts[0].shape[1]), jnp.bfloat16)
    return pl.pallas_call(
        sums_kernel,
        out_shape=(
            F32(SHARDS, SHARDS, HALF),
            F32(SHARDS, HALF),
            pltpu.VMEM((SLOTS, BLK, BLK), jnp.float32),
        ),
        in_specs=[SMEM, SMEM] + [VMEM] * PARTS,
        out_specs=(VMEM, VMEM, VMEM),
        scratch_shapes=[
            slab,
            slab,
            pltpu.VMEM(((BLOCKS + 1) * BLK, HALF), jnp.float32),
            pltpu.VMEM((BLOCKS + 1, 8, BLK), jnp.float32),
        ],
        compiler_params=PARAMS,
        name="sums",
    )(meta, pairs, *parts)


def margins(meta, pairs, row_all, col_all, tiles):
    return pl.pallas_call(
        margin_kernel,
        out_shape=(F32(SLOTS, BLK), F32(SLOTS, BLK), F32(1, HALF), F32(1, HALF)),
        in_specs=[SMEM, SMEM, VMEM, VMEM, VMEM],
        out_specs=(VMEM,) * 4,
        scratch_shapes=[
            pltpu.VMEM((SHARDS, HALF), jnp.float32),
            pltpu.VMEM((SHARDS, HALF), jnp.float32),
            pltpu.VMEM((BLOCKS * BLK, HALF), jnp.float32),
        ],
        compiler_params=PARAMS,
        name="margins",
    )(meta, pairs, row_all, col_all, pltpu.with_memory_space_constraint(tiles, pltpu.VMEM))


def gather(own_s, own_t):
    send = lambda v, axis, step: lax.ppermute(v, axis, ring(lax.axis_size(axis), step))
    near = [send(own_s, "zl", k) for k in (1, 2, 3)]
    across = send(own_t, "zh", 1)
    s_own = [own_s] + [send(own_s, "x", k) for k in (1, -1, 2)]
    t_own = [own_t] + [send(own_t, "y", k) for k in (1, -1, 2)]

    near, s_own, t_own = lax.optimization_barrier((near, s_own, t_own))
    rest = jnp.concatenate(near)
    t_own = jnp.concatenate(t_own)
    up, down = send(rest, "x", 1), send(rest, "x", -1)

    up, down, across, t_own = lax.optimization_barrier((up, down, across, t_own))
    up_far, down_far = send(up[:192], "x", 1), send(down[192:], "x", -1)
    t_across = jnp.concatenate([across] + [send(across, "y", k) for k in (1, -1, 2)])
    t_parts = [t_own, send(t_own, "c", 1), t_across, send(t_across, "c", 1)]
    return s_own + [rest, up, down, up_far, down_far] + t_parts


def total(row_sums, col_sums):
    cols = col_sums + lax.ppermute(col_sums, "c", ring(2, 1))
    far = lax.ppermute(cols, "zh", ring(2, 1))
    row_all = lax.all_to_all(row_sums, GROUP, 0, 0, tiled=True)
    cols = jnp.broadcast_to((cols + far)[None], (4,) + cols.shape)
    return row_all, lax.all_to_all(cols, "y", 0, 0, tiled=True)


def per_device(source, target, pairs, counts):
    zh, y, c, x, zl = (lax.axis_index(a) for a in AXES)
    my_pairs = pairs.reshape(-1)
    meta = jnp.stack(
        [counts[0, 0], zh, y, c, x, zl, x * 4 + zl, zh * 8 + y * 2 + c]
    ).astype(jnp.int32)
    parts = gather(unit_rows(source), unit_rows(target))
    row_sums, col_sums, tiles = sums(meta, my_pairs, parts)
    row_all, col_all = total(row_sums, col_sums)
    row_best, col_best, src_piece, tgt_piece = margins(meta, my_pairs, row_all, col_all, tiles)
    return (
        row_best.reshape(1, 1, SLOTS, BLK),
        col_best.reshape(1, 1, SLOTS, BLK),
        src_piece.reshape(HALF),
        tgt_piece.reshape(HALF),
    )


def solution(mesh):
    fine = Mesh(mesh.devices.reshape(2, 4, 2, 4, 4), AXES)
    src_axes, tgt_axes = AXES, GROUP + BANK
    return jax.shard_map(
        per_device,
        mesh=fine,
        in_specs=(
            P(src_axes, None),
            P(tgt_axes, None),
            P(BANK, GROUP, None, None),
            P(BANK, GROUP),
        ),
        out_specs=(
            P(BANK, GROUP, None, None),
            P(BANK, GROUP, None, None),
            P(src_axes),
            P(tgt_axes),
        ),
        check_vma=False,
    )
```

```python
import math

import jax
import jax.numpy as jnp
from jax import lax
from jax.experimental import pallas as pl
from jax.experimental.pallas import tpu as pltpu
from jax.sharding import Mesh
from jax.sharding import PartitionSpec as P

BLK = 256
HALF = 128
SLOTS = 48
BLOCKS = 8
SHARDS = 16
TEMP_INV = 20.0
EXP2_SCALE = TEMP_INV * math.log2(math.e)
HALF_TEMP = 0.5 / TEMP_INV
NT = (((1,), (1,)), ((), ()))
AXES = ("zh", "y", "c", "x", "zl")
BANK = ("zh", "y", "c")
GROUP = ("x", "zl")


def unit_rows(rows):
    values = rows.astype(jnp.float32)
    width = values.shape[-1]
    scale = lax.rsqrt(jnp.mean(values * values, axis=-1, keepdims=True) + 1e-06)
    return (values * (scale * (1.0 / math.sqrt(width)))).astype(jnp.bfloat16)


def ring(n, step):
    return [(i, (i + step) % n) for i in range(n)]


GROUP_TILES = 8

REST = (1, 3, 2)
NEAR_PLACE = {(0, 0, 0): (0, 0, 128), (1, 0, 0): (1, 0, 128), (3, 0, 0): (2, 0, 128)}
for order, dz in enumerate(REST):
    for part, dx in ((3, 0), (4, 1), (5, 3)):
        NEAR_PLACE[(dx, dz, 0)] = (part, 128 * order, 128)
NEAR_PARTS = 6
FAR_PLACE = {
    (2, 0, 0): (0, 0, 128),
    (2, 1, 0): (1, 0, 128),
    (2, 3, 0): (1, 128, 64),
    (2, 3, 64): (2, 0, 64),
    (2, 2, 0): (2, 64, 128),
}
FAR_PARTS = 3
TGT_PLACE = {}
for dh in range(2):
    for dc in range(2):
        for order, dy in enumerate((0, 1, 3, 2)):
            TGT_PLACE[(dh, dy, dc)] = (2 * dh + dc, 128 * order)
TGT_PARTS = 4


def load_source(meta, place, parts, src, of_x):
    for (dx, dz, offset), (part, first, rows) in place.items():
        shard = of_x(dx) * 4 + lax.rem(meta[5] - dz + 4, 4)
        dst = pl.ds(pl.multiple_of(shard * HALF + offset, 64), rows)
        src[dst, :] = parts[part][first : first + rows, :]


def load_target(meta, parts, tgt):
    zh, y, c = meta[1], meta[2], meta[3]
    for (dh, dy, dc), (part, first) in TGT_PLACE.items():
        shard = lax.rem(zh + dh, 2) * 8 + lax.rem(y - dy + 4, 4) * 2 + lax.rem(c + dc, 2)
        dst = pl.ds(pl.multiple_of(shard * HALF, HALF), HALF)
        tgt[dst, :] = parts[part][first : first + HALF, :]


def pick(meta, pairs, todo, far):
    far_x = lax.rem(meta[4] + 2, 4)

    def step(p, n):
        todo[n] = p
        is_far = lax.div(pairs[2 * p], 2) == far_x
        return n + (is_far == far).astype(jnp.int32)

    return lax.fori_loop(0, meta[0], step, jnp.int32(0))


def add_tiles(pairs, todo, n, width, src, row_of, tgt, tiles, acc_row, acc_col):
    dead_row = acc_row.shape[0] // BLK - 1

    def group(k, carry):
        for u in range(width):
            live = k * width + u < n
            p = todo[jnp.minimum(k * width + u, n - 1)]
            i, j = row_of(pairs[2 * p]), pairs[2 * p + 1]
            left = src[pl.ds(pl.multiple_of(i * BLK, BLK), BLK), :]
            right = tgt[pl.ds(pl.multiple_of(j * BLK, BLK), BLK), :]
            scores = lax.dot_general(left, right, NT, preferred_element_type=jnp.float32)
            tiles[p] = scores
            i = jnp.where(live, i, dead_row)
            j = jnp.where(live, j, BLOCKS)
            w = jnp.exp2(scores * EXP2_SCALE)
            rows = pl.ds(pl.multiple_of(i * BLK, BLK), BLK)
            acc_row[rows, :] += w[:, :HALF] + w[:, HALF:]
            acc_col[j] += w.reshape(BLK // 8, 8, BLK).sum(0)
        return carry

    lax.fori_loop(0, (n + width - 1) // width, group, 0)


def row_totals(acc_row, count):
    return jnp.concatenate(
        [
            jnp.sum(acc_row[h * HALF : (h + 1) * HALF, :].T, axis=0, keepdims=True)
            for h in range(count)
        ],
        0,
    )


def near_kernel(meta, pairs, *refs):
    parts, refs = refs[: NEAR_PARTS + TGT_PARTS], refs[NEAR_PARTS + TGT_PARTS :]
    row_out, acc_col, tiles, tgt, src, acc_row, todo = refs
    load_source(meta, NEAR_PLACE, parts[:NEAR_PARTS], src, lambda dx: lax.rem(meta[4] - dx + 4, 4))
    load_target(meta, parts[NEAR_PARTS:], tgt)
    acc_row[...] = jnp.zeros_like(acc_row)
    acc_col[...] = jnp.zeros_like(acc_col)
    n = pick(meta, pairs, todo, False)
    add_tiles(pairs, todo, n, GROUP_TILES, src, lambda i: i, tgt, tiles, acc_row, acc_col)
    row_out[...] = row_totals(acc_row, SHARDS)


def far_kernel(meta, pairs, *refs):
    parts, refs = refs[:FAR_PARTS], refs[FAR_PARTS:]
    row_in, col_in, tgt, tiles_in, row_out, col_out, tiles, src, acc_row, acc_col, todo = refs
    del tiles_in
    load_source(meta, FAR_PLACE, parts, src, lambda dx: 0)
    acc_row[...] = jnp.zeros_like(acc_row)
    acc_col[...] = col_in[...]
    n = pick(meta, pairs, todo, True)
    add_tiles(pairs, todo, n, 4, src, lambda i: lax.rem(i, 2), tgt, tiles, acc_row, acc_col)
    far_rows = row_totals(acc_row, 4)
    rows = row_in[...]
    far_x = lax.rem(meta[4] + 2, 4)
    rows = jnp.concatenate(
        [rows[4 * v : 4 * v + 4] + jnp.where(far_x == v, far_rows, 0.0) for v in range(4)], 0
    )
    row_out[...] = jnp.broadcast_to(rows[None], row_out.shape)
    cols = []
    for j in range(BLOCKS):
        col = jnp.sum(acc_col[j], axis=0, keepdims=True)
        cols += [col[:, :HALF], col[:, HALF:]]
    col_out[...] = jnp.concatenate(cols, 0)


def margin_kernel(meta, pairs, row_all, c0, c1, c2, c3, tiles, row_best, col_best, src_piece, tgt_piece,
                  s16, t16, s_cols):
    count = meta[0]
    s16[...] = jnp.log(jnp.sum(row_all[...], axis=0)) * HALF_TEMP
    t16[...] = jnp.log((c0[...] + c1[...]) + (c2[...] + c3[...])) * HALF_TEMP
    row_best[...] = jnp.zeros_like(row_best)
    col_best[...] = jnp.zeros_like(col_best)
    for h in range(SHARDS):
        s_cols[h * HALF : (h + 1) * HALF, :] = jnp.broadcast_to(
            s16[h : h + 1, :], (HALF, HALF)
        ).T
    src_piece[...] = s16[pl.ds(meta[6], 1), :] * (2 * TEMP_INV)
    tgt_piece[...] = t16[pl.ds(meta[7], 1), :] * (2 * TEMP_INV)

    def group(k, carry):
        row_rows, col_rows = [], []
        for u in range(GROUP_TILES):
            p = k * GROUP_TILES + u
            i, j = pairs[2 * p], pairs[2 * p + 1]
            ta, tb = t16[pl.ds(2 * j, 1), :], t16[pl.ds(2 * j + 1, 1), :]
            sa, sb = s16[pl.ds(2 * i, 1), :], s16[pl.ds(2 * i + 1, 1), :]
            sc = s_cols[pl.ds(pl.multiple_of(i * BLK, BLK), BLK), :]
            scores = tiles[p]
            ua, ub = scores[:, :HALF], scores[:, HALF:]
            best = jnp.maximum(ua - ta, ub - tb)
            ra = jnp.max(best[:HALF].T, axis=0, keepdims=True)
            rb = jnp.max(best[HALF:].T, axis=0, keepdims=True)
            ca = jnp.max(ua - sc, axis=0, keepdims=True)
            cb = jnp.max(ub - sc, axis=0, keepdims=True)
            live = p < count
            row_rows.append(jnp.where(live, jnp.concatenate([ra - sa, rb - sb], 1), 0.0))
            col_rows.append(jnp.where(live, jnp.concatenate([ca - ta, cb - tb], 1), 0.0))
        some = pl.ds(pl.multiple_of(k * GROUP_TILES, GROUP_TILES), GROUP_TILES)
        row_best[some, :] = jnp.concatenate(row_rows, 0) * TEMP_INV
        col_best[some, :] = jnp.concatenate(col_rows, 0) * TEMP_INV
        return carry

    lax.fori_loop(0, (count + GROUP_TILES - 1) // GROUP_TILES, group, 0)


VMEM = pl.BlockSpec(memory_space=pltpu.VMEM)
SMEM = pl.BlockSpec(memory_space=pltpu.SMEM)


F32 = lambda *shape: jax.ShapeDtypeStruct(shape, jnp.float32)
PARAMS = pltpu.CompilerParams(vmem_limit_bytes=20 * 1024 * 1024)


def pinned(v):
    return pltpu.with_memory_space_constraint(v, pltpu.VMEM)


def sums(meta, pairs, near_parts, far_parts, tgt_parts):
    width = tgt_parts[0].shape[1]
    tile_store = pltpu.VMEM((SLOTS, BLK, BLK), jnp.float32)
    col_store = pltpu.VMEM((BLOCKS + 1, 8, BLK), jnp.float32)
    slab = pltpu.VMEM((BLOCKS * BLK, width), jnp.bfloat16)
    todo = pltpu.SMEM((SLOTS + 8,), jnp.int32)
    near_rows, near_cols, tiles, tgt = pl.pallas_call(
        near_kernel,
        out_shape=(pltpu.VMEM((SHARDS, HALF), jnp.float32), col_store, tile_store, slab),
        in_specs=[SMEM, SMEM] + [VMEM] * (NEAR_PARTS + TGT_PARTS),
        out_specs=(VMEM,) * 4,
        scratch_shapes=[slab, pltpu.VMEM(((BLOCKS + 1) * BLK, HALF), jnp.float32), todo],
        compiler_params=PARAMS,
        cost_estimate=pl.CostEstimate(
            flops=40 * 2 * BLK * BLK * width, bytes_accessed=12 << 20, transcendentals=40 * BLK * BLK
        ),
        name="near_sums",
    )(meta, pairs, *near_parts, *tgt_parts)
    return pl.pallas_call(
        far_kernel,
        out_shape=(F32(SHARDS, SHARDS, HALF), F32(SHARDS, HALF), tile_store),
        in_specs=[SMEM, SMEM] + [VMEM] * (FAR_PARTS + 4),
        out_specs=(VMEM,) * 3,
        scratch_shapes=[
            pltpu.VMEM((2 * BLK, width), jnp.bfloat16),
            pltpu.VMEM((3 * BLK, HALF), jnp.float32),
            col_store,
            todo,
        ],
        input_output_aliases={2 + FAR_PARTS + 3: 2},
        compiler_params=PARAMS,
        name="far_sums",
    )(meta, pairs, *far_parts, pinned(near_rows), pinned(near_cols), pinned(tgt), pinned(tiles))


def margins(meta, pairs, row_all, col_all, tiles):
    return pl.pallas_call(
        margin_kernel,
        out_shape=(F32(SLOTS, BLK), F32(SLOTS, BLK), F32(1, HALF), F32(1, HALF)),
        in_specs=[SMEM, SMEM] + [VMEM] * 6,
        out_specs=(VMEM,) * 4,
        scratch_shapes=[
            pltpu.VMEM((SHARDS, HALF), jnp.float32),
            pltpu.VMEM((SHARDS, HALF), jnp.float32),
            pltpu.VMEM((BLOCKS * BLK, HALF), jnp.float32),
        ],
        compiler_params=PARAMS,
        name="margins",
    )(meta, pairs, row_all, *col_all, pinned(tiles))


def gather(own_s, own_t):
    send = lambda v, axis, step: lax.ppermute(v, axis, ring(lax.axis_size(axis), step))
    near = [send(own_s, "zl", k) for k in REST]
    across = send(own_t, "zh", 1)
    near[0], own_s, own_t = lax.optimization_barrier((near[0], own_s, own_t))
    s_own = [send(own_s, "x", k) for k in (1, -1, 2)]
    t_own = [own_t] + [send(own_t, "y", k) for k in (1, -1, 2)]

    near, s_own, t_own = lax.optimization_barrier((near, s_own, t_own))
    rest = jnp.concatenate(near)
    up, down = send(rest, "x", 1), send(rest, "x", -1)
    across, t_own = lax.optimization_barrier((across, t_own))
    t_across = [across] + [send(across, "y", k) for k in (1, -1, 2)]
    t_own = jnp.concatenate(t_own)
    t_own_c = send(t_own, "c", 1)

    up, down, t_across = lax.optimization_barrier((up, down, t_across))
    up_far, down_far = send(up[:192], "x", 1), send(down[192:], "x", -1)
    t_across = jnp.concatenate(t_across)
    t_parts = [t_own, t_own_c, t_across, send(t_across, "c", 1)]
    return [own_s, s_own[0], s_own[1], rest, up, down], [s_own[2], up_far, down_far], t_parts


def total(row_sums, col_sums):
    cols = col_sums + lax.ppermute(col_sums, "c", ring(2, 1))
    far = lax.ppermute(cols, "zh", ring(2, 1))
    cols, row_sums = lax.optimization_barrier((cols, row_sums))
    row_all = lax.all_to_all(row_sums, GROUP, 0, 0, tiled=True)
    cols = cols + far
    return row_all, [cols] + [lax.ppermute(cols, "y", ring(4, k)) for k in (1, -1, 2)]


def per_device(source, target, pairs, counts):
    zh, y, c, x, zl = (lax.axis_index(a) for a in AXES)
    my_pairs = pairs.reshape(-1)
    meta = jnp.stack(
        [counts[0, 0], zh, y, c, x, zl, x * 4 + zl, zh * 8 + y * 2 + c]
    ).astype(jnp.int32)
    pieces = gather(unit_rows(source), unit_rows(target))
    row_sums, col_sums, tiles = sums(meta, my_pairs, *pieces)
    row_all, col_all = total(row_sums, col_sums)
    row_best, col_best, src_piece, tgt_piece = margins(meta, my_pairs, row_all, col_all, tiles)
    return (
        row_best.reshape(1, 1, SLOTS, BLK),
        col_best.reshape(1, 1, SLOTS, BLK),
        src_piece.reshape(HALF),
        tgt_piece.reshape(HALF),
    )


def solution(mesh):
    fine = Mesh(mesh.devices.reshape(2, 4, 2, 4, 4), AXES)
    src_axes, tgt_axes = AXES, GROUP + BANK
    return jax.shard_map(
        per_device,
        mesh=fine,
        in_specs=(
            P(src_axes, None),
            P(tgt_axes, None),
            P(BANK, GROUP, None, None),
            P(BANK, GROUP),
        ),
        out_specs=(
            P(BANK, GROUP, None, None),
            P(BANK, GROUP, None, None),
            P(src_axes),
            P(tgt_axes),
        ),
        check_vma=False,
    )
```

```python
import math

import jax
import jax.numpy as jnp
from jax import lax
from jax.experimental import pallas as pl
from jax.experimental.pallas import tpu as pltpu
from jax.sharding import Mesh
from jax.sharding import PartitionSpec as P

BLK = 256
HALF = 128
SLOTS = 48
BLOCKS = 8
SHARDS = 16
TEMP_INV = 20.0
EXP2_SCALE = TEMP_INV * math.log2(math.e)
HALF_TEMP = 0.5 / TEMP_INV
NT = (((1,), (1,)), ((), ()))
AXES = ("zh", "y", "c", "x", "zl")
BANK = ("zh", "y", "c")
GROUP = ("x", "zl")


def unit_rows(rows):
    values = rows.astype(jnp.float32)
    width = values.shape[-1]
    scale = lax.rsqrt(jnp.mean(values * values, axis=-1, keepdims=True) + 1e-06)
    return (values * (scale * (1.0 / math.sqrt(width)))).astype(jnp.bfloat16)


def ring(n, step):
    return [(i, (i + step) % n) for i in range(n)]


GROUP_TILES = 8

REST = (1, 3, 2)
NEAR_PLACE = {(0, 0, 0): (0, 0, 128), (1, 0, 0): (1, 0, 128), (3, 0, 0): (2, 0, 128)}
for order, dz in enumerate(REST):
    for part, dx in ((3, 0), (4, 1), (5, 3)):
        NEAR_PLACE[(dx, dz, 0)] = (part, 128 * order, 128)
NEAR_PARTS = 6
FAR_PLACE = {
    (2, 0, 0): (0, 0, 128),
    (2, 1, 0): (1, 0, 128),
    (2, 3, 0): (1, 128, 64),
    (2, 3, 64): (2, 0, 64),
    (2, 2, 0): (2, 64, 128),
}
FAR_PARTS = 3
TGT_PLACE = {}
for order, dy in enumerate((0, 1, 3, 2)):
    TGT_PLACE[(0, dy, 0)] = (0, 128 * order)
    TGT_PLACE[(0, dy, 1)] = (1, 128 * order)
    TGT_PLACE[(1, dy, 0)] = (2 + order, 0)
    TGT_PLACE[(1, dy, 1)] = (6 + order, 0)
TGT_PARTS = 10


def load_source(meta, place, parts, src, of_x):
    for (dx, dz, offset), (part, first, rows) in place.items():
        shard = of_x(dx) * 4 + lax.rem(meta[5] - dz + 4, 4)
        dst = pl.ds(pl.multiple_of(shard * HALF + offset, 64), rows)
        src[dst, :] = parts[part][first : first + rows, :]


def load_target(meta, parts, tgt):
    zh, y, c = meta[1], meta[2], meta[3]
    for (dh, dy, dc), (part, first) in TGT_PLACE.items():
        shard = lax.rem(zh + dh, 2) * 8 + lax.rem(y - dy + 4, 4) * 2 + lax.rem(c + dc, 2)
        dst = pl.ds(pl.multiple_of(shard * HALF, HALF), HALF)
        tgt[dst, :] = parts[part][first : first + HALF, :]


def add_tiles(todo, begin, n, width, src, row_of, tgt, tiles, acc_row, acc_col):
    dead_row = acc_row.shape[0] // BLK - 1

    def group(k, carry):
        for u in range(width):
            live = k * width + u < n
            q = jnp.minimum(k * width + u, n - 1)
            i, j = row_of(todo[3 * (begin + q)]), todo[3 * (begin + q) + 1]
            left = src[pl.ds(pl.multiple_of(i * BLK, BLK), BLK), :]
            right = tgt[pl.ds(pl.multiple_of(j * BLK, BLK), BLK), :]
            scores = lax.dot_general(left, right, NT, preferred_element_type=jnp.float32)
            tiles[q] = scores
            i = jnp.where(live, i, dead_row)
            j = jnp.where(live, j, BLOCKS)
            w = jnp.exp2(scores * EXP2_SCALE)
            rows = pl.ds(pl.multiple_of(i * BLK, BLK), BLK)
            acc_row[rows, :] += w[:, :HALF] + w[:, HALF:]
            acc_col[j] += w.reshape(BLK // 8, 8, BLK).sum(0)
        return carry

    lax.fori_loop(0, (n + width - 1) // width, group, 0)


def row_totals(acc_row, count):
    return jnp.concatenate(
        [
            jnp.sum(acc_row[h * HALF : (h + 1) * HALF, :].T, axis=0, keepdims=True)
            for h in range(count)
        ],
        0,
    )


def near_kernel(meta, todo, *refs):
    parts, refs = refs[: NEAR_PARTS + TGT_PARTS], refs[NEAR_PARTS + TGT_PARTS :]
    row_out, acc_col, tiles, tgt, src, acc_row = refs
    load_source(meta, NEAR_PLACE, parts[:NEAR_PARTS], src, lambda dx: lax.rem(meta[4] - dx + 4, 4))
    load_target(meta, parts[NEAR_PARTS:], tgt)
    acc_row[...] = jnp.zeros_like(acc_row)
    acc_col[...] = jnp.zeros_like(acc_col)
    add_tiles(todo, 0, meta[8], GROUP_TILES, src, lambda i: i, tgt, tiles, acc_row, acc_col)
    row_out[...] = row_totals(acc_row, SHARDS)


def far_kernel(meta, todo, *refs):
    parts, refs = refs[:FAR_PARTS], refs[FAR_PARTS:]
    row_in, col_in, tgt, row_out, col_out, tiles, src, acc_row, acc_col = refs
    load_source(meta, FAR_PLACE, parts, src, lambda dx: 0)
    acc_row[...] = jnp.zeros_like(acc_row)
    acc_col[...] = col_in[...]
    near = meta[8]
    add_tiles(todo, near, meta[0] - near, 4, src, lambda i: lax.rem(i, 2), tgt, tiles, acc_row, acc_col)
    far_rows = row_totals(acc_row, 4)
    rows = row_in[...]
    far_x = lax.rem(meta[4] + 2, 4)
    rows = jnp.concatenate(
        [rows[4 * v : 4 * v + 4] + jnp.where(far_x == v, far_rows, 0.0) for v in range(4)], 0
    )
    row_out[...] = rows
    cols = []
    for j in range(BLOCKS):
        col = jnp.sum(acc_col[j], axis=0, keepdims=True)
        cols += [col[:, :HALF], col[:, HALF:]]
    col_out[...] = jnp.concatenate(cols, 0)


def margin_kernel(meta, todo, r0, r1, r2, r3, c0, c1, near_tiles, far_tiles, row_best, col_best,
                  src_piece, tgt_piece, s16, t16, s_cols, row_slots, col_slots):
    s16[...] = jnp.log((r0[...] + r1[...]) + (r2[...] + r3[...])) * HALF_TEMP
    t16[...] = jnp.log(c0[...] + c1[...]) * HALF_TEMP
    row_slots[...] = jnp.zeros_like(row_slots)
    col_slots[...] = jnp.zeros_like(col_slots)
    for h in range(SHARDS):
        s_cols[h * HALF : (h + 1) * HALF, :] = jnp.broadcast_to(
            s16[h : h + 1, :], (HALF, HALF)
        ).T
    src_piece[...] = s16[pl.ds(meta[6], 1), :] * (2 * TEMP_INV)
    tgt_piece[...] = t16[pl.ds(meta[7], 1), :] * (2 * TEMP_INV)

    def best_of(begin, n, width, tiles):
        def group(k, carry):
            for u in range(width):
                q = jnp.minimum(k * width + u, n - 1)
                i, j, p = (todo[3 * (begin + q) + v] for v in range(3))
                ta, tb = t16[pl.ds(2 * j, 1), :], t16[pl.ds(2 * j + 1, 1), :]
                sa, sb = s16[pl.ds(2 * i, 1), :], s16[pl.ds(2 * i + 1, 1), :]
                sc = s_cols[pl.ds(pl.multiple_of(i * BLK, BLK), BLK), :]
                scores = tiles[q]
                ua, ub = scores[:, :HALF], scores[:, HALF:]
                best = jnp.maximum(ua - ta, ub - tb)
                ra = jnp.max(best[:HALF].T, axis=0, keepdims=True)
                rb = jnp.max(best[HALF:].T, axis=0, keepdims=True)
                ca = jnp.max(ua - sc, axis=0, keepdims=True)
                cb = jnp.max(ub - sc, axis=0, keepdims=True)
                row_slots[p] = jnp.concatenate([ra - sa, rb - sb], 1) * TEMP_INV
                col_slots[p] = jnp.concatenate([ca - ta, cb - tb], 1) * TEMP_INV
            return carry

        lax.fori_loop(0, (n + width - 1) // width, group, 0)

    near = meta[8]
    best_of(0, near, GROUP_TILES, near_tiles)
    best_of(near, meta[0] - near, 4, far_tiles)
    for k in range(0, SLOTS, 8):
        row_best[k : k + 8, :] = jnp.concatenate([row_slots[k + v] for v in range(8)], 0)
        col_best[k : k + 8, :] = jnp.concatenate([col_slots[k + v] for v in range(8)], 0)


VMEM = pl.BlockSpec(memory_space=pltpu.VMEM)
SMEM = pl.BlockSpec(memory_space=pltpu.SMEM)


F32 = lambda *shape: jax.ShapeDtypeStruct(shape, jnp.float32)
PARAMS = pltpu.CompilerParams(vmem_limit_bytes=20 * 1024 * 1024)


def pinned(v):
    return pltpu.with_memory_space_constraint(v, pltpu.VMEM)


def sums(meta, todo, near_parts, far_parts, tgt_parts):
    width = tgt_parts[0].shape[1]
    near_store = pltpu.VMEM((SLOTS, BLK, BLK), jnp.float32)
    far_store = pltpu.VMEM((2 * BLOCKS, BLK, BLK), jnp.float32)
    col_store = pltpu.VMEM((BLOCKS + 1, 8, BLK), jnp.float32)
    slab = pltpu.VMEM((BLOCKS * BLK, width), jnp.bfloat16)
    near_rows, near_cols, near_tiles, tgt = pl.pallas_call(
        near_kernel,
        out_shape=(pltpu.VMEM((SHARDS, HALF), jnp.float32), col_store, near_store, slab),
        in_specs=[SMEM, SMEM] + [VMEM] * (NEAR_PARTS + TGT_PARTS),
        out_specs=(VMEM,) * 4,
        scratch_shapes=[slab, pltpu.VMEM(((BLOCKS + 1) * BLK, HALF), jnp.float32)],
        compiler_params=PARAMS,
        cost_estimate=pl.CostEstimate(
            flops=40 * 2 * BLK * BLK * width, bytes_accessed=12 << 20, transcendentals=40 * BLK * BLK
        ),
        name="near_sums",
    )(meta, todo, *near_parts, *tgt_parts)
    row_sums, col_sums, far_tiles = pl.pallas_call(
        far_kernel,
        out_shape=(F32(SHARDS, HALF), F32(SHARDS, HALF), far_store),
        in_specs=[SMEM, SMEM] + [VMEM] * (FAR_PARTS + 3),
        out_specs=(VMEM,) * 3,
        scratch_shapes=[
            pltpu.VMEM((2 * BLK, width), jnp.bfloat16),
            pltpu.VMEM((3 * BLK, HALF), jnp.float32),
            col_store,
        ],
        compiler_params=PARAMS,
        name="far_sums",
    )(meta, todo, *far_parts, pinned(near_rows), pinned(near_cols), pinned(tgt))
    return row_sums, col_sums, near_tiles, far_tiles


def margins(meta, todo, row_all, col_all, near_tiles, far_tiles):
    return pl.pallas_call(
        margin_kernel,
        out_shape=(F32(SLOTS, BLK), F32(SLOTS, BLK), F32(1, HALF), F32(1, HALF)),
        in_specs=[SMEM, SMEM] + [VMEM] * 8,
        out_specs=(VMEM,) * 4,
        scratch_shapes=[
            pltpu.VMEM((SHARDS, HALF), jnp.float32),
            pltpu.VMEM((SHARDS, HALF), jnp.float32),
            pltpu.VMEM((BLOCKS * BLK, HALF), jnp.float32),
            pltpu.VMEM((SLOTS, 1, BLK), jnp.float32),
            pltpu.VMEM((SLOTS, 1, BLK), jnp.float32),
        ],
        compiler_params=PARAMS,
        name="margins",
    )(meta, todo, *row_all, *col_all, pinned(near_tiles), pinned(far_tiles))


def gather(own_s, own_t):
    send = lambda v, axis, step: lax.ppermute(v, axis, ring(lax.axis_size(axis), step))
    after = lambda v, done: lax.optimization_barrier((v, done))
    s_own = [send(own_s, "x", k) for k in (1, -1)]
    near = [send(own_s, "zl", k) for k in REST]
    (own_t, again), s_own = after((own_t, own_s), s_own)
    s_own.append(send(again, "x", 2))
    across = send(own_t, "zh", 1)
    own_t, s_own = after(own_t, s_own)
    t_own = [own_t] + [send(own_t, "y", k) for k in (1, -1, 2)]

    rest = jnp.concatenate(near)
    up, down = send(rest, "x", 1), send(rest, "x", -1)
    across, t_own = after(across, t_own)
    t_own = jnp.concatenate(t_own)
    t_own_c = send(t_own, "c", 1)
    t_across = [across] + [send(across, "y", k) for k in (1, -1, 2)]

    (up, down), t_across = after((up, down), t_across)
    t_across_c = [send(v, "c", 1) for v in t_across]
    up_far, down_far = send(up[:192], "x", 1), send(down[192:], "x", -1)
    t_parts = [t_own, t_own_c] + t_across + t_across_c
    return [own_s, s_own[0], s_own[1], rest, up, down], [s_own[2], up_far, down_far], t_parts


def total(row_sums, col_sums):
    send = lambda v, axis, step: lax.ppermute(v, axis, ring(lax.axis_size(axis), step))
    cols = col_sums + send(col_sums, "c", 1)
    rows = [row_sums] + [send(row_sums, "x", k) for k in (1, -1, 2)]
    cols = [cols] + [send(cols, "y", k) for k in (1, -1, 2)]
    rows, cols = lax.optimization_barrier((rows, cols))
    rows, cols = (rows[0] + rows[1]) + (rows[2] + rows[3]), (cols[0] + cols[1]) + (cols[2] + cols[3])
    return [rows] + [send(rows, "zl", k) for k in (1, -1, 2)], [cols, send(cols, "zh", 1)]


def listing(pairs, count, far_x):
    slot = jnp.arange(pairs.shape[0], dtype=jnp.int32)
    live = slot < count
    near = live & (pairs[:, 0] // 2 != far_x)
    kind = jnp.where(near, 0, jnp.where(live, 1, 2))
    key = kind * SLOTS + slot
    place = jnp.sum(key[None, :] < key[:, None], axis=1, dtype=jnp.int32)
    entry = jnp.concatenate([pairs, slot[:, None]], 1)
    todo = jnp.sum(jnp.where(place[None, :, None] == slot[:, None, None], entry[None], 0), axis=1)
    return todo.reshape(-1).astype(jnp.int32), jnp.sum(near, dtype=jnp.int32)


def per_device(source, target, pairs, counts):
    zh, y, c, x, zl = (lax.axis_index(a) for a in AXES)
    count = counts[0, 0]
    todo, near = listing(pairs[0, 0], count, (x + 2) % 4)
    meta = jnp.stack([count, zh, y, c, x, zl, x * 4 + zl, zh * 8 + y * 2 + c, near]).astype(jnp.int32)
    pieces = gather(unit_rows(source), unit_rows(target))
    row_sums, col_sums, near_tiles, far_tiles = sums(meta, todo, *pieces)
    row_all, col_all = total(row_sums, col_sums)
    row_best, col_best, src_piece, tgt_piece = margins(
        meta, todo, row_all, col_all, near_tiles, far_tiles
    )
    return (
        row_best.reshape(1, 1, SLOTS, BLK),
        col_best.reshape(1, 1, SLOTS, BLK),
        src_piece.reshape(HALF),
        tgt_piece.reshape(HALF),
    )


def solution(mesh):
    fine = Mesh(mesh.devices.reshape(2, 4, 2, 4, 4), AXES)
    src_axes, tgt_axes = AXES, GROUP + BANK
    return jax.shard_map(
        per_device,
        mesh=fine,
        in_specs=(
            P(src_axes, None),
            P(tgt_axes, None),
            P(BANK, GROUP, None, None),
            P(BANK, GROUP),
        ),
        out_specs=(
            P(BANK, GROUP, None, None),
            P(BANK, GROUP, None, None),
            P(src_axes),
            P(tgt_axes),
        ),
        check_vma=False,
    )
```

```python
import math

import jax
import jax.numpy as jnp
from jax import lax
from jax.experimental import pallas as pl
from jax.experimental.pallas import tpu as pltpu
from jax.sharding import Mesh
from jax.sharding import PartitionSpec as P

BLK = 256
HALF = 128
SLOTS = 48
BLOCKS = 8
SHARDS = 16
TEMP_INV = 20.0
EXP2_SCALE = TEMP_INV * math.log2(math.e)
HALF_TEMP = 0.5 / TEMP_INV
NT = (((1,), (1,)), ((), ()))
AXES = ("zh", "y", "c", "x", "zl")
BANK = ("zh", "y", "c")
GROUP = ("x", "zl")


def unit_rows(rows):
    values = rows.astype(jnp.float32)
    width = values.shape[-1]
    scale = lax.rsqrt(jnp.mean(values * values, axis=-1, keepdims=True) + 1e-06)
    return (values * (scale * (1.0 / math.sqrt(width)))).astype(jnp.bfloat16)


def ring(n, step):
    return [(i, (i + step) % n) for i in range(n)]


GROUP_TILES = 8

REST = (1, 3, 2)
NEAR_PLACE = {(0, 0, 0): (0, 0, 128), (1, 0, 0): (1, 0, 128), (3, 0, 0): (2, 0, 128)}
for order, dz in enumerate(REST):
    for part, dx in ((3, 0), (4, 1), (5, 3)):
        NEAR_PLACE[(dx, dz, 0)] = (part, 128 * order, 128)
NEAR_PARTS = 6
FAR_PLACE = {
    (2, 0, 0): (0, 0, 128),
    (2, 1, 0): (1, 0, 128),
    (2, 3, 0): (1, 128, 64),
    (2, 3, 64): (2, 0, 64),
    (2, 2, 0): (2, 64, 128),
}
FAR_PARTS = 3
TGT_PLACE = {}
for order, dy in enumerate((0, 1, 3, 2)):
    TGT_PLACE[(0, dy, 0)] = (0, 128 * order)
    TGT_PLACE[(0, dy, 1)] = (1, 128 * order)
    TGT_PLACE[(1, dy, 0)] = (2 + order, 0)
    TGT_PLACE[(1, dy, 1)] = (6 + order, 0)
TGT_PARTS = 10


def load_source(meta, place, parts, src, of_x):
    for (dx, dz, offset), (part, first, rows) in place.items():
        shard = of_x(dx) * 4 + lax.rem(meta[5] - dz + 4, 4)
        dst = pl.ds(pl.multiple_of(shard * HALF + offset, 64), rows)
        src[dst, :] = parts[part][first : first + rows, :]


def load_target(meta, parts, tgt):
    zh, y, c = meta[1], meta[2], meta[3]
    for (dh, dy, dc), (part, first) in TGT_PLACE.items():
        shard = lax.rem(zh + dh, 2) * 8 + lax.rem(y - dy + 4, 4) * 2 + lax.rem(c + dc, 2)
        dst = pl.ds(pl.multiple_of(shard * HALF, HALF), HALF)
        tgt[dst, :] = parts[part][first : first + HALF, :]


def add_tiles(todo, begin, n, width, src, row_of, tgt, tiles, acc_row, acc_col):
    dead_row = acc_row.shape[0] // BLK - 1

    def group(k, carry):
        for u in range(width):
            live = k * width + u < n
            q = jnp.minimum(k * width + u, n - 1)
            i, j = row_of(todo[3 * (begin + q)]), todo[3 * (begin + q) + 1]
            left = src[pl.ds(pl.multiple_of(i * BLK, BLK), BLK), :]
            right = tgt[pl.ds(pl.multiple_of(j * BLK, BLK), BLK), :]
            scores = lax.dot_general(left, right, NT, preferred_element_type=jnp.float32)
            tiles[q] = scores
            i = jnp.where(live, i, dead_row)
            j = jnp.where(live, j, BLOCKS)
            w = jnp.exp2(scores * EXP2_SCALE)
            rows = pl.ds(pl.multiple_of(i * BLK, BLK), BLK)
            acc_row[rows, :] += w[:, :HALF] + w[:, HALF:]
            acc_col[j] += w.reshape(BLK // 8, 8, BLK).sum(0)
        return carry

    lax.fori_loop(0, (n + width - 1) // width, group, 0)


def row_totals(acc_row, count):
    return jnp.concatenate(
        [
            jnp.sum(acc_row[h * HALF : (h + 1) * HALF, :].T, axis=0, keepdims=True)
            for h in range(count)
        ],
        0,
    )


def near_kernel(meta, todo, *refs):
    parts, refs = refs[: NEAR_PARTS + TGT_PARTS], refs[NEAR_PARTS + TGT_PARTS :]
    row_out, acc_col, tiles, tgt, src, acc_row = refs
    load_source(meta, NEAR_PLACE, parts[:NEAR_PARTS], src, lambda dx: lax.rem(meta[4] - dx + 4, 4))
    load_target(meta, parts[NEAR_PARTS:], tgt)
    acc_row[...] = jnp.zeros_like(acc_row)
    acc_col[...] = jnp.zeros_like(acc_col)
    add_tiles(todo, 0, meta[8], GROUP_TILES, src, lambda i: i, tgt, tiles, acc_row, acc_col)
    row_out[...] = row_totals(acc_row, SHARDS)


def far_kernel(meta, todo, *refs):
    parts, refs = refs[:FAR_PARTS], refs[FAR_PARTS:]
    row_in, col_in, tgt, row_out, col_out, tiles, src, acc_row, acc_col = refs
    load_source(meta, FAR_PLACE, parts, src, lambda dx: 0)
    acc_row[...] = jnp.zeros_like(acc_row)
    acc_col[...] = col_in[...]
    near = meta[8]
    add_tiles(todo, near, meta[0] - near, 4, src, lambda i: lax.rem(i, 2), tgt, tiles, acc_row, acc_col)
    far_rows = row_totals(acc_row, 4)
    rows = row_in[...]
    far_x = lax.rem(meta[4] + 2, 4)
    rows = jnp.concatenate(
        [rows[4 * v : 4 * v + 4] + jnp.where(far_x == v, far_rows, 0.0) for v in range(4)], 0
    )
    row_out[...] = rows
    cols = []
    for j in range(BLOCKS):
        col = jnp.sum(acc_col[j], axis=0, keepdims=True)
        cols += [col[:, :HALF], col[:, HALF:]]
    col_out[...] = jnp.concatenate(cols, 0)


def margin_kernel(meta, todo, r0, r1, r2, r3, c0, c1, near_tiles, far_tiles, row_best, col_best,
                  src_piece, tgt_piece, s16, t16, s_cols, row_slots, col_slots):
    s16[...] = jnp.log((r0[...] + r1[...]) + (r2[...] + r3[...])) * HALF_TEMP
    t16[...] = jnp.log(c0[...] + c1[...]) * HALF_TEMP
    row_slots[...] = jnp.zeros_like(row_slots)
    col_slots[...] = jnp.zeros_like(col_slots)
    for h in range(SHARDS):
        s_cols[h * HALF : (h + 1) * HALF, :] = jnp.broadcast_to(
            s16[h : h + 1, :], (HALF, HALF)
        ).T
    src_piece[...] = s16[pl.ds(meta[6], 1), :] * (2 * TEMP_INV)
    tgt_piece[...] = t16[pl.ds(meta[7], 1), :] * (2 * TEMP_INV)

    def best_of(begin, n, width, tiles):
        def group(k, carry):
            for u in range(width):
                q = jnp.minimum(k * width + u, n - 1)
                i, j, p = (todo[3 * (begin + q) + v] for v in range(3))
                ta, tb = t16[pl.ds(2 * j, 1), :], t16[pl.ds(2 * j + 1, 1), :]
                sa, sb = s16[pl.ds(2 * i, 1), :], s16[pl.ds(2 * i + 1, 1), :]
                sc = s_cols[pl.ds(pl.multiple_of(i * BLK, BLK), BLK), :]
                scores = tiles[q]
                ua, ub = scores[:, :HALF], scores[:, HALF:]
                best = jnp.maximum(ua - ta, ub - tb)
                ra = jnp.max(best[:HALF].T, axis=0, keepdims=True)
                rb = jnp.max(best[HALF:].T, axis=0, keepdims=True)
                ca = jnp.max(ua - sc, axis=0, keepdims=True)
                cb = jnp.max(ub - sc, axis=0, keepdims=True)
                row_slots[p] = jnp.concatenate([ra - sa, rb - sb], 1) * TEMP_INV
                col_slots[p] = jnp.concatenate([ca - ta, cb - tb], 1) * TEMP_INV
            return carry

        lax.fori_loop(0, (n + width - 1) // width, group, 0)

    near = meta[8]
    best_of(0, near, GROUP_TILES, near_tiles)
    best_of(near, meta[0] - near, 4, far_tiles)
    for k in range(0, SLOTS, 8):
        row_best[k : k + 8, :] = jnp.concatenate([row_slots[k + v] for v in range(8)], 0)
        col_best[k : k + 8, :] = jnp.concatenate([col_slots[k + v] for v in range(8)], 0)


VMEM = pl.BlockSpec(memory_space=pltpu.VMEM)
SMEM = pl.BlockSpec(memory_space=pltpu.SMEM)


F32 = lambda *shape: jax.ShapeDtypeStruct(shape, jnp.float32)
PARAMS = pltpu.CompilerParams(vmem_limit_bytes=20 * 1024 * 1024)


def pinned(v):
    return pltpu.with_memory_space_constraint(v, pltpu.VMEM)


def unit_kernel(source, target, own_s, own_t):
    own_s[...] = unit_rows(source[...])
    own_t[...] = unit_rows(target[...])


def unit(source, target):
    return pl.pallas_call(
        unit_kernel,
        out_shape=[jax.ShapeDtypeStruct(v.shape, v.dtype) for v in (source, target)],
        in_specs=[VMEM] * 2,
        out_specs=[VMEM] * 2,
        compiler_params=PARAMS,
        name="unit",
    )(source, target)


def sums(meta, todo, near_parts, far_parts, tgt_parts):
    width = tgt_parts[0].shape[1]
    near_store = pltpu.VMEM((SLOTS, BLK, BLK), jnp.float32)
    far_store = pltpu.VMEM((2 * BLOCKS, BLK, BLK), jnp.float32)
    col_store = pltpu.VMEM((BLOCKS + 1, 8, BLK), jnp.float32)
    slab = pltpu.VMEM((BLOCKS * BLK, width), jnp.bfloat16)
    near_rows, near_cols, near_tiles, tgt = pl.pallas_call(
        near_kernel,
        out_shape=(pltpu.VMEM((SHARDS, HALF), jnp.float32), col_store, near_store, slab),
        in_specs=[SMEM, SMEM] + [VMEM] * (NEAR_PARTS + TGT_PARTS),
        out_specs=(VMEM,) * 4,
        scratch_shapes=[slab, pltpu.VMEM(((BLOCKS + 1) * BLK, HALF), jnp.float32)],
        compiler_params=PARAMS,
        cost_estimate=pl.CostEstimate(
            flops=40 * 2 * BLK * BLK * width, bytes_accessed=12 << 20, transcendentals=40 * BLK * BLK
        ),
        name="near_sums",
    )(meta, todo, *near_parts, *tgt_parts)
    row_sums, col_sums, far_tiles = pl.pallas_call(
        far_kernel,
        out_shape=(F32(SHARDS, HALF), F32(SHARDS, HALF), far_store),
        in_specs=[SMEM, SMEM] + [VMEM] * (FAR_PARTS + 3),
        out_specs=(VMEM,) * 3,
        scratch_shapes=[
            pltpu.VMEM((2 * BLK, width), jnp.bfloat16),
            pltpu.VMEM((3 * BLK, HALF), jnp.float32),
            col_store,
        ],
        compiler_params=PARAMS,
        name="far_sums",
    )(meta, todo, *far_parts, pinned(near_rows), pinned(near_cols), pinned(tgt))
    return row_sums, col_sums, near_tiles, far_tiles


def margins(meta, todo, row_all, col_all, near_tiles, far_tiles):
    return pl.pallas_call(
        margin_kernel,
        out_shape=(F32(SLOTS, BLK), F32(SLOTS, BLK), F32(1, HALF), F32(1, HALF)),
        in_specs=[SMEM, SMEM] + [VMEM] * 8,
        out_specs=(VMEM,) * 4,
        scratch_shapes=[
            pltpu.VMEM((SHARDS, HALF), jnp.float32),
            pltpu.VMEM((SHARDS, HALF), jnp.float32),
            pltpu.VMEM((BLOCKS * BLK, HALF), jnp.float32),
            pltpu.VMEM((SLOTS, 1, BLK), jnp.float32),
            pltpu.VMEM((SLOTS, 1, BLK), jnp.float32),
        ],
        compiler_params=PARAMS,
        name="margins",
    )(meta, todo, *row_all, *col_all, pinned(near_tiles), pinned(far_tiles))


def gather(own_s, own_t, todo):
    send = lambda v, axis, step: lax.ppermute(v, axis, ring(lax.axis_size(axis), step))
    after = lambda v, done: lax.optimization_barrier((v, done))
    near = [send(own_s, "zl", k) for k in REST]
    s_own = [send(own_s, "x", k) for k in (1, -1)]
    (t_y, again), s_own = after((own_t, own_s), s_own)
    s_own.append(send(again, "x", 2))
    t_own = [own_t] + [send(t_y, "y", k) for k in (1, -1, 2)]
    t_zh, near[0] = after(own_t, near[0])
    across = send(t_zh, "zh", 1)

    near, (todo, s_own) = after(near, (todo, s_own))
    rest = jnp.concatenate(near)
    up, down = send(rest, "x", 1), send(rest, "x", -1)
    across, t_own = after(across, t_own)
    t_own = jnp.concatenate(t_own)
    t_own_c = send(t_own, "c", 1)
    t_across = [across] + [send(across, "y", k) for k in (1, -1, 2)]

    (up, down), t_across = after((up, down), t_across)
    t_across_c = [send(v, "c", 1) for v in t_across]
    up_far, down_far = send(up[:192], "x", 1), send(down[192:], "x", -1)
    t_parts = [t_own, t_own_c] + t_across + t_across_c
    return [own_s, s_own[0], s_own[1], rest, up, down], [s_own[2], up_far, down_far], t_parts, todo


def total(row_sums, col_sums):
    send = lambda v, axis, step: lax.ppermute(v, axis, ring(lax.axis_size(axis), step))
    cols = col_sums + send(col_sums, "c", 1)
    rows = [row_sums] + [send(row_sums, "x", k) for k in (1, -1, 2)]
    cols = [cols] + [send(cols, "y", k) for k in (1, -1, 2)]
    rows, cols = lax.optimization_barrier((rows, cols))
    rows, cols = (rows[0] + rows[1]) + (rows[2] + rows[3]), (cols[0] + cols[1]) + (cols[2] + cols[3])
    return [rows] + [send(rows, "zl", k) for k in (1, -1, 2)], [cols, send(cols, "zh", 1)]


def listing(pairs, count, far_x):
    slot = jnp.arange(pairs.shape[0], dtype=jnp.int32)
    live = slot < count
    near = live & (pairs[:, 0] // 2 != far_x)
    kind = jnp.where(near, 0, jnp.where(live, 1, 2))
    key = kind * SLOTS + slot
    place = jnp.sum(key[None, :] < key[:, None], axis=1, dtype=jnp.int32)
    entry = jnp.concatenate([pairs, slot[:, None]], 1)
    todo = jnp.sum(jnp.where(place[None, :, None] == slot[:, None, None], entry[None], 0), axis=1)
    return todo.reshape(-1).astype(jnp.int32), jnp.sum(near, dtype=jnp.int32)


def per_device(source, target, pairs, counts):
    zh, y, c, x, zl = (lax.axis_index(a) for a in AXES)
    count = counts[0, 0]
    todo, near = listing(pairs[0, 0], count, (x + 2) % 4)
    meta = jnp.stack([count, zh, y, c, x, zl, x * 4 + zl, zh * 8 + y * 2 + c, near]).astype(jnp.int32)
    *pieces, (meta, todo) = gather(*unit(source, target), (meta, todo))
    row_sums, col_sums, near_tiles, far_tiles = sums(meta, todo, *pieces)
    row_all, col_all = total(row_sums, col_sums)
    row_best, col_best, src_piece, tgt_piece = margins(
        meta, todo, row_all, col_all, near_tiles, far_tiles
    )
    return (
        row_best.reshape(1, 1, SLOTS, BLK),
        col_best.reshape(1, 1, SLOTS, BLK),
        src_piece.reshape(HALF),
        tgt_piece.reshape(HALF),
    )


def solution(mesh):
    fine = Mesh(mesh.devices.reshape(2, 4, 2, 4, 4), AXES)
    src_axes, tgt_axes = AXES, GROUP + BANK
    return jax.shard_map(
        per_device,
        mesh=fine,
        in_specs=(
            P(src_axes, None),
            P(tgt_axes, None),
            P(BANK, GROUP, None, None),
            P(BANK, GROUP),
        ),
        out_specs=(
            P(BANK, GROUP, None, None),
            P(BANK, GROUP, None, None),
            P(src_axes),
            P(tgt_axes),
        ),
        check_vma=False,
    )
```

```python
import math

import jax
import jax.numpy as jnp
from jax import lax
from jax.experimental import pallas as pl
from jax.experimental.pallas import tpu as pltpu
from jax.sharding import Mesh
from jax.sharding import PartitionSpec as P

BLK = 256
HALF = 128
SLOTS = 48
BLOCKS = 8
SHARDS = 16
TEMP_INV = 20.0
EXP2_SCALE = TEMP_INV * math.log2(math.e)
HALF_TEMP = 0.5 / TEMP_INV
NT = (((1,), (1,)), ((), ()))
AXES = ("zh", "y", "c", "x", "zl")
BANK = ("zh", "y", "c")
GROUP = ("x", "zl")


def unit_rows(rows):
    values = rows.astype(jnp.float32)
    width = values.shape[-1]
    scale = lax.rsqrt(jnp.mean(values * values, axis=-1, keepdims=True) + 1e-06)
    return (values * (scale * (1.0 / math.sqrt(width)))).astype(jnp.bfloat16)


def ring(n, step):
    return [(i, (i + step) % n) for i in range(n)]


GROUP_TILES = 8

REST = (1, 3, 2)
NEAR_PLACE = {(0, 0, 0): (0, 0, 128), (1, 0, 0): (1, 0, 128), (3, 0, 0): (2, 0, 128)}
for order, dz in enumerate(REST):
    for part, dx in ((3, 0), (4, 1), (5, 3)):
        NEAR_PLACE[(dx, dz, 0)] = (part, 128 * order, 128)
NEAR_PARTS = 6
FAR_PLACE = {
    (2, 0, 0): (0, 0, 128),
    (2, 1, 0): (1, 0, 128),
    (2, 3, 0): (1, 128, 64),
    (2, 3, 64): (2, 0, 64),
    (2, 2, 0): (2, 64, 128),
}
FAR_PARTS = 3
TGT_PLACE = {}
for order, dy in enumerate((0, 1, 3, 2)):
    TGT_PLACE[(0, dy, 0)] = (0, 128 * order)
    TGT_PLACE[(0, dy, 1)] = (1, 128 * order)
    TGT_PLACE[(1, dy, 0)] = (2 + order, 0)
    TGT_PLACE[(1, dy, 1)] = (6 + order, 0)
TGT_PARTS = 10


def load_source(meta, place, parts, src, of_x):
    for (dx, dz, offset), (part, first, rows) in place.items():
        shard = of_x(dx) * 4 + lax.rem(meta[5] - dz + 4, 4)
        dst = pl.ds(pl.multiple_of(shard * HALF + offset, 64), rows)
        src[dst, :] = parts[part][first : first + rows, :]


def load_target(meta, parts, tgt):
    zh, y, c = meta[1], meta[2], meta[3]
    for (dh, dy, dc), (part, first) in TGT_PLACE.items():
        shard = lax.rem(zh + dh, 2) * 8 + lax.rem(y - dy + 4, 4) * 2 + lax.rem(c + dc, 2)
        dst = pl.ds(pl.multiple_of(shard * HALF, HALF), HALF)
        tgt[dst, :] = parts[part][first : first + HALF, :]


def add_tiles(todo, begin, n, width, src, row_of, tgt, tiles, acc_row, acc_col):
    dead_row = acc_row.shape[0] // BLK - 1

    def group(k, carry):
        for u in range(width):
            live = k * width + u < n
            q = jnp.minimum(k * width + u, n - 1)
            i, j = row_of(todo[3 * (begin + q)]), todo[3 * (begin + q) + 1]
            left = src[pl.ds(pl.multiple_of(i * BLK, BLK), BLK), :]
            right = tgt[pl.ds(pl.multiple_of(j * BLK, BLK), BLK), :]
            scores = lax.dot_general(left, right, NT, preferred_element_type=jnp.float32)
            tiles[q] = scores
            i = jnp.where(live, i, dead_row)
            j = jnp.where(live, j, BLOCKS)
            w = jnp.exp2(scores * EXP2_SCALE)
            rows = pl.ds(pl.multiple_of(i * BLK, BLK), BLK)
            acc_row[rows, :] += w[:, :HALF] + w[:, HALF:]
            acc_col[j] += w.reshape(BLK // 8, 8, BLK).sum(0)
        return carry

    lax.fori_loop(0, (n + width - 1) // width, group, 0)


def row_totals(acc_row, count):
    return jnp.concatenate(
        [
            jnp.sum(acc_row[h * HALF : (h + 1) * HALF, :].T, axis=0, keepdims=True)
            for h in range(count)
        ],
        0,
    )


def near_kernel(meta, todo, *refs):
    parts, refs = refs[: NEAR_PARTS + TGT_PARTS], refs[NEAR_PARTS + TGT_PARTS :]
    row_out, acc_col, tiles, tgt, src, acc_row = refs
    load_source(meta, NEAR_PLACE, parts[:NEAR_PARTS], src, lambda dx: lax.rem(meta[4] - dx + 4, 4))
    load_target(meta, parts[NEAR_PARTS:], tgt)
    acc_row[...] = jnp.zeros_like(acc_row)
    acc_col[...] = jnp.zeros_like(acc_col)
    add_tiles(todo, 0, meta[8], GROUP_TILES, src, lambda i: i, tgt, tiles, acc_row, acc_col)
    row_out[...] = row_totals(acc_row, SHARDS)


def far_kernel(meta, todo, *refs):
    parts, refs = refs[:FAR_PARTS], refs[FAR_PARTS:]
    row_in, col_in, tgt, row_out, col_out, tiles, src, acc_row, acc_col = refs
    load_source(meta, FAR_PLACE, parts, src, lambda dx: 0)
    acc_row[...] = jnp.zeros_like(acc_row)
    acc_col[...] = col_in[...]
    near = meta[8]
    add_tiles(todo, near, meta[0] - near, 4, src, lambda i: lax.rem(i, 2), tgt, tiles, acc_row, acc_col)
    far_rows = row_totals(acc_row, 4)
    rows = row_in[...]
    far_x = lax.rem(meta[4] + 2, 4)
    rows = jnp.concatenate(
        [rows[4 * v : 4 * v + 4] + jnp.where(far_x == v, far_rows, 0.0) for v in range(4)], 0
    )
    row_out[...] = rows
    cols = []
    for j in range(BLOCKS):
        col = jnp.sum(acc_col[j], axis=0, keepdims=True)
        cols += [col[:, :HALF], col[:, HALF:]]
    col_out[...] = jnp.concatenate(cols, 0)


def margin_kernel(meta, todo, r0, r1, r2, r3, c0, c1, near_tiles, far_tiles, row_best, col_best,
                  src_piece, tgt_piece, s16, t16, s_cols, row_slots, col_slots):
    s16[...] = jnp.log((r0[...] + r1[...]) + (r2[...] + r3[...])) * HALF_TEMP
    t16[...] = jnp.log(c0[...] + c1[...]) * HALF_TEMP
    row_slots[...] = jnp.zeros_like(row_slots)
    col_slots[...] = jnp.zeros_like(col_slots)
    for h in range(SHARDS):
        s_cols[h * HALF : (h + 1) * HALF, :] = jnp.broadcast_to(
            s16[h : h + 1, :], (HALF, HALF)
        ).T
    src_piece[...] = s16[pl.ds(meta[6], 1), :] * (2 * TEMP_INV)
    tgt_piece[...] = t16[pl.ds(meta[7], 1), :] * (2 * TEMP_INV)

    def best_of(begin, n, width, tiles):
        def group(k, carry):
            for u in range(width):
                q = jnp.minimum(k * width + u, n - 1)
                i, j, p = (todo[3 * (begin + q) + v] for v in range(3))
                ta, tb = t16[pl.ds(2 * j, 1), :], t16[pl.ds(2 * j + 1, 1), :]
                sa, sb = s16[pl.ds(2 * i, 1), :], s16[pl.ds(2 * i + 1, 1), :]
                sc = s_cols[pl.ds(pl.multiple_of(i * BLK, BLK), BLK), :]
                scores = tiles[q]
                ua, ub = scores[:, :HALF], scores[:, HALF:]
                best = jnp.maximum(ua - ta, ub - tb)
                ra = jnp.max(best[:HALF].T, axis=0, keepdims=True)
                rb = jnp.max(best[HALF:].T, axis=0, keepdims=True)
                ca = jnp.max(ua - sc, axis=0, keepdims=True)
                cb = jnp.max(ub - sc, axis=0, keepdims=True)
                row_slots[p] = jnp.concatenate([ra - sa, rb - sb], 1) * TEMP_INV
                col_slots[p] = jnp.concatenate([ca - ta, cb - tb], 1) * TEMP_INV
            return carry

        lax.fori_loop(0, (n + width - 1) // width, group, 0)

    near = meta[8]
    best_of(0, near, GROUP_TILES, near_tiles)
    best_of(near, meta[0] - near, 4, far_tiles)
    for k in range(0, SLOTS, 8):
        row_best[k : k + 8, :] = jnp.concatenate([row_slots[k + v] for v in range(8)], 0)
        col_best[k : k + 8, :] = jnp.concatenate([col_slots[k + v] for v in range(8)], 0)


VMEM = pl.BlockSpec(memory_space=pltpu.VMEM)
SMEM = pl.BlockSpec(memory_space=pltpu.SMEM)


F32 = lambda *shape: jax.ShapeDtypeStruct(shape, jnp.float32)
PARAMS = pltpu.CompilerParams(vmem_limit_bytes=20 * 1024 * 1024)


def pinned(v):
    return pltpu.with_memory_space_constraint(v, pltpu.VMEM)


def unit_kernel(source, target, own_s, own_t, s_rows, t_rows, sems):
    copies = [
        pltpu.make_async_copy(source, s_rows, sems.at[0]),
        pltpu.make_async_copy(target, t_rows, sems.at[1]),
    ]
    for copy in copies:
        copy.start()
    copies[0].wait()
    own_s[...] = unit_rows(s_rows[...])
    copies[1].wait()
    own_t[...] = unit_rows(t_rows[...])


def unit(source, target):
    return pl.pallas_call(
        unit_kernel,
        out_shape=[jax.ShapeDtypeStruct(v.shape, v.dtype) for v in (source, target)],
        in_specs=[pl.BlockSpec(memory_space=pltpu.HBM)] * 2,
        out_specs=[VMEM] * 2,
        scratch_shapes=[pltpu.VMEM(v.shape, v.dtype) for v in (source, target)]
        + [pltpu.SemaphoreType.DMA((2,))],
        compiler_params=PARAMS,
        name="unit",
    )(*(pltpu.with_memory_space_constraint(v, pltpu.HBM) for v in (source, target)))


def sums(meta, todo, near_parts, far_parts, tgt_parts):
    width = tgt_parts[0].shape[1]
    near_store = pltpu.VMEM((SLOTS, BLK, BLK), jnp.float32)
    far_store = pltpu.VMEM((2 * BLOCKS, BLK, BLK), jnp.float32)
    col_store = pltpu.VMEM((BLOCKS + 1, 8, BLK), jnp.float32)
    slab = pltpu.VMEM((BLOCKS * BLK, width), jnp.bfloat16)
    near_rows, near_cols, near_tiles, tgt = pl.pallas_call(
        near_kernel,
        out_shape=(pltpu.VMEM((SHARDS, HALF), jnp.float32), col_store, near_store, slab),
        in_specs=[SMEM, SMEM] + [VMEM] * (NEAR_PARTS + TGT_PARTS),
        out_specs=(VMEM,) * 4,
        scratch_shapes=[slab, pltpu.VMEM(((BLOCKS + 1) * BLK, HALF), jnp.float32)],
        compiler_params=PARAMS,
        cost_estimate=pl.CostEstimate(
            flops=40 * 2 * BLK * BLK * width, bytes_accessed=12 << 20, transcendentals=40 * BLK * BLK
        ),
        name="near_sums",
    )(meta, todo, *near_parts, *tgt_parts)
    row_sums, col_sums, far_tiles = pl.pallas_call(
        far_kernel,
        out_shape=(F32(SHARDS, HALF), F32(SHARDS, HALF), far_store),
        in_specs=[SMEM, SMEM] + [VMEM] * (FAR_PARTS + 3),
        out_specs=(VMEM,) * 3,
        scratch_shapes=[
            pltpu.VMEM((2 * BLK, width), jnp.bfloat16),
            pltpu.VMEM((3 * BLK, HALF), jnp.float32),
            col_store,
        ],
        compiler_params=PARAMS,
        name="far_sums",
    )(meta, todo, *far_parts, pinned(near_rows), pinned(near_cols), pinned(tgt))
    return row_sums, col_sums, near_tiles, far_tiles


def margins(meta, todo, row_all, col_all, near_tiles, far_tiles):
    return pl.pallas_call(
        margin_kernel,
        out_shape=(F32(SLOTS, BLK), F32(SLOTS, BLK), F32(1, HALF), F32(1, HALF)),
        in_specs=[SMEM, SMEM] + [VMEM] * 8,
        out_specs=(VMEM,) * 4,
        scratch_shapes=[
            pltpu.VMEM((SHARDS, HALF), jnp.float32),
            pltpu.VMEM((SHARDS, HALF), jnp.float32),
            pltpu.VMEM((BLOCKS * BLK, HALF), jnp.float32),
            pltpu.VMEM((SLOTS, 1, BLK), jnp.float32),
            pltpu.VMEM((SLOTS, 1, BLK), jnp.float32),
        ],
        compiler_params=PARAMS,
        name="margins",
    )(meta, todo, *row_all, *col_all, pinned(near_tiles), pinned(far_tiles))


def gather(own_s, own_t, todo):
    send = lambda v, axis, step: lax.ppermute(v, axis, ring(lax.axis_size(axis), step))
    after = lambda v, done: lax.optimization_barrier((v, done))
    near = [send(own_s, "zl", k) for k in REST]
    s_own = [send(own_s, "x", k) for k in (1, -1)]
    (t_y, again), s_own = after((own_t, own_s), s_own)
    t_near = [send(t_y, "y", k) for k in (1, -1)]
    (t_zh, again), t_near = after((t_y, again), t_near)
    across = send(t_zh, "zh", 1)
    t_own = [own_t] + t_near + [send(t_zh, "y", 2)]
    s_own.append(send(again, "x", 2))

    near, (todo, across, s_own) = after(near, (todo, across, s_own))
    rest = jnp.concatenate(near)
    up, down = send(rest, "x", 1), send(rest, "x", -1)
    t_own = jnp.concatenate(t_own)
    t_own_c = send(t_own, "c", 1)
    across, t_own_c = after(across, t_own_c)
    t_across = [across] + [send(across, "y", k) for k in (2, 1, -1)]
    t_across = [t_across[0], t_across[2], t_across[3], t_across[1]]

    up_far, down_far = send(up[:192], "x", 1), send(down[192:], "x", -1)
    t_across_c = [send(v, "c", 1) for v in t_across]
    t_parts = [t_own, t_own_c] + t_across + t_across_c
    return [own_s, s_own[0], s_own[1], rest, up, down], [s_own[2], up_far, down_far], t_parts, todo


def total(row_sums, col_sums):
    send = lambda v, axis, step: lax.ppermute(v, axis, ring(lax.axis_size(axis), step))
    cols = col_sums + send(col_sums, "c", 1)
    rows = [row_sums] + [send(row_sums, "x", k) for k in (1, -1, 2)]
    cols = [cols] + [send(cols, "y", k) for k in (1, -1, 2)]
    rows, cols = lax.optimization_barrier((rows, cols))
    rows, cols = (rows[0] + rows[1]) + (rows[2] + rows[3]), (cols[0] + cols[1]) + (cols[2] + cols[3])
    return [rows] + [send(rows, "zl", k) for k in (1, -1, 2)], [cols, send(cols, "zh", 1)]


def listing(pairs, count, far_x):
    slot = jnp.arange(pairs.shape[0], dtype=jnp.int32)
    live = slot < count
    near = live & (pairs[:, 0] // 2 != far_x)
    kind = jnp.where(near, 0, jnp.where(live, 1, 2))
    key = kind * SLOTS + slot
    place = jnp.sum(key[None, :] < key[:, None], axis=1, dtype=jnp.int32)
    entry = jnp.concatenate([pairs, slot[:, None]], 1)
    todo = jnp.sum(jnp.where(place[None, :, None] == slot[:, None, None], entry[None], 0), axis=1)
    return todo.reshape(-1).astype(jnp.int32), jnp.sum(near, dtype=jnp.int32)


def per_device(source, target, pairs, counts):
    zh, y, c, x, zl = (lax.axis_index(a) for a in AXES)
    count = counts[0, 0]
    todo, near = listing(pairs[0, 0], count, (x + 2) % 4)
    meta = jnp.stack([count, zh, y, c, x, zl, x * 4 + zl, zh * 8 + y * 2 + c, near]).astype(jnp.int32)
    *pieces, (meta, todo) = gather(*unit(source, target), (meta, todo))
    row_sums, col_sums, near_tiles, far_tiles = sums(meta, todo, *pieces)
    row_all, col_all = total(row_sums, col_sums)
    row_best, col_best, src_piece, tgt_piece = margins(
        meta, todo, row_all, col_all, near_tiles, far_tiles
    )
    return (
        row_best.reshape(1, 1, SLOTS, BLK),
        col_best.reshape(1, 1, SLOTS, BLK),
        src_piece.reshape(HALF),
        tgt_piece.reshape(HALF),
    )


def solution(mesh):
    fine = Mesh(mesh.devices.reshape(2, 4, 2, 4, 4), AXES)
    src_axes, tgt_axes = AXES, GROUP + BANK
    return jax.shard_map(
        per_device,
        mesh=fine,
        in_specs=(
            P(src_axes, None),
            P(tgt_axes, None),
            P(BANK, GROUP, None, None),
            P(BANK, GROUP),
        ),
        out_specs=(
            P(BANK, GROUP, None, None),
            P(BANK, GROUP, None, None),
            P(src_axes),
            P(tgt_axes),
        ),
        check_vma=False,
    )
```

```python
import math

import jax
import jax.numpy as jnp
from jax import lax
from jax.experimental import pallas as pl
from jax.experimental.pallas import tpu as pltpu
from jax.sharding import Mesh
from jax.sharding import PartitionSpec as P

BLK = 256
HALF = 128
SLOTS = 48
BLOCKS = 8
SHARDS = 16
TEMP_INV = 20.0
EXP2_SCALE = TEMP_INV * math.log2(math.e)
HALF_TEMP = 0.5 / TEMP_INV
NT = (((1,), (1,)), ((), ()))
AXES = ("zh", "y", "c", "x", "zl")
BANK = ("zh", "y", "c")
GROUP = ("x", "zl")


def unit_rows(rows):
    values = rows.astype(jnp.float32)
    width = values.shape[-1]
    scale = lax.rsqrt(jnp.mean(values * values, axis=-1, keepdims=True) + 1e-06)
    return (values * (scale * (1.0 / math.sqrt(width)))).astype(jnp.bfloat16)


def ring(n, step):
    return [(i, (i + step) % n) for i in range(n)]


GROUP_TILES = 8

REST = (1, 3, 2)
NEAR_PLACE = {(0, 0, 0): (0, 0, 128), (1, 0, 0): (1, 0, 128), (3, 0, 0): (2, 0, 128)}
for order, dz in enumerate(REST):
    for part, dx in ((3, 0), (4, 1), (5, 3)):
        NEAR_PLACE[(dx, dz, 0)] = (part, 128 * order, 128)
NEAR_PARTS = 6
FAR_PLACE = {
    (2, 0, 0): (0, 0, 128),
    (2, 1, 0): (1, 0, 128),
    (2, 3, 0): (1, 128, 64),
    (2, 3, 64): (2, 0, 64),
    (2, 2, 0): (2, 64, 128),
}
FAR_PARTS = 3
TGT_PLACE = {}
for order, dy in enumerate((0, 1, 3, 2)):
    TGT_PLACE[(0, dy, 0)] = (0, 128 * order)
    TGT_PLACE[(0, dy, 1)] = (1, 128 * order)
    TGT_PLACE[(1, dy, 0)] = (2 + order, 0)
    TGT_PLACE[(1, dy, 1)] = (6 + order, 0)
TGT_PARTS = 10


def load_source(meta, place, parts, src, of_x):
    for (dx, dz, offset), (part, first, rows) in place.items():
        shard = of_x(dx) * 4 + lax.rem(meta[5] - dz + 4, 4)
        dst = pl.ds(pl.multiple_of(shard * HALF + offset, 64), rows)
        src[dst, :] = parts[part][first : first + rows, :]


def load_target(meta, parts, tgt):
    zh, y, c = meta[1], meta[2], meta[3]
    for (dh, dy, dc), (part, first) in TGT_PLACE.items():
        shard = lax.rem(zh + dh, 2) * 8 + lax.rem(y - dy + 4, 4) * 2 + lax.rem(c + dc, 2)
        dst = pl.ds(pl.multiple_of(shard * HALF, HALF), HALF)
        tgt[dst, :] = parts[part][first : first + HALF, :]


def add_tiles(todo, begin, n, width, src, row_of, tgt, tiles, acc_row, acc_col):
    dead_row = acc_row.shape[0] // BLK - 1

    def group(k, carry):
        for u in range(width):
            live = k * width + u < n
            q = jnp.minimum(k * width + u, n - 1)
            i, j = row_of(todo[3 * (begin + q)]), todo[3 * (begin + q) + 1]
            left = src[pl.ds(pl.multiple_of(i * BLK, BLK), BLK), :]
            right = tgt[pl.ds(pl.multiple_of(j * BLK, BLK), BLK), :]
            scores = lax.dot_general(left, right, NT, preferred_element_type=jnp.float32)
            tiles[q] = scores
            i = jnp.where(live, i, dead_row)
            j = jnp.where(live, j, BLOCKS)
            w = jnp.exp2(scores * EXP2_SCALE)
            rows = pl.ds(pl.multiple_of(i * BLK, BLK), BLK)
            acc_row[rows, :] += w[:, :HALF] + w[:, HALF:]
            acc_col[j] += w.reshape(BLK // 8, 8, BLK).sum(0)
        return carry

    lax.fori_loop(0, (n + width - 1) // width, group, 0)


def row_totals(acc_row, count):
    return jnp.concatenate(
        [
            jnp.sum(acc_row[h * HALF : (h + 1) * HALF, :].T, axis=0, keepdims=True)
            for h in range(count)
        ],
        0,
    )


def near_kernel(meta, todo, *refs):
    parts, refs = refs[: NEAR_PARTS + TGT_PARTS], refs[NEAR_PARTS + TGT_PARTS :]
    row_out, acc_col, tiles, tgt, src, acc_row = refs
    load_source(meta, NEAR_PLACE, parts[:NEAR_PARTS], src, lambda dx: lax.rem(meta[4] - dx + 4, 4))
    load_target(meta, parts[NEAR_PARTS:], tgt)
    acc_row[...] = jnp.zeros_like(acc_row)
    acc_col[...] = jnp.zeros_like(acc_col)
    add_tiles(todo, 0, meta[8], GROUP_TILES, src, lambda i: i, tgt, tiles, acc_row, acc_col)
    row_out[...] = row_totals(acc_row, SHARDS)


def far_kernel(meta, todo, *refs):
    parts, refs = refs[:FAR_PARTS], refs[FAR_PARTS:]
    row_in, col_in, tgt, row_out, col_out, tiles, src, acc_row, acc_col = refs
    load_source(meta, FAR_PLACE, parts, src, lambda dx: 0)
    acc_row[...] = jnp.zeros_like(acc_row)
    acc_col[...] = col_in[...]
    near = meta[8]
    add_tiles(todo, near, meta[0] - near, 4, src, lambda i: lax.rem(i, 2), tgt, tiles, acc_row, acc_col)
    far_rows = row_totals(acc_row, 4)
    rows = row_in[...]
    far_x = lax.rem(meta[4] + 2, 4)
    rows = jnp.concatenate(
        [rows[4 * v : 4 * v + 4] + jnp.where(far_x == v, far_rows, 0.0) for v in range(4)], 0
    )
    row_out[...] = rows
    cols = []
    for j in range(BLOCKS):
        col = jnp.sum(acc_col[j], axis=0, keepdims=True)
        cols += [col[:, :HALF], col[:, HALF:]]
    col_out[...] = jnp.concatenate(cols, 0)


def margin_kernel(meta, todo, r0, r1, r2, r3, c0, c1, near_tiles, far_tiles, row_best, col_best,
                  src_piece, tgt_piece, s16, t16, s_cols, row_slots, col_slots):
    s16[...] = jnp.log((r0[...] + r1[...]) + (r2[...] + r3[...])) * HALF_TEMP
    t16[...] = jnp.log(c0[...] + c1[...]) * HALF_TEMP
    row_slots[...] = jnp.zeros_like(row_slots)
    col_slots[...] = jnp.zeros_like(col_slots)
    for h in range(SHARDS):
        s_cols[h * HALF : (h + 1) * HALF, :] = jnp.broadcast_to(
            s16[h : h + 1, :], (HALF, HALF)
        ).T
    src_piece[...] = s16[pl.ds(meta[6], 1), :] * (2 * TEMP_INV)
    tgt_piece[...] = t16[pl.ds(meta[7], 1), :] * (2 * TEMP_INV)

    def best_of(begin, n, width, tiles):
        def group(k, carry):
            for u in range(width):
                q = jnp.minimum(k * width + u, n - 1)
                i, j, p = (todo[3 * (begin + q) + v] for v in range(3))
                ta, tb = t16[pl.ds(2 * j, 1), :], t16[pl.ds(2 * j + 1, 1), :]
                sa, sb = s16[pl.ds(2 * i, 1), :], s16[pl.ds(2 * i + 1, 1), :]
                sc = s_cols[pl.ds(pl.multiple_of(i * BLK, BLK), BLK), :]
                scores = tiles[q]
                ua, ub = scores[:, :HALF], scores[:, HALF:]
                best = jnp.maximum(ua - ta, ub - tb)
                ra = jnp.max(best[:HALF].T, axis=0, keepdims=True)
                rb = jnp.max(best[HALF:].T, axis=0, keepdims=True)
                ca = jnp.max(ua - sc, axis=0, keepdims=True)
                cb = jnp.max(ub - sc, axis=0, keepdims=True)
                row_slots[p] = jnp.concatenate([ra - sa, rb - sb], 1) * TEMP_INV
                col_slots[p] = jnp.concatenate([ca - ta, cb - tb], 1) * TEMP_INV
            return carry

        lax.fori_loop(0, (n + width - 1) // width, group, 0)

    near = meta[8]
    best_of(0, near, GROUP_TILES, near_tiles)
    best_of(near, meta[0] - near, 4, far_tiles)
    for k in range(0, SLOTS, 8):
        row_best[k : k + 8, :] = jnp.concatenate([row_slots[k + v] for v in range(8)], 0)
        col_best[k : k + 8, :] = jnp.concatenate([col_slots[k + v] for v in range(8)], 0)


VMEM = pl.BlockSpec(memory_space=pltpu.VMEM)
SMEM = pl.BlockSpec(memory_space=pltpu.SMEM)


F32 = lambda *shape: jax.ShapeDtypeStruct(shape, jnp.float32)
PARAMS = pltpu.CompilerParams(vmem_limit_bytes=20 * 1024 * 1024)


def pinned(v):
    return pltpu.with_memory_space_constraint(v, pltpu.VMEM)


def unit_kernel(source, target, own_s, own_t, s_rows, t_rows, sems):
    copies = [
        pltpu.make_async_copy(source, s_rows, sems.at[0]),
        pltpu.make_async_copy(target, t_rows, sems.at[1]),
    ]
    for copy in copies:
        copy.start()
    copies[0].wait()
    own_s[...] = unit_rows(s_rows[...])
    copies[1].wait()
    own_t[...] = unit_rows(t_rows[...])


def unit(source, target):
    return pl.pallas_call(
        unit_kernel,
        out_shape=[jax.ShapeDtypeStruct(v.shape, v.dtype) for v in (source, target)],
        in_specs=[pl.BlockSpec(memory_space=pltpu.HBM)] * 2,
        out_specs=[VMEM] * 2,
        scratch_shapes=[pltpu.VMEM(v.shape, v.dtype) for v in (source, target)]
        + [pltpu.SemaphoreType.DMA((2,))],
        compiler_params=PARAMS,
        name="unit",
    )(*(pltpu.with_memory_space_constraint(v, pltpu.HBM) for v in (source, target)))


def sums(meta, todo, near_parts, far_parts, tgt_parts):
    width = tgt_parts[0].shape[1]
    near_store = pltpu.VMEM((SLOTS, BLK, BLK), jnp.float32)
    far_store = pltpu.VMEM((2 * BLOCKS, BLK, BLK), jnp.float32)
    col_store = pltpu.VMEM((BLOCKS + 1, 8, BLK), jnp.float32)
    slab = pltpu.VMEM((BLOCKS * BLK, width), jnp.bfloat16)
    near_rows, near_cols, near_tiles, tgt = pl.pallas_call(
        near_kernel,
        out_shape=(pltpu.VMEM((SHARDS, HALF), jnp.float32), col_store, near_store, slab),
        in_specs=[SMEM, SMEM] + [VMEM] * (NEAR_PARTS + TGT_PARTS),
        out_specs=(VMEM,) * 4,
        scratch_shapes=[slab, pltpu.VMEM(((BLOCKS + 1) * BLK, HALF), jnp.float32)],
        compiler_params=PARAMS,
        cost_estimate=pl.CostEstimate(
            flops=40 * 2 * BLK * BLK * width, bytes_accessed=12 << 20, transcendentals=40 * BLK * BLK
        ),
        name="near_sums",
    )(meta, todo, *near_parts, *tgt_parts)
    row_sums, col_sums, far_tiles = pl.pallas_call(
        far_kernel,
        out_shape=(F32(SHARDS, HALF), F32(SHARDS, HALF), far_store),
        in_specs=[SMEM, SMEM] + [VMEM] * (FAR_PARTS + 3),
        out_specs=(VMEM,) * 3,
        scratch_shapes=[
            pltpu.VMEM((2 * BLK, width), jnp.bfloat16),
            pltpu.VMEM((3 * BLK, HALF), jnp.float32),
            col_store,
        ],
        compiler_params=PARAMS,
        name="far_sums",
    )(meta, todo, *far_parts, pinned(near_rows), pinned(near_cols), pinned(tgt))
    return row_sums, col_sums, near_tiles, far_tiles


def margins(meta, todo, row_all, col_all, near_tiles, far_tiles):
    return pl.pallas_call(
        margin_kernel,
        out_shape=(F32(SLOTS, BLK), F32(SLOTS, BLK), F32(1, HALF), F32(1, HALF)),
        in_specs=[SMEM, SMEM] + [VMEM] * 8,
        out_specs=(VMEM,) * 4,
        scratch_shapes=[
            pltpu.VMEM((SHARDS, HALF), jnp.float32),
            pltpu.VMEM((SHARDS, HALF), jnp.float32),
            pltpu.VMEM((BLOCKS * BLK, HALF), jnp.float32),
            pltpu.VMEM((SLOTS, 1, BLK), jnp.float32),
            pltpu.VMEM((SLOTS, 1, BLK), jnp.float32),
        ],
        compiler_params=PARAMS,
        name="margins",
    )(meta, todo, *row_all, *col_all, pinned(near_tiles), pinned(far_tiles))


def gather(own_s, own_t, todo):
    send = lambda v, axis, step: lax.ppermute(v, axis, ring(lax.axis_size(axis), step))
    after = lambda v, done: lax.optimization_barrier((v, done))
    near = [send(own_s, "zl", k) for k in REST]
    s_own = [send(own_s, "x", k) for k in (1, -1)]
    (t_y, again), s_own = after((own_t, own_s), s_own)
    s_own.append(send(again, "x", 2))
    t_own = [own_t] + [send(t_y, "y", k) for k in (1, -1, 2)]
    t_zh, near[0] = after(own_t, near[0])
    across = send(t_zh, "zh", 1)

    near, (todo, s_own) = after(near, (todo, s_own))
    rest = jnp.concatenate(near)
    up, down = send(rest, "x", 1), send(rest, "x", -1)
    t_own = jnp.concatenate(t_own)
    t_own_c = send(t_own, "c", 1)
    across, t_own_c = after(across, t_own_c)
    t_across = [across] + [send(across, "y", k) for k in (2, 1, -1)]
    t_across = [t_across[0], t_across[2], t_across[3], t_across[1]]

    up_far, down_far = send(up[:192], "x", 1), send(down[192:], "x", -1)
    t_across_c = [send(v, "c", 1) for v in t_across]
    t_parts = [t_own, t_own_c] + t_across + t_across_c
    return [own_s, s_own[0], s_own[1], rest, up, down], [s_own[2], up_far, down_far], t_parts, todo


def total(row_sums, col_sums):
    send = lambda v, axis, step: lax.ppermute(v, axis, ring(lax.axis_size(axis), step))
    cols = col_sums + send(col_sums, "c", 1)
    rows = [row_sums] + [send(row_sums, "x", k) for k in (1, -1, 2)]
    cols = [cols] + [send(cols, "y", k) for k in (1, -1, 2)]
    rows, cols = lax.optimization_barrier((rows, cols))
    rows, cols = (rows[0] + rows[1]) + (rows[2] + rows[3]), (cols[0] + cols[1]) + (cols[2] + cols[3])
    return [rows] + [send(rows, "zl", k) for k in (1, -1, 2)], [cols, send(cols, "zh", 1)]


def listing(pairs, count, far_x):
    slot = jnp.arange(pairs.shape[0], dtype=jnp.int32)
    live = slot < count
    near = live & (pairs[:, 0] // 2 != far_x)
    kind = jnp.where(near, 0, jnp.where(live, 1, 2))
    key = kind * SLOTS + slot
    place = jnp.sum(key[None, :] < key[:, None], axis=1, dtype=jnp.int32)
    entry = jnp.concatenate([pairs, slot[:, None]], 1)
    todo = jnp.sum(jnp.where(place[None, :, None] == slot[:, None, None], entry[None], 0), axis=1)
    return todo.reshape(-1).astype(jnp.int32), jnp.sum(near, dtype=jnp.int32)


def per_device(source, target, pairs, counts):
    zh, y, c, x, zl = (lax.axis_index(a) for a in AXES)
    count = counts[0, 0]
    todo, near = listing(pairs[0, 0], count, (x + 2) % 4)
    meta = jnp.stack([count, zh, y, c, x, zl, x * 4 + zl, zh * 8 + y * 2 + c, near]).astype(jnp.int32)
    *pieces, (meta, todo) = gather(*unit(source, target), (meta, todo))
    row_sums, col_sums, near_tiles, far_tiles = sums(meta, todo, *pieces)
    row_all, col_all = total(row_sums, col_sums)
    row_best, col_best, src_piece, tgt_piece = margins(
        meta, todo, row_all, col_all, near_tiles, far_tiles
    )
    return (
        row_best.reshape(1, 1, SLOTS, BLK),
        col_best.reshape(1, 1, SLOTS, BLK),
        src_piece.reshape(HALF),
        tgt_piece.reshape(HALF),
    )


def solution(mesh):
    fine = Mesh(mesh.devices.reshape(2, 4, 2, 4, 4), AXES)
    src_axes, tgt_axes = AXES, GROUP + BANK
    return jax.shard_map(
        per_device,
        mesh=fine,
        in_specs=(
            P(src_axes, None),
            P(tgt_axes, None),
            P(BANK, GROUP, None, None),
            P(BANK, GROUP),
        ),
        out_specs=(
            P(BANK, GROUP, None, None),
            P(BANK, GROUP, None, None),
            P(src_axes),
            P(tgt_axes),
        ),
        check_vma=False,
    )
```

```python
import math

import jax
import jax.numpy as jnp
from jax import lax
from jax.experimental import pallas as pl
from jax.experimental.pallas import tpu as pltpu
from jax.sharding import Mesh
from jax.sharding import PartitionSpec as P

BLK = 256
HALF = 128
SLOTS = 48
BLOCKS = 8
SHARDS = 16
TEMP_INV = 20.0
EXP2_SCALE = TEMP_INV * math.log2(math.e)
HALF_TEMP = 0.5 / TEMP_INV
NT = (((1,), (1,)), ((), ()))
AXES = ("zh", "y", "c", "x", "zl")
BANK = ("zh", "y", "c")
GROUP = ("x", "zl")


def unit_rows(rows):
    values = rows.astype(jnp.float32)
    width = values.shape[-1]
    scale = lax.rsqrt(jnp.mean(values * values, axis=-1, keepdims=True) + 1e-06)
    return (values * (scale * (1.0 / math.sqrt(width)))).astype(jnp.bfloat16)


def ring(n, step):
    return [(i, (i + step) % n) for i in range(n)]


GROUP_TILES = 8

REST = (1, 3, 2)
NEAR_PLACE = {(0, 0, 0): (0, 0, 128), (1, 0, 0): (1, 0, 128), (3, 0, 0): (2, 0, 128)}
for order, dz in enumerate(REST):
    for part, dx in ((3, 0), (4, 1), (5, 3)):
        NEAR_PLACE[(dx, dz, 0)] = (part, 128 * order, 128)
NEAR_PARTS = 6
FAR_PLACE = {
    (2, 0, 0): (0, 0, 128),
    (2, 1, 0): (1, 0, 128),
    (2, 3, 0): (1, 128, 64),
    (2, 3, 64): (2, 0, 64),
    (2, 2, 0): (2, 64, 128),
}
FAR_PARTS = 3
TGT_PLACE = {}
for order, dy in enumerate((0, 1, 3, 2)):
    TGT_PLACE[(0, dy, 0)] = (0, 128 * order)
    TGT_PLACE[(0, dy, 1)] = (1, 128 * order)
for order, dy in enumerate((0, 2, 1, 3)):
    TGT_PLACE[(1, dy, 0)] = (2 + order, 0)
    TGT_PLACE[(1, dy, 1)] = (6 + order, 0)
TGT_PARTS = 10


def load_source(meta, place, parts, src, of_x):
    for (dx, dz, offset), (part, first, rows) in place.items():
        shard = of_x(dx) * 4 + lax.rem(meta[5] - dz + 4, 4)
        dst = pl.ds(pl.multiple_of(shard * HALF + offset, 64), rows)
        src[dst, :] = parts[part][first : first + rows, :]


def load_target(meta, parts, tgt):
    zh, y, c = meta[1], meta[2], meta[3]
    for (dh, dy, dc), (part, first) in TGT_PLACE.items():
        shard = lax.rem(zh + dh, 2) * 8 + lax.rem(y - dy + 4, 4) * 2 + lax.rem(c + dc, 2)
        dst = pl.ds(pl.multiple_of(shard * HALF, HALF), HALF)
        tgt[dst, :] = parts[part][first : first + HALF, :]


def add_tiles(todo, begin, n, width, src, row_of, tgt, tiles, acc_row, acc_col):
    dead_row = acc_row.shape[0] // BLK - 1

    def group(k, carry):
        for u in range(width):
            live = k * width + u < n
            q = jnp.minimum(k * width + u, n - 1)
            i, j = row_of(todo[3 * (begin + q)]), todo[3 * (begin + q) + 1]
            left = src[pl.ds(pl.multiple_of(i * BLK, BLK), BLK), :]
            right = tgt[pl.ds(pl.multiple_of(j * BLK, BLK), BLK), :]
            scores = lax.dot_general(left, right, NT, preferred_element_type=jnp.float32)
            tiles[q] = scores
            i = jnp.where(live, i, dead_row)
            j = jnp.where(live, j, BLOCKS)
            w = jnp.exp2(scores * EXP2_SCALE)
            rows = pl.ds(pl.multiple_of(i * BLK, BLK), BLK)
            acc_row[rows, :] += w[:, :HALF] + w[:, HALF:]
            acc_col[j] += w.reshape(BLK // 8, 8, BLK).sum(0)
        return carry

    lax.fori_loop(0, (n + width - 1) // width, group, 0)


def row_totals(acc_row, count):
    return jnp.concatenate(
        [
            jnp.sum(acc_row[h * HALF : (h + 1) * HALF, :].T, axis=0, keepdims=True)
            for h in range(count)
        ],
        0,
    )


def near_kernel(meta, todo, *refs):
    parts, refs = refs[: NEAR_PARTS + TGT_PARTS], refs[NEAR_PARTS + TGT_PARTS :]
    row_out, acc_col, tiles, tgt, src, acc_row = refs
    load_source(meta, NEAR_PLACE, parts[:NEAR_PARTS], src, lambda dx: lax.rem(meta[4] - dx + 4, 4))
    load_target(meta, parts[NEAR_PARTS:], tgt)
    acc_row[...] = jnp.zeros_like(acc_row)
    acc_col[...] = jnp.zeros_like(acc_col)
    add_tiles(todo, 0, meta[8], GROUP_TILES, src, lambda i: i, tgt, tiles, acc_row, acc_col)
    row_out[...] = row_totals(acc_row, SHARDS)


def far_kernel(meta, todo, *refs):
    parts, refs = refs[:FAR_PARTS], refs[FAR_PARTS:]
    row_in, col_in, tgt, row_out, col_out, tiles, src, acc_row, acc_col = refs
    load_source(meta, FAR_PLACE, parts, src, lambda dx: 0)
    acc_row[...] = jnp.zeros_like(acc_row)
    acc_col[...] = col_in[...]
    near = meta[8]
    add_tiles(todo, near, meta[0] - near, 4, src, lambda i: lax.rem(i, 2), tgt, tiles, acc_row, acc_col)
    far_rows = row_totals(acc_row, 4)
    rows = row_in[...]
    far_x = lax.rem(meta[4] + 2, 4)
    rows = jnp.concatenate(
        [rows[4 * v : 4 * v + 4] + jnp.where(far_x == v, far_rows, 0.0) for v in range(4)], 0
    )
    row_out[...] = rows
    cols = []
    for j in range(BLOCKS):
        col = jnp.sum(acc_col[j], axis=0, keepdims=True)
        cols += [col[:, :HALF], col[:, HALF:]]
    col_out[...] = jnp.concatenate(cols, 0)


def margin_kernel(meta, todo, r0, r1, r2, r3, c0, c1, near_tiles, far_tiles, row_best, col_best,
                  src_piece, tgt_piece, s16, t16, s_cols, row_slots, col_slots):
    s16[...] = jnp.log((r0[...] + r1[...]) + (r2[...] + r3[...])) * HALF_TEMP
    t16[...] = jnp.log(c0[...] + c1[...]) * HALF_TEMP
    row_slots[...] = jnp.zeros_like(row_slots)
    col_slots[...] = jnp.zeros_like(col_slots)
    for h in range(SHARDS):
        s_cols[h * HALF : (h + 1) * HALF, :] = jnp.broadcast_to(
            s16[h : h + 1, :], (HALF, HALF)
        ).T
    src_piece[...] = s16[pl.ds(meta[6], 1), :] * (2 * TEMP_INV)
    tgt_piece[...] = t16[pl.ds(meta[7], 1), :] * (2 * TEMP_INV)

    def best_of(begin, n, width, tiles):
        def group(k, carry):
            for u in range(width):
                q = jnp.minimum(k * width + u, n - 1)
                i, j, p = (todo[3 * (begin + q) + v] for v in range(3))
                ta, tb = t16[pl.ds(2 * j, 1), :], t16[pl.ds(2 * j + 1, 1), :]
                sa, sb = s16[pl.ds(2 * i, 1), :], s16[pl.ds(2 * i + 1, 1), :]
                sc = s_cols[pl.ds(pl.multiple_of(i * BLK, BLK), BLK), :]
                scores = tiles[q]
                ua, ub = scores[:, :HALF], scores[:, HALF:]
                best = jnp.maximum(ua - ta, ub - tb)
                ra = jnp.max(best[:HALF].T, axis=0, keepdims=True)
                rb = jnp.max(best[HALF:].T, axis=0, keepdims=True)
                ca = jnp.max(ua - sc, axis=0, keepdims=True)
                cb = jnp.max(ub - sc, axis=0, keepdims=True)
                row_slots[p] = jnp.concatenate([ra - sa, rb - sb], 1) * TEMP_INV
                col_slots[p] = jnp.concatenate([ca - ta, cb - tb], 1) * TEMP_INV
            return carry

        lax.fori_loop(0, (n + width - 1) // width, group, 0)

    near = meta[8]
    best_of(0, near, GROUP_TILES, near_tiles)
    best_of(near, meta[0] - near, 4, far_tiles)
    for k in range(0, SLOTS, 8):
        row_best[k : k + 8, :] = jnp.concatenate([row_slots[k + v] for v in range(8)], 0)
        col_best[k : k + 8, :] = jnp.concatenate([col_slots[k + v] for v in range(8)], 0)


VMEM = pl.BlockSpec(memory_space=pltpu.VMEM)
SMEM = pl.BlockSpec(memory_space=pltpu.SMEM)


F32 = lambda *shape: jax.ShapeDtypeStruct(shape, jnp.float32)
PARAMS = pltpu.CompilerParams(vmem_limit_bytes=20 * 1024 * 1024)


def pinned(v):
    return pltpu.with_memory_space_constraint(v, pltpu.VMEM)


def list_tiles(pairs, count, far_x, todo):
    def append(far):
        def step(p, n):
            i = pairs[0, p]
            todo[3 * n] = i
            todo[3 * n + 1] = pairs[1, p]
            todo[3 * n + 2] = p
            return n + ((lax.div(i, 2) == far_x) == far).astype(jnp.int32)

        return step

    near = lax.fori_loop(0, count, append(False), jnp.int32(0))
    lax.fori_loop(0, count, append(True), near)
    return near


def list_kernel(pairs, counts, meta, todo):
    zh, y, c, x, zl = (lax.axis_index(a) for a in AXES)
    near = list_tiles(pairs, counts[0, 0], lax.rem(x + 2, 4), todo)
    for k, v in enumerate([counts[0, 0], zh, y, c, x, zl, x * 4 + zl, zh * 8 + y * 2 + c, near]):
        meta[k] = v


def listing(pairs, counts):
    return pl.pallas_call(
        list_kernel,
        out_shape=[jax.ShapeDtypeStruct((n,), jnp.int32) for n in (9, 3 * (SLOTS + 1))],
        in_specs=[SMEM, SMEM],
        out_specs=[SMEM, SMEM],
        compiler_params=PARAMS,
        cost_estimate=pl.CostEstimate(flops=10**10, bytes_accessed=0, transcendentals=0),
        name="listing",
    )(jnp.swapaxes(pairs[0, 0], 0, 1), counts)


def unit_kernel(source, target, own_s, own_t, s_rows, t_rows, sems):
    copies = [
        pltpu.make_async_copy(source, s_rows, sems.at[0]),
        pltpu.make_async_copy(target, t_rows, sems.at[1]),
    ]
    for copy in copies:
        copy.start()
    copies[0].wait()
    own_s[...] = unit_rows(s_rows[...])
    copies[1].wait()
    own_t[...] = unit_rows(t_rows[...])


def unit(source, target):
    return pl.pallas_call(
        unit_kernel,
        out_shape=[jax.ShapeDtypeStruct(v.shape, v.dtype) for v in (source, target)],
        in_specs=[pl.BlockSpec(memory_space=pltpu.HBM)] * 2,
        out_specs=[VMEM] * 2,
        scratch_shapes=[pltpu.VMEM(v.shape, v.dtype) for v in (source, target)]
        + [pltpu.SemaphoreType.DMA((2,))],
        compiler_params=PARAMS,
        name="unit",
    )(*(pltpu.with_memory_space_constraint(v, pltpu.HBM) for v in (source, target)))


def sums(meta, todo, near_parts, far_parts, tgt_parts):
    width = tgt_parts[0].shape[1]
    near_store = pltpu.VMEM((SLOTS, BLK, BLK), jnp.float32)
    far_store = pltpu.VMEM((2 * BLOCKS, BLK, BLK), jnp.float32)
    col_store = pltpu.VMEM((BLOCKS + 1, 8, BLK), jnp.float32)
    slab = pltpu.VMEM((BLOCKS * BLK, width), jnp.bfloat16)
    near_rows, near_cols, near_tiles, tgt = pl.pallas_call(
        near_kernel,
        out_shape=(pltpu.VMEM((SHARDS, HALF), jnp.float32), col_store, near_store, slab),
        in_specs=[SMEM, SMEM] + [VMEM] * (NEAR_PARTS + TGT_PARTS),
        out_specs=(VMEM,) * 4,
        scratch_shapes=[slab, pltpu.VMEM(((BLOCKS + 1) * BLK, HALF), jnp.float32)],
        compiler_params=PARAMS,
        cost_estimate=pl.CostEstimate(
            flops=40 * 2 * BLK * BLK * width, bytes_accessed=12 << 20, transcendentals=40 * BLK * BLK
        ),
        name="near_sums",
    )(meta, todo, *near_parts, *tgt_parts)
    row_sums, col_sums, far_tiles = pl.pallas_call(
        far_kernel,
        out_shape=(F32(SHARDS, HALF), F32(SHARDS, HALF), far_store),
        in_specs=[SMEM, SMEM] + [VMEM] * (FAR_PARTS + 3),
        out_specs=(VMEM,) * 3,
        scratch_shapes=[
            pltpu.VMEM((2 * BLK, width), jnp.bfloat16),
            pltpu.VMEM((3 * BLK, HALF), jnp.float32),
            col_store,
        ],
        compiler_params=PARAMS,
        name="far_sums",
    )(meta, todo, *far_parts, pinned(near_rows), pinned(near_cols), pinned(tgt))
    return row_sums, col_sums, near_tiles, far_tiles


def margins(meta, todo, row_all, col_all, near_tiles, far_tiles):
    return pl.pallas_call(
        margin_kernel,
        out_shape=(F32(SLOTS, BLK), F32(SLOTS, BLK), F32(1, HALF), F32(1, HALF)),
        in_specs=[SMEM, SMEM] + [VMEM] * 8,
        out_specs=(VMEM,) * 4,
        scratch_shapes=[
            pltpu.VMEM((SHARDS, HALF), jnp.float32),
            pltpu.VMEM((SHARDS, HALF), jnp.float32),
            pltpu.VMEM((BLOCKS * BLK, HALF), jnp.float32),
            pltpu.VMEM((SLOTS, 1, BLK), jnp.float32),
            pltpu.VMEM((SLOTS, 1, BLK), jnp.float32),
        ],
        compiler_params=PARAMS,
        name="margins",
    )(meta, todo, *row_all, *col_all, pinned(near_tiles), pinned(far_tiles))


def gather(own_s, own_t, todo):
    send = lambda v, axis, step: lax.ppermute(v, axis, ring(lax.axis_size(axis), step))
    after = lambda v, done: lax.optimization_barrier((v, done))
    near = [send(own_s, "zl", k) for k in REST]
    s_own = [send(own_s, "x", k) for k in (1, -1)]
    (t_y, again), (s_own, todo) = after((own_t, own_s), (s_own, todo))
    t_near = [send(t_y, "y", k) for k in (1, -1)]
    (t_zh, again), (t_near, near[0], near[1]) = after((t_y, again), (t_near, near[0], near[1]))
    across = send(t_zh, "zh", 1)
    t_own = [own_t] + t_near + [send(t_zh, "y", 2)]
    s_own.append(send(again, "x", 2))

    near, (across, s_own) = after(near, (across, s_own))
    rest = jnp.concatenate(near)
    up, down = send(rest, "x", 1), send(rest, "x", -1)
    t_own = jnp.concatenate(t_own)
    t_own_c = send(t_own, "c", 1)
    across, t_own_c = after(across, t_own_c)
    t_across = [across] + [send(across, "y", k) for k in (2, 1, -1)]

    up_far, down_far = send(up[:192], "x", 1), send(down[192:], "x", -1)
    t_across_c = [send(v, "c", 1) for v in t_across]
    t_parts = [t_own, t_own_c] + t_across + t_across_c
    return [own_s, s_own[0], s_own[1], rest, up, down], [s_own[2], up_far, down_far], t_parts, todo


def total(row_sums, col_sums):
    send = lambda v, axis, step: lax.ppermute(v, axis, ring(lax.axis_size(axis), step))
    cols = col_sums + send(col_sums, "c", 1)
    rows = [row_sums] + [send(row_sums, "x", k) for k in (1, -1, 2)]
    cols = [cols] + [send(cols, "y", k) for k in (1, -1, 2)]
    rows, cols = lax.optimization_barrier((rows, cols))
    rows, cols = (rows[0] + rows[1]) + (rows[2] + rows[3]), (cols[0] + cols[1]) + (cols[2] + cols[3])
    return [rows] + [send(rows, "zl", k) for k in (1, -1, 2)], [cols, send(cols, "zh", 1)]


def per_device(source, target, pairs, counts):
    own_s, own_t = unit(source, target)
    own_s, (pairs, counts) = lax.optimization_barrier((own_s, (pairs, counts)))
    *pieces, (meta, todo) = gather(own_s, own_t, listing(pairs, counts))
    row_sums, col_sums, near_tiles, far_tiles = sums(meta, todo, *pieces)
    row_all, col_all = total(row_sums, col_sums)
    row_best, col_best, src_piece, tgt_piece = margins(
        meta, todo, row_all, col_all, near_tiles, far_tiles
    )
    return (
        row_best.reshape(1, 1, SLOTS, BLK),
        col_best.reshape(1, 1, SLOTS, BLK),
        src_piece.reshape(HALF),
        tgt_piece.reshape(HALF),
    )


def solution(mesh):
    fine = Mesh(mesh.devices.reshape(2, 4, 2, 4, 4), AXES)
    src_axes, tgt_axes = AXES, GROUP + BANK
    return jax.shard_map(
        per_device,
        mesh=fine,
        in_specs=(
            P(src_axes, None),
            P(tgt_axes, None),
            P(BANK, GROUP, None, None),
            P(BANK, GROUP),
        ),
        out_specs=(
            P(BANK, GROUP, None, None),
            P(BANK, GROUP, None, None),
            P(src_axes),
            P(tgt_axes),
        ),
        check_vma=False,
    )
```

```python
import math

import jax
import jax.numpy as jnp
from jax import lax
from jax.experimental import pallas as pl
from jax.experimental.pallas import tpu as pltpu
from jax.sharding import Mesh
from jax.sharding import PartitionSpec as P

BLK = 256
HALF = 128
SLOTS = 48
BLOCKS = 8
SHARDS = 16
TEMP_INV = 20.0
EXP2_SCALE = TEMP_INV * math.log2(math.e)
HALF_TEMP = 0.5 / TEMP_INV
NT = (((1,), (1,)), ((), ()))
AXES = ("zh", "y", "c", "x", "zl")
BANK = ("zh", "y", "c")
GROUP = ("x", "zl")


def unit_rows(rows):
    values = rows.astype(jnp.float32)
    width = values.shape[-1]
    scale = lax.rsqrt(jnp.mean(values * values, axis=-1, keepdims=True) + 1e-06)
    return (values * (scale * (1.0 / math.sqrt(width)))).astype(jnp.bfloat16)


def ring(n, step):
    return [(i, (i + step) % n) for i in range(n)]


GROUP_TILES = 8

REST = (1, 3, 2)
NEAR_PLACE = {(0, 0, 0): (0, 0, 128), (1, 0, 0): (1, 0, 128), (3, 0, 0): (2, 0, 128)}
for order, dz in enumerate(REST):
    for part, dx in ((3, 0), (4, 1), (5, 3)):
        NEAR_PLACE[(dx, dz, 0)] = (part, 128 * order, 128)
NEAR_PARTS = 6
FAR_PLACE = {
    (2, 0, 0): (0, 0, 128),
    (2, 1, 0): (1, 0, 128),
    (2, 3, 0): (1, 128, 64),
    (2, 3, 64): (2, 0, 64),
    (2, 2, 0): (2, 64, 128),
}
FAR_PARTS = 3
TGT_PLACE = {}
for order, dy in enumerate((0, 1, 3, 2)):
    TGT_PLACE[(0, dy, 0)] = (0, 128 * order)
    TGT_PLACE[(0, dy, 1)] = (1, 128 * order)
for order, dy in enumerate((0, 2, 1, 3)):
    TGT_PLACE[(1, dy, 0)] = (2 + order, 0)
    TGT_PLACE[(1, dy, 1)] = (6 + order, 0)
TGT_PARTS = 10


def load_source(meta, place, parts, src, of_x):
    for (dx, dz, offset), (part, first, rows) in place.items():
        shard = of_x(dx) * 4 + lax.rem(meta[5] - dz + 4, 4)
        dst = pl.ds(pl.multiple_of(shard * HALF + offset, 64), rows)
        src[dst, :] = parts[part][first : first + rows, :]


def load_target(meta, parts, tgt):
    zh, y, c = meta[1], meta[2], meta[3]
    for (dh, dy, dc), (part, first) in TGT_PLACE.items():
        shard = lax.rem(zh + dh, 2) * 8 + lax.rem(y - dy + 4, 4) * 2 + lax.rem(c + dc, 2)
        dst = pl.ds(pl.multiple_of(shard * HALF, HALF), HALF)
        tgt[dst, :] = parts[part][first : first + HALF, :]


def add_tiles(todo, begin, n, width, src, row_of, tgt, tiles, acc_row, acc_col):
    dead_row = acc_row.shape[0] // BLK - 1

    def group(k, carry):
        for u in range(width):
            live = k * width + u < n
            q = jnp.minimum(k * width + u, n - 1)
            i, j = row_of(todo[3 * (begin + q)]), todo[3 * (begin + q) + 1]
            left = src[pl.ds(pl.multiple_of(i * BLK, BLK), BLK), :]
            right = tgt[pl.ds(pl.multiple_of(j * BLK, BLK), BLK), :]
            scores = lax.dot_general(left, right, NT, preferred_element_type=jnp.float32)
            tiles[q] = scores
            i = jnp.where(live, i, dead_row)
            j = jnp.where(live, j, BLOCKS)
            w = jnp.exp2(scores * EXP2_SCALE)
            rows = pl.ds(pl.multiple_of(i * BLK, BLK), BLK)
            acc_row[rows, :] += w[:, :HALF] + w[:, HALF:]
            acc_col[j] += w.reshape(BLK // 8, 8, BLK).sum(0)
        return carry

    lax.fori_loop(0, (n + width - 1) // width, group, 0)


def row_totals(acc_row, count):
    return jnp.concatenate(
        [
            jnp.sum(acc_row[h * HALF : (h + 1) * HALF, :].T, axis=0, keepdims=True)
            for h in range(count)
        ],
        0,
    )


def near_kernel(meta, todo, *refs):
    parts, refs = refs[: NEAR_PARTS + TGT_PARTS], refs[NEAR_PARTS + TGT_PARTS :]
    row_out, acc_col, tiles, tgt, src, acc_row = refs
    load_source(meta, NEAR_PLACE, parts[:NEAR_PARTS], src, lambda dx: lax.rem(meta[4] - dx + 4, 4))
    load_target(meta, parts[NEAR_PARTS:], tgt)
    acc_row[...] = jnp.zeros_like(acc_row)
    acc_col[...] = jnp.zeros_like(acc_col)
    add_tiles(todo, 0, meta[8], GROUP_TILES, src, lambda i: i, tgt, tiles, acc_row, acc_col)
    row_out[...] = row_totals(acc_row, SHARDS)


def far_kernel(meta, todo, *refs):
    parts, refs = refs[:FAR_PARTS], refs[FAR_PARTS:]
    row_in, col_in, tgt, row_out, col_out, tiles, src, acc_row, acc_col = refs
    load_source(meta, FAR_PLACE, parts, src, lambda dx: 0)
    acc_row[...] = jnp.zeros_like(acc_row)
    acc_col[...] = col_in[...]
    near = meta[8]
    add_tiles(todo, near, meta[0] - near, 4, src, lambda i: lax.rem(i, 2), tgt, tiles, acc_row, acc_col)
    far_rows = row_totals(acc_row, 4)
    rows = row_in[...]
    far_x = lax.rem(meta[4] + 2, 4)
    rows = jnp.concatenate(
        [rows[4 * v : 4 * v + 4] + jnp.where(far_x == v, far_rows, 0.0) for v in range(4)], 0
    )
    row_out[...] = rows
    cols = []
    for j in range(BLOCKS):
        col = jnp.sum(acc_col[j], axis=0, keepdims=True)
        cols += [col[:, :HALF], col[:, HALF:]]
    col_out[...] = jnp.concatenate(cols, 0)


def margin_kernel(meta, todo, r0, r1, r2, r3, c0, c1, c2, c3, near_tiles, far_tiles, row_best, col_best,
                  src_piece, tgt_piece, s16, t16, s_cols, row_slots, col_slots):
    s16[...] = jnp.log((r0[...] + r1[...]) + (r2[...] + r3[...])) * HALF_TEMP
    t16[...] = jnp.log((c0[...] + c1[...]) + (c2[...] + c3[...])) * HALF_TEMP
    row_slots[...] = jnp.zeros_like(row_slots)
    col_slots[...] = jnp.zeros_like(col_slots)
    for h in range(SHARDS):
        s_cols[h * HALF : (h + 1) * HALF, :] = jnp.broadcast_to(
            s16[h : h + 1, :], (HALF, HALF)
        ).T
    src_piece[...] = s16[pl.ds(meta[6], 1), :] * (2 * TEMP_INV)
    tgt_piece[...] = t16[pl.ds(meta[7], 1), :] * (2 * TEMP_INV)

    def best_of(begin, n, width, tiles):
        def group(k, carry):
            for u in range(width):
                q = jnp.minimum(k * width + u, n - 1)
                i, j, p = (todo[3 * (begin + q) + v] for v in range(3))
                ta, tb = t16[pl.ds(2 * j, 1), :], t16[pl.ds(2 * j + 1, 1), :]
                sa, sb = s16[pl.ds(2 * i, 1), :], s16[pl.ds(2 * i + 1, 1), :]
                sc = s_cols[pl.ds(pl.multiple_of(i * BLK, BLK), BLK), :]
                scores = tiles[q]
                ua, ub = scores[:, :HALF], scores[:, HALF:]
                best = jnp.maximum(ua - ta, ub - tb)
                ra = jnp.max(best[:HALF].T, axis=0, keepdims=True)
                rb = jnp.max(best[HALF:].T, axis=0, keepdims=True)
                ca = jnp.max(ua - sc, axis=0, keepdims=True)
                cb = jnp.max(ub - sc, axis=0, keepdims=True)
                row_slots[p] = jnp.concatenate([ra - sa, rb - sb], 1) * TEMP_INV
                col_slots[p] = jnp.concatenate([ca - ta, cb - tb], 1) * TEMP_INV
            return carry

        lax.fori_loop(0, (n + width - 1) // width, group, 0)

    near = meta[8]
    best_of(0, near, GROUP_TILES, near_tiles)
    best_of(near, meta[0] - near, 4, far_tiles)
    for k in range(0, SLOTS, 8):
        row_best[k : k + 8, :] = jnp.concatenate([row_slots[k + v] for v in range(8)], 0)
        col_best[k : k + 8, :] = jnp.concatenate([col_slots[k + v] for v in range(8)], 0)


VMEM = pl.BlockSpec(memory_space=pltpu.VMEM)
SMEM = pl.BlockSpec(memory_space=pltpu.SMEM)


F32 = lambda *shape: jax.ShapeDtypeStruct(shape, jnp.float32)
PARAMS = pltpu.CompilerParams(vmem_limit_bytes=20 * 1024 * 1024)


def pinned(v):
    return pltpu.with_memory_space_constraint(v, pltpu.VMEM)


def unit_kernel(source, target, own_s, own_t, s_rows, t_rows, sems):
    copies = [
        pltpu.make_async_copy(source, s_rows, sems.at[0]),
        pltpu.make_async_copy(target, t_rows, sems.at[1]),
    ]
    for copy in copies:
        copy.start()
    copies[0].wait()
    own_s[...] = unit_rows(s_rows[...])
    copies[1].wait()
    own_t[...] = unit_rows(t_rows[...])


def unit(source, target):
    return pl.pallas_call(
        unit_kernel,
        out_shape=[jax.ShapeDtypeStruct(v.shape, v.dtype) for v in (source, target)],
        in_specs=[pl.BlockSpec(memory_space=pltpu.HBM)] * 2,
        out_specs=[VMEM] * 2,
        scratch_shapes=[pltpu.VMEM(v.shape, v.dtype) for v in (source, target)]
        + [pltpu.SemaphoreType.DMA((2,))],
        compiler_params=PARAMS,
        name="unit",
    )(*(pltpu.with_memory_space_constraint(v, pltpu.HBM) for v in (source, target)))


def sums(meta, todo, near_parts, far_parts, tgt_parts):
    width = tgt_parts[0].shape[1]
    near_store = pltpu.VMEM((SLOTS, BLK, BLK), jnp.float32)
    far_store = pltpu.VMEM((2 * BLOCKS, BLK, BLK), jnp.float32)
    col_store = pltpu.VMEM((BLOCKS + 1, 8, BLK), jnp.float32)
    slab = pltpu.VMEM((BLOCKS * BLK, width), jnp.bfloat16)
    near_rows, near_cols, near_tiles, tgt = pl.pallas_call(
        near_kernel,
        out_shape=(pltpu.VMEM((SHARDS, HALF), jnp.float32), col_store, near_store, slab),
        in_specs=[SMEM, SMEM] + [VMEM] * (NEAR_PARTS + TGT_PARTS),
        out_specs=(VMEM,) * 4,
        scratch_shapes=[slab, pltpu.VMEM(((BLOCKS + 1) * BLK, HALF), jnp.float32)],
        compiler_params=PARAMS,
        cost_estimate=pl.CostEstimate(
            flops=40 * 2 * BLK * BLK * width, bytes_accessed=12 << 20, transcendentals=40 * BLK * BLK
        ),
        name="near_sums",
    )(meta, todo, *near_parts, *tgt_parts)
    row_sums, col_sums, far_tiles = pl.pallas_call(
        far_kernel,
        out_shape=(F32(SHARDS, HALF), F32(SHARDS, HALF), far_store),
        in_specs=[SMEM, SMEM] + [VMEM] * (FAR_PARTS + 3),
        out_specs=(VMEM,) * 3,
        scratch_shapes=[
            pltpu.VMEM((2 * BLK, width), jnp.bfloat16),
            pltpu.VMEM((3 * BLK, HALF), jnp.float32),
            col_store,
        ],
        compiler_params=PARAMS,
        name="far_sums",
    )(meta, todo, *far_parts, pinned(near_rows), pinned(near_cols), pinned(tgt))
    return row_sums, col_sums, near_tiles, far_tiles


def margins(meta, todo, row_all, col_all, near_tiles, far_tiles):
    return pl.pallas_call(
        margin_kernel,
        out_shape=(F32(SLOTS, BLK), F32(SLOTS, BLK), F32(1, HALF), F32(1, HALF)),
        in_specs=[SMEM, SMEM] + [VMEM] * 10,
        out_specs=(VMEM,) * 4,
        scratch_shapes=[
            pltpu.VMEM((SHARDS, HALF), jnp.float32),
            pltpu.VMEM((SHARDS, HALF), jnp.float32),
            pltpu.VMEM((BLOCKS * BLK, HALF), jnp.float32),
            pltpu.VMEM((SLOTS, 1, BLK), jnp.float32),
            pltpu.VMEM((SLOTS, 1, BLK), jnp.float32),
        ],
        compiler_params=PARAMS,
        name="margins",
    )(meta, todo, *row_all, *col_all, pinned(near_tiles), pinned(far_tiles))


def gather(own_s, own_t, todo):
    send = lambda v, axis, step: lax.ppermute(v, axis, ring(lax.axis_size(axis), step))
    after = lambda v, done: lax.optimization_barrier((v, done))
    near = [send(own_s, "zl", k) for k in REST]
    s_own = [send(own_s, "x", k) for k in (1, -1)]
    (t_y, again), s_own = after((own_t, own_s), s_own)
    t_near = [send(t_y, "y", k) for k in (1, -1)]
    (t_zh, again), t_near = after((t_y, again), t_near)
    across = send(t_zh, "zh", 1)
    t_own = [own_t] + t_near + [send(t_zh, "y", 2)]
    s_own.append(send(again, "x", 2))

    near, (todo, across, s_own) = after(near, (todo, across, s_own))
    rest = jnp.concatenate(near)
    up, down = send(rest, "x", 1), send(rest, "x", -1)
    t_own = jnp.concatenate(t_own)
    t_own_c = send(t_own, "c", 1)
    across, t_own_c = after(across, t_own_c)
    t_across = [across] + [send(across, "y", k) for k in (2, 1, -1)]

    up_far, down_far = send(up[:192], "x", 1), send(down[192:], "x", -1)
    t_across_c = [send(v, "c", 1) for v in t_across]
    t_parts = [t_own, t_own_c] + t_across + t_across_c
    return [own_s, s_own[0], s_own[1], rest, up, down], [s_own[2], up_far, down_far], t_parts, todo


def total(row_sums, col_sums):
    send = lambda v, axis, step: lax.ppermute(v, axis, ring(lax.axis_size(axis), step))
    cols = col_sums + send(col_sums, "c", 1)
    cols = cols + send(cols, "zh", 1)
    rows = [row_sums] + [send(row_sums, "x", k) for k in (2, 1, -1)]
    rows = (rows[0] + rows[1]) + (rows[2] + rows[3])
    return [rows] + [send(rows, "zl", k) for k in (2, 1, -1)], [cols] + [send(cols, "y", k) for k in (2, 1, -1)]


def listing(pairs, count, far_x):
    slot = jnp.arange(pairs.shape[0], dtype=jnp.int32)
    live = slot < count
    near = live & (pairs[:, 0] // 2 != far_x)
    kind = jnp.where(near, 0, jnp.where(live, 1, 2))
    key = kind * SLOTS + slot
    place = jnp.sum(key[None, :] < key[:, None], axis=1, dtype=jnp.int32)
    entry = jnp.concatenate([pairs, slot[:, None]], 1)
    todo = jnp.sum(jnp.where(place[None, :, None] == slot[:, None, None], entry[None], 0), axis=1)
    return todo.reshape(-1).astype(jnp.int32), jnp.sum(near, dtype=jnp.int32)


def per_device(source, target, pairs, counts):
    zh, y, c, x, zl = (lax.axis_index(a) for a in AXES)
    count = counts[0, 0]
    todo, near = listing(pairs[0, 0], count, (x + 2) % 4)
    meta = jnp.stack([count, zh, y, c, x, zl, x * 4 + zl, zh * 8 + y * 2 + c, near]).astype(jnp.int32)
    *pieces, (meta, todo) = gather(*unit(source, target), (meta, todo))
    row_sums, col_sums, near_tiles, far_tiles = sums(meta, todo, *pieces)
    row_all, col_all = total(row_sums, col_sums)
    row_best, col_best, src_piece, tgt_piece = margins(
        meta, todo, row_all, col_all, near_tiles, far_tiles
    )
    return (
        row_best.reshape(1, 1, SLOTS, BLK),
        col_best.reshape(1, 1, SLOTS, BLK),
        src_piece.reshape(HALF),
        tgt_piece.reshape(HALF),
    )


def solution(mesh):
    fine = Mesh(mesh.devices.reshape(2, 4, 2, 4, 4), AXES)
    src_axes, tgt_axes = AXES, GROUP + BANK
    return jax.shard_map(
        per_device,
        mesh=fine,
        in_specs=(
            P(src_axes, None),
            P(tgt_axes, None),
            P(BANK, GROUP, None, None),
            P(BANK, GROUP),
        ),
        out_specs=(
            P(BANK, GROUP, None, None),
            P(BANK, GROUP, None, None),
            P(src_axes),
            P(tgt_axes),
        ),
        check_vma=False,
    )
```

```python
import math

import jax
import jax.numpy as jnp
from jax import lax
from jax.experimental import pallas as pl
from jax.experimental.pallas import tpu as pltpu
from jax.sharding import Mesh
from jax.sharding import PartitionSpec as P

BLK = 256
HALF = 128
SLOTS = 48
BLOCKS = 8
SHARDS = 16
TEMP_INV = 20.0
EXP2_SCALE = TEMP_INV * math.log2(math.e)
HALF_TEMP = 0.5 / TEMP_INV
NT = (((1,), (1,)), ((), ()))
AXES = ("zh", "y", "c", "x", "zl")
BANK = ("zh", "y", "c")
GROUP = ("x", "zl")


def unit_rows(rows):
    values = rows.astype(jnp.float32)
    width = values.shape[-1]
    scale = lax.rsqrt(jnp.mean(values * values, axis=-1, keepdims=True) + 1e-06)
    return (values * (scale * (1.0 / math.sqrt(width)))).astype(jnp.bfloat16)


def ring(n, step):
    return [(i, (i + step) % n) for i in range(n)]


GROUP_TILES = 8

REST = (1, 3, 2)
NEAR_PLACE = {(0, 0, 0): (0, 0, 128), (1, 0, 0): (1, 0, 128), (3, 0, 0): (2, 0, 128)}
for order, dz in enumerate(REST):
    for part, dx in ((3, 0), (4, 1), (5, 3)):
        NEAR_PLACE[(dx, dz, 0)] = (part, 128 * order, 128)
NEAR_PARTS = 6
FAR_PLACE = {
    (2, 0, 0): (0, 0, 128),
    (2, 1, 0): (1, 0, 128),
    (2, 3, 0): (1, 128, 64),
    (2, 3, 64): (2, 0, 64),
    (2, 2, 0): (2, 64, 128),
}
FAR_PARTS = 3
TGT_PLACE = {}
for order, dy in enumerate((0, 1, 3, 2)):
    TGT_PLACE[(0, dy, 0)] = (0, 128 * order)
    TGT_PLACE[(0, dy, 1)] = (1, 128 * order)
for order, dy in enumerate((0, 2, 1, 3)):
    TGT_PLACE[(1, dy, 0)] = (2 + order, 0)
    TGT_PLACE[(1, dy, 1)] = (6 + order, 0)
TGT_PARTS = 10


def load_source(meta, place, parts, src, of_x):
    for (dx, dz, offset), (part, first, rows) in place.items():
        shard = of_x(dx) * 4 + lax.rem(meta[5] - dz + 4, 4)
        dst = pl.ds(pl.multiple_of(shard * HALF + offset, 64), rows)
        src[dst, :] = parts[part][first : first + rows, :]


def load_target(meta, parts, tgt):
    zh, y, c = meta[1], meta[2], meta[3]
    for (dh, dy, dc), (part, first) in TGT_PLACE.items():
        shard = lax.rem(zh + dh, 2) * 8 + lax.rem(y - dy + 4, 4) * 2 + lax.rem(c + dc, 2)
        dst = pl.ds(pl.multiple_of(shard * HALF, HALF), HALF)
        tgt[dst, :] = parts[part][first : first + HALF, :]


def add_tiles(todo, begin, n, width, src, row_of, tgt, tiles, acc_row, acc_col):
    dead_row = acc_row.shape[0] // BLK - 1

    def group(k, carry):
        for u in range(width):
            live = k * width + u < n
            q = jnp.minimum(k * width + u, n - 1)
            i, j = row_of(todo[3 * (begin + q)]), todo[3 * (begin + q) + 1]
            left = src[pl.ds(pl.multiple_of(i * BLK, BLK), BLK), :]
            right = tgt[pl.ds(pl.multiple_of(j * BLK, BLK), BLK), :]
            scores = lax.dot_general(left, right, NT, preferred_element_type=jnp.float32)
            tiles[q] = scores
            i = jnp.where(live, i, dead_row)
            j = jnp.where(live, j, BLOCKS)
            w = jnp.exp2(scores * EXP2_SCALE)
            rows = pl.ds(pl.multiple_of(i * BLK, BLK), BLK)
            acc_row[rows, :] += w[:, :HALF] + w[:, HALF:]
            acc_col[j] += w.reshape(BLK // 8, 8, BLK).sum(0)
        return carry

    lax.fori_loop(0, (n + width - 1) // width, group, 0)


def row_totals(acc_row, count):
    return jnp.concatenate(
        [
            jnp.sum(acc_row[h * HALF : (h + 1) * HALF, :].T, axis=0, keepdims=True)
            for h in range(count)
        ],
        0,
    )


def near_kernel(meta, todo, *refs):
    parts, refs = refs[: NEAR_PARTS + TGT_PARTS], refs[NEAR_PARTS + TGT_PARTS :]
    row_out, acc_col, tiles, tgt, src, acc_row = refs
    load_source(meta, NEAR_PLACE, parts[:NEAR_PARTS], src, lambda dx: lax.rem(meta[4] - dx + 4, 4))
    load_target(meta, parts[NEAR_PARTS:], tgt)
    acc_row[...] = jnp.zeros_like(acc_row)
    acc_col[...] = jnp.zeros_like(acc_col)
    add_tiles(todo, 0, meta[8], GROUP_TILES, src, lambda i: i, tgt, tiles, acc_row, acc_col)
    row_out[...] = row_totals(acc_row, SHARDS)


def far_kernel(meta, todo, *refs):
    parts, refs = refs[:FAR_PARTS], refs[FAR_PARTS:]
    row_in, col_in, tgt, row_out, col_out, tiles, src, acc_row, acc_col = refs
    load_source(meta, FAR_PLACE, parts, src, lambda dx: 0)
    acc_row[...] = jnp.zeros_like(acc_row)
    acc_col[...] = col_in[...]
    near = meta[8]
    add_tiles(todo, near, meta[0] - near, 4, src, lambda i: lax.rem(i, 2), tgt, tiles, acc_row, acc_col)
    far_rows = row_totals(acc_row, 4)
    rows = row_in[...]
    far_x = lax.rem(meta[4] + 2, 4)
    rows = jnp.concatenate(
        [rows[4 * v : 4 * v + 4] + jnp.where(far_x == v, far_rows, 0.0) for v in range(4)], 0
    )
    row_out[...] = rows
    cols = []
    for j in range(BLOCKS):
        col = jnp.sum(acc_col[j], axis=0, keepdims=True)
        cols += [col[:, :HALF], col[:, HALF:]]
    col_out[...] = jnp.concatenate(cols, 0)


def margin_kernel(meta, todo, r0, r1, r2, r3, c0, c1, c2, c3, near_tiles, far_tiles, row_best, col_best,
                  src_piece, tgt_piece, s16, t16, s_cols, row_slots, col_slots):
    s16[...] = jnp.log((r0[...] + r1[...]) + (r2[...] + r3[...])) * HALF_TEMP
    t16[...] = jnp.log((c0[...] + c1[...]) + (c2[...] + c3[...])) * HALF_TEMP
    row_slots[...] = jnp.zeros_like(row_slots)
    col_slots[...] = jnp.zeros_like(col_slots)
    for h in range(SHARDS):
        s_cols[h * HALF : (h + 1) * HALF, :] = jnp.broadcast_to(
            s16[h : h + 1, :], (HALF, HALF)
        ).T
    src_piece[...] = s16[pl.ds(meta[6], 1), :] * (2 * TEMP_INV)
    tgt_piece[...] = t16[pl.ds(meta[7], 1), :] * (2 * TEMP_INV)

    def best_of(begin, n, width, tiles):
        def group(k, carry):
            for u in range(width):
                q = jnp.minimum(k * width + u, n - 1)
                i, j, p = (todo[3 * (begin + q) + v] for v in range(3))
                ta, tb = t16[pl.ds(2 * j, 1), :], t16[pl.ds(2 * j + 1, 1), :]
                sa, sb = s16[pl.ds(2 * i, 1), :], s16[pl.ds(2 * i + 1, 1), :]
                sc = s_cols[pl.ds(pl.multiple_of(i * BLK, BLK), BLK), :]
                scores = tiles[q]
                ua, ub = scores[:, :HALF], scores[:, HALF:]
                best = jnp.maximum(ua - ta, ub - tb)
                ra = jnp.max(best[:HALF].T, axis=0, keepdims=True)
                rb = jnp.max(best[HALF:].T, axis=0, keepdims=True)
                ca = jnp.max(ua - sc, axis=0, keepdims=True)
                cb = jnp.max(ub - sc, axis=0, keepdims=True)
                row_slots[p] = jnp.concatenate([ra - sa, rb - sb], 1) * TEMP_INV
                col_slots[p] = jnp.concatenate([ca - ta, cb - tb], 1) * TEMP_INV
            return carry

        lax.fori_loop(0, (n + width - 1) // width, group, 0)

    near = meta[8]
    best_of(0, near, GROUP_TILES, near_tiles)
    best_of(near, meta[0] - near, 4, far_tiles)
    for k in range(0, SLOTS, 8):
        row_best[k : k + 8, :] = jnp.concatenate([row_slots[k + v] for v in range(8)], 0)
        col_best[k : k + 8, :] = jnp.concatenate([col_slots[k + v] for v in range(8)], 0)


VMEM = pl.BlockSpec(memory_space=pltpu.VMEM)
SMEM = pl.BlockSpec(memory_space=pltpu.SMEM)


F32 = lambda *shape: jax.ShapeDtypeStruct(shape, jnp.float32)
PARAMS = pltpu.CompilerParams(vmem_limit_bytes=20 * 1024 * 1024)


def pinned(v):
    return pltpu.with_memory_space_constraint(v, pltpu.VMEM)


def unit_kernel(source, target, own_s, own_t, s_rows, t_rows, sems):
    copies = [
        pltpu.make_async_copy(source, s_rows, sems.at[0]),
        pltpu.make_async_copy(target, t_rows, sems.at[1]),
    ]
    for copy in copies:
        copy.start()
    copies[0].wait()
    own_s[...] = unit_rows(s_rows[...])
    copies[1].wait()
    own_t[...] = unit_rows(t_rows[...])


def unit(source, target):
    return pl.pallas_call(
        unit_kernel,
        out_shape=[jax.ShapeDtypeStruct(v.shape, v.dtype) for v in (source, target)],
        in_specs=[pl.BlockSpec(memory_space=pltpu.HBM)] * 2,
        out_specs=[VMEM] * 2,
        scratch_shapes=[pltpu.VMEM(v.shape, v.dtype) for v in (source, target)]
        + [pltpu.SemaphoreType.DMA((2,))],
        compiler_params=PARAMS,
        name="unit",
    )(*(pltpu.with_memory_space_constraint(v, pltpu.HBM) for v in (source, target)))


def sums(meta, todo, near_parts, far_parts, tgt_parts):
    width = tgt_parts[0].shape[1]
    near_store = pltpu.VMEM((SLOTS, BLK, BLK), jnp.float32)
    far_store = pltpu.VMEM((2 * BLOCKS, BLK, BLK), jnp.float32)
    col_store = pltpu.VMEM((BLOCKS + 1, 8, BLK), jnp.float32)
    slab = pltpu.VMEM((BLOCKS * BLK, width), jnp.bfloat16)
    near_rows, near_cols, near_tiles, tgt = pl.pallas_call(
        near_kernel,
        out_shape=(pltpu.VMEM((SHARDS, HALF), jnp.float32), col_store, near_store, slab),
        in_specs=[SMEM, SMEM] + [VMEM] * (NEAR_PARTS + TGT_PARTS),
        out_specs=(VMEM,) * 4,
        scratch_shapes=[slab, pltpu.VMEM(((BLOCKS + 1) * BLK, HALF), jnp.float32)],
        compiler_params=PARAMS,
        cost_estimate=pl.CostEstimate(
            flops=40 * 2 * BLK * BLK * width, bytes_accessed=12 << 20, transcendentals=40 * BLK * BLK
        ),
        name="near_sums",
    )(meta, todo, *near_parts, *tgt_parts)
    row_sums, col_sums, far_tiles = pl.pallas_call(
        far_kernel,
        out_shape=(F32(SHARDS, HALF), F32(SHARDS, HALF), far_store),
        in_specs=[SMEM, SMEM] + [VMEM] * (FAR_PARTS + 3),
        out_specs=(VMEM,) * 3,
        scratch_shapes=[
            pltpu.VMEM((2 * BLK, width), jnp.bfloat16),
            pltpu.VMEM((3 * BLK, HALF), jnp.float32),
            col_store,
        ],
        compiler_params=PARAMS,
        name="far_sums",
    )(meta, todo, *far_parts, pinned(near_rows), pinned(near_cols), pinned(tgt))
    return row_sums, col_sums, near_tiles, far_tiles


def margins(meta, todo, row_all, col_all, near_tiles, far_tiles):
    return pl.pallas_call(
        margin_kernel,
        out_shape=(F32(SLOTS, BLK), F32(SLOTS, BLK), F32(1, HALF), F32(1, HALF)),
        in_specs=[SMEM, SMEM] + [VMEM] * 10,
        out_specs=(VMEM,) * 4,
        scratch_shapes=[
            pltpu.VMEM((SHARDS, HALF), jnp.float32),
            pltpu.VMEM((SHARDS, HALF), jnp.float32),
            pltpu.VMEM((BLOCKS * BLK, HALF), jnp.float32),
            pltpu.VMEM((SLOTS, 1, BLK), jnp.float32),
            pltpu.VMEM((SLOTS, 1, BLK), jnp.float32),
        ],
        compiler_params=PARAMS,
        name="margins",
    )(meta, todo, *row_all, *col_all, pinned(near_tiles), pinned(far_tiles))


def gather(own_s, own_t, todo):
    send = lambda v, axis, step: lax.ppermute(v, axis, ring(lax.axis_size(axis), step))
    after = lambda v, done: lax.optimization_barrier((v, done))
    near = [send(own_s, "zl", k) for k in REST]
    s_own = [send(own_s, "x", k) for k in (1, -1)]
    (t_y, again), s_own = after((own_t, own_s), s_own)
    t_near = [send(t_y, "y", k) for k in (1, -1)]
    (t_zh, again), (t_near, todo) = after((t_y, again), (t_near, todo))
    across = send(t_zh, "zh", 1)
    t_own = [own_t] + t_near + [send(t_zh, "y", 2)]
    s_own.append(send(again, "x", 2))

    near, (todo, across, s_own) = after(near, (todo, across, s_own))
    rest = jnp.concatenate(near)
    up, down = send(rest, "x", 1), send(rest, "x", -1)
    t_own = jnp.concatenate(t_own)
    t_own_c = send(t_own, "c", 1)
    across, t_own_c = after(across, t_own_c)
    t_across = [across] + [send(across, "y", k) for k in (2, 1, -1)]

    up_far, down_far = send(up[:192], "x", 1), send(down[192:], "x", -1)
    t_across_c = [send(v, "c", 1) for v in t_across]
    t_parts = [t_own, t_own_c] + t_across + t_across_c
    return [own_s, s_own[0], s_own[1], rest, up, down], [s_own[2], up_far, down_far], t_parts, todo


def total(row_sums, col_sums):
    send = lambda v, axis, step: lax.ppermute(v, axis, ring(lax.axis_size(axis), step))
    cols = col_sums + send(col_sums, "c", 1)
    cols = cols + send(cols, "zh", 1)
    rows = [row_sums] + [send(row_sums, "x", k) for k in (2, 1, -1)]
    rows = (rows[0] + rows[1]) + (rows[2] + rows[3])
    return [rows] + [send(rows, "zl", k) for k in (2, 1, -1)], [cols] + [send(cols, "y", k) for k in (2, 1, -1)]


def listing(pairs, count, far_x):
    slot = jnp.arange(pairs.shape[0], dtype=jnp.int32)
    live = slot < count
    near = live & (pairs[:, 0] // 2 != far_x)
    kind = jnp.where(near, 0, jnp.where(live, 1, 2))
    key = kind * SLOTS + slot
    place = jnp.sum(key[None, :] < key[:, None], axis=1, dtype=jnp.int32)
    entry = jnp.concatenate([pairs, slot[:, None]], 1)
    todo = jnp.sum(jnp.where(place[None, :, None] == slot[:, None, None], entry[None], 0), axis=1)
    return todo.reshape(-1).astype(jnp.int32), jnp.sum(near, dtype=jnp.int32)


def per_device(source, target, pairs, counts):
    zh, y, c, x, zl = (lax.axis_index(a) for a in AXES)
    count = counts[0, 0]
    todo, near = listing(pairs[0, 0], count, (x + 2) % 4)
    meta = jnp.stack([count, zh, y, c, x, zl, x * 4 + zl, zh * 8 + y * 2 + c, near]).astype(jnp.int32)
    *pieces, (meta, todo) = gather(*unit(source, target), (meta, todo))
    row_sums, col_sums, near_tiles, far_tiles = sums(meta, todo, *pieces)
    row_all, col_all = total(row_sums, col_sums)
    row_best, col_best, src_piece, tgt_piece = margins(
        meta, todo, row_all, col_all, near_tiles, far_tiles
    )
    return (
        row_best.reshape(1, 1, SLOTS, BLK),
        col_best.reshape(1, 1, SLOTS, BLK),
        src_piece.reshape(HALF),
        tgt_piece.reshape(HALF),
    )


def solution(mesh):
    fine = Mesh(mesh.devices.reshape(2, 4, 2, 4, 4), AXES)
    src_axes, tgt_axes = AXES, GROUP + BANK
    return jax.shard_map(
        per_device,
        mesh=fine,
        in_specs=(
            P(src_axes, None),
            P(tgt_axes, None),
            P(BANK, GROUP, None, None),
            P(BANK, GROUP),
        ),
        out_specs=(
            P(BANK, GROUP, None, None),
            P(BANK, GROUP, None, None),
            P(src_axes),
            P(tgt_axes),
        ),
        check_vma=False,
    )
```

```python
import math

import jax
import jax.numpy as jnp
from jax import lax
from jax.experimental import pallas as pl
from jax.experimental.pallas import tpu as pltpu
from jax.sharding import Mesh
from jax.sharding import PartitionSpec as P

BLK = 256
HALF = 128
SLOTS = 48
BLOCKS = 8
SHARDS = 16
TEMP_INV = 20.0
EXP2_SCALE = TEMP_INV * math.log2(math.e)
HALF_TEMP = 0.5 / TEMP_INV
NT = (((1,), (1,)), ((), ()))
AXES = ("zh", "y", "c", "x", "zl")
BANK = ("zh", "y", "c")
GROUP = ("x", "zl")


def unit_rows(rows):
    values = rows.astype(jnp.float32)
    width = values.shape[-1]
    scale = lax.rsqrt(jnp.mean(values * values, axis=-1, keepdims=True) + 1e-06)
    return (values * (scale * (1.0 / math.sqrt(width)))).astype(jnp.bfloat16)


def ring(n, step):
    return [(i, (i + step) % n) for i in range(n)]


GROUP_TILES = 8

REST = (1, 3, 2)
NEAR_PLACE = {(0, 0, 0): (0, 0, 128), (1, 0, 0): (1, 0, 128), (3, 0, 0): (2, 0, 128)}
for order, dz in enumerate(REST):
    for part, dx in ((3, 0), (4, 1), (5, 3)):
        NEAR_PLACE[(dx, dz, 0)] = (part, 128 * order, 128)
NEAR_PARTS = 6
FAR_PLACE = {
    (2, 0, 0): (0, 0, 128),
    (2, 1, 0): (1, 0, 128),
    (2, 3, 0): (1, 128, 128),
    (2, 2, 0): (2, 0, 128),
}
FAR_PARTS = 3
TGT_PLACE = {}
for order, dy in enumerate((0, 1, 3, 2)):
    TGT_PLACE[(0, dy, 0)] = (0, 128 * order)
    TGT_PLACE[(0, dy, 1)] = (1, 128 * order)
for order, dy in enumerate((0, 2, 1, 3)):
    TGT_PLACE[(1, dy, 0)] = (2 + order, 0)
    TGT_PLACE[(1, dy, 1)] = (6 + order, 0)
TGT_PARTS = 10


def load_source(meta, place, parts, src, of_x):
    for (dx, dz, offset), (part, first, rows) in place.items():
        shard = of_x(dx) * 4 + lax.rem(meta[5] - dz + 4, 4)
        dst = pl.ds(pl.multiple_of(shard * HALF + offset, 64), rows)
        src[dst, :] = parts[part][first : first + rows, :]


def load_target(meta, parts, tgt):
    zh, y, c = meta[1], meta[2], meta[3]
    for (dh, dy, dc), (part, first) in TGT_PLACE.items():
        shard = lax.rem(zh + dh, 2) * 8 + lax.rem(y - dy + 4, 4) * 2 + lax.rem(c + dc, 2)
        dst = pl.ds(pl.multiple_of(shard * HALF, HALF), HALF)
        tgt[dst, :] = parts[part][first : first + HALF, :]


def add_tiles(todo, begin, n, width, src, row_of, tgt, tiles, acc_row, acc_col):
    dead_row = acc_row.shape[0] // BLK - 1

    def group(k, carry):
        for u in range(width):
            live = k * width + u < n
            q = jnp.minimum(k * width + u, n - 1)
            i, j = row_of(todo[3 * (begin + q)]), todo[3 * (begin + q) + 1]
            left = src[pl.ds(pl.multiple_of(i * BLK, BLK), BLK), :]
            right = tgt[pl.ds(pl.multiple_of(j * BLK, BLK), BLK), :]
            scores = lax.dot_general(left, right, NT, preferred_element_type=jnp.float32)
            tiles[q] = scores
            i = jnp.where(live, i, dead_row)
            j = jnp.where(live, j, BLOCKS)
            w = jnp.exp2(scores * EXP2_SCALE)
            rows = pl.ds(pl.multiple_of(i * BLK, BLK), BLK)
            acc_row[rows, :] += w[:, :HALF] + w[:, HALF:]
            acc_col[j] += w.reshape(BLK // 8, 8, BLK).sum(0)
        return carry

    lax.fori_loop(0, (n + width - 1) // width, group, 0)


def row_totals(acc_row, count):
    return jnp.concatenate(
        [
            jnp.sum(acc_row[h * HALF : (h + 1) * HALF, :].T, axis=0, keepdims=True)
            for h in range(count)
        ],
        0,
    )


def near_kernel(meta, todo, *refs):
    parts, refs = refs[: NEAR_PARTS + TGT_PARTS], refs[NEAR_PARTS + TGT_PARTS :]
    row_out, acc_col, tiles, tgt, src, acc_row = refs
    load_source(meta, NEAR_PLACE, parts[:NEAR_PARTS], src, lambda dx: lax.rem(meta[4] - dx + 4, 4))
    load_target(meta, parts[NEAR_PARTS:], tgt)
    acc_row[...] = jnp.zeros_like(acc_row)
    acc_col[...] = jnp.zeros_like(acc_col)
    add_tiles(todo, 0, meta[8], GROUP_TILES, src, lambda i: i, tgt, tiles, acc_row, acc_col)
    row_out[...] = row_totals(acc_row, SHARDS)


def far_kernel(meta, todo, *refs):
    parts, refs = refs[:FAR_PARTS], refs[FAR_PARTS:]
    row_in, col_in, tgt, row_out, col_out, tiles, src, acc_row, acc_col = refs
    load_source(meta, FAR_PLACE, parts, src, lambda dx: 0)
    acc_row[...] = jnp.zeros_like(acc_row)
    acc_col[...] = col_in[...]
    near = meta[8]
    add_tiles(todo, near, meta[0] - near, 4, src, lambda i: lax.rem(i, 2), tgt, tiles, acc_row, acc_col)
    far_rows = row_totals(acc_row, 4)
    rows = row_in[...]
    far_x = lax.rem(meta[4] + 2, 4)
    rows = jnp.concatenate(
        [rows[4 * v : 4 * v + 4] + jnp.where(far_x == v, far_rows, 0.0) for v in range(4)], 0
    )
    row_out[...] = rows
    cols = []
    for j in range(BLOCKS):
        col = jnp.sum(acc_col[j], axis=0, keepdims=True)
        cols += [col[:, :HALF], col[:, HALF:]]
    col_out[...] = jnp.concatenate(cols, 0)


def margin_kernel(meta, todo, r0, r1, r2, r3, c0, c1, c2, c3, near_tiles, far_tiles, row_best, col_best,
                  src_piece, tgt_piece, s16, t16, s_cols, row_slots, col_slots):
    s16[...] = jnp.log((r0[...] + r1[...]) + (r2[...] + r3[...])) * HALF_TEMP
    t16[...] = jnp.log((c0[...] + c1[...]) + (c2[...] + c3[...])) * HALF_TEMP
    row_slots[...] = jnp.zeros_like(row_slots)
    col_slots[...] = jnp.zeros_like(col_slots)
    for h in range(SHARDS):
        s_cols[h * HALF : (h + 1) * HALF, :] = jnp.broadcast_to(
            s16[h : h + 1, :], (HALF, HALF)
        ).T
    src_piece[...] = s16[pl.ds(meta[6], 1), :] * (2 * TEMP_INV)
    tgt_piece[...] = t16[pl.ds(meta[7], 1), :] * (2 * TEMP_INV)

    def best_of(begin, n, width, tiles):
        def group(k, carry):
            for u in range(width):
                q = jnp.minimum(k * width + u, n - 1)
                i, j, p = (todo[3 * (begin + q) + v] for v in range(3))
                ta, tb = t16[pl.ds(2 * j, 1), :], t16[pl.ds(2 * j + 1, 1), :]
                sa, sb = s16[pl.ds(2 * i, 1), :], s16[pl.ds(2 * i + 1, 1), :]
                sc = s_cols[pl.ds(pl.multiple_of(i * BLK, BLK), BLK), :]
                scores = tiles[q]
                ua, ub = scores[:, :HALF], scores[:, HALF:]
                best = jnp.maximum(ua - ta, ub - tb)
                ra = jnp.max(best[:HALF].T, axis=0, keepdims=True)
                rb = jnp.max(best[HALF:].T, axis=0, keepdims=True)
                ca = jnp.max(ua - sc, axis=0, keepdims=True)
                cb = jnp.max(ub - sc, axis=0, keepdims=True)
                row_slots[p] = jnp.concatenate([ra - sa, rb - sb], 1) * TEMP_INV
                col_slots[p] = jnp.concatenate([ca - ta, cb - tb], 1) * TEMP_INV
            return carry

        lax.fori_loop(0, (n + width - 1) // width, group, 0)

    near = meta[8]
    best_of(0, near, GROUP_TILES, near_tiles)
    best_of(near, meta[0] - near, 4, far_tiles)
    for k in range(0, SLOTS, 8):
        row_best[k : k + 8, :] = jnp.concatenate([row_slots[k + v] for v in range(8)], 0)
        col_best[k : k + 8, :] = jnp.concatenate([col_slots[k + v] for v in range(8)], 0)


VMEM = pl.BlockSpec(memory_space=pltpu.VMEM)
SMEM = pl.BlockSpec(memory_space=pltpu.SMEM)


F32 = lambda *shape: jax.ShapeDtypeStruct(shape, jnp.float32)
PARAMS = pltpu.CompilerParams(vmem_limit_bytes=20 * 1024 * 1024)


def pinned(v):
    return pltpu.with_memory_space_constraint(v, pltpu.VMEM)


def unit_kernel(source, target, own_s, own_t, s_rows, t_rows, sems):
    copies = [
        pltpu.make_async_copy(source, s_rows, sems.at[0]),
        pltpu.make_async_copy(target, t_rows, sems.at[1]),
    ]
    for copy in copies:
        copy.start()
    copies[0].wait()
    own_s[...] = unit_rows(s_rows[...])
    copies[1].wait()
    own_t[...] = unit_rows(t_rows[...])


def unit(source, target):
    return pl.pallas_call(
        unit_kernel,
        out_shape=[jax.ShapeDtypeStruct(v.shape, v.dtype) for v in (source, target)],
        in_specs=[pl.BlockSpec(memory_space=pltpu.HBM)] * 2,
        out_specs=[VMEM] * 2,
        scratch_shapes=[pltpu.VMEM(v.shape, v.dtype) for v in (source, target)]
        + [pltpu.SemaphoreType.DMA((2,))],
        compiler_params=PARAMS,
        name="unit",
    )(*(pltpu.with_memory_space_constraint(v, pltpu.HBM) for v in (source, target)))


def sums(meta, todo, near_parts, far_parts, tgt_parts):
    width = tgt_parts[0].shape[1]
    near_store = pltpu.VMEM((SLOTS, BLK, BLK), jnp.float32)
    far_store = pltpu.VMEM((2 * BLOCKS, BLK, BLK), jnp.float32)
    col_store = pltpu.VMEM((BLOCKS + 1, 8, BLK), jnp.float32)
    slab = pltpu.VMEM((BLOCKS * BLK, width), jnp.bfloat16)
    near_rows, near_cols, near_tiles, tgt = pl.pallas_call(
        near_kernel,
        out_shape=(pltpu.VMEM((SHARDS, HALF), jnp.float32), col_store, near_store, slab),
        in_specs=[SMEM, SMEM] + [VMEM] * (NEAR_PARTS + TGT_PARTS),
        out_specs=(VMEM,) * 4,
        scratch_shapes=[slab, pltpu.VMEM(((BLOCKS + 1) * BLK, HALF), jnp.float32)],
        compiler_params=PARAMS,
        cost_estimate=pl.CostEstimate(
            flops=40 * 2 * BLK * BLK * width, bytes_accessed=12 << 20, transcendentals=40 * BLK * BLK
        ),
        name="near_sums",
    )(meta, todo, *near_parts, *tgt_parts)
    row_sums, col_sums, far_tiles = pl.pallas_call(
        far_kernel,
        out_shape=(F32(SHARDS, HALF), F32(SHARDS, HALF), far_store),
        in_specs=[SMEM, SMEM] + [VMEM] * (FAR_PARTS + 3),
        out_specs=(VMEM,) * 3,
        scratch_shapes=[
            pltpu.VMEM((2 * BLK, width), jnp.bfloat16),
            pltpu.VMEM((3 * BLK, HALF), jnp.float32),
            col_store,
        ],
        compiler_params=PARAMS,
        name="far_sums",
    )(meta, todo, *far_parts, pinned(near_rows), pinned(near_cols), pinned(tgt))
    return row_sums, col_sums, near_tiles, far_tiles


def margins(meta, todo, row_all, col_all, near_tiles, far_tiles):
    return pl.pallas_call(
        margin_kernel,
        out_shape=(F32(SLOTS, BLK), F32(SLOTS, BLK), F32(1, HALF), F32(1, HALF)),
        in_specs=[SMEM, SMEM] + [VMEM] * 10,
        out_specs=(VMEM,) * 4,
        scratch_shapes=[
            pltpu.VMEM((SHARDS, HALF), jnp.float32),
            pltpu.VMEM((SHARDS, HALF), jnp.float32),
            pltpu.VMEM((BLOCKS * BLK, HALF), jnp.float32),
            pltpu.VMEM((SLOTS, 1, BLK), jnp.float32),
            pltpu.VMEM((SLOTS, 1, BLK), jnp.float32),
        ],
        compiler_params=PARAMS,
        name="margins",
    )(meta, todo, *row_all, *col_all, pinned(near_tiles), pinned(far_tiles))


def gather(own_s, own_t, todo):
    send = lambda v, axis, step: lax.ppermute(v, axis, ring(lax.axis_size(axis), step))
    after = lambda v, done: lax.optimization_barrier((v, done))
    near = [send(own_s, "zl", k) for k in REST]
    s_own = [send(own_s, "x", k) for k in (1, -1)]
    (t_y, again), s_own = after((own_t, own_s), s_own)
    t_near = [send(t_y, "y", k) for k in (1, -1)]
    (t_zh, again), (t_near, todo) = after((t_y, again), (t_near, todo))
    across = send(t_zh, "zh", 1)
    t_own = [own_t] + t_near + [send(t_zh, "y", 2)]
    s_own.append(send(again, "x", 2))

    near, (todo, across) = after(near, (todo, across))
    rest = jnp.concatenate(near)
    up = send(rest, "x", 1)
    later, s_own = after(rest, s_own)
    down = send(later, "x", -1)
    t_own = jnp.concatenate(t_own)
    t_own_c = send(t_own, "c", 1)
    across, t_own_c = after(across, t_own_c)
    t_across = [across] + [send(across, "y", k) for k in (2, 1, -1)]

    up_far, down_far = send(up[:256], "x", 1), send(down[256:], "x", -1)
    t_across_c = [send(v, "c", 1) for v in t_across]
    t_parts = [t_own, t_own_c] + t_across + t_across_c
    return [own_s, s_own[0], s_own[1], rest, up, down], [s_own[2], up_far, down_far], t_parts, todo


def total(row_sums, col_sums):
    send = lambda v, axis, step: lax.ppermute(v, axis, ring(lax.axis_size(axis), step))
    cols = col_sums + send(col_sums, "c", 1)
    cols = cols + send(cols, "zh", 1)
    rows = [row_sums] + [send(row_sums, "x", k) for k in (2, 1, -1)]
    rows = (rows[0] + rows[1]) + (rows[2] + rows[3])
    return [rows] + [send(rows, "zl", k) for k in (2, 1, -1)], [cols] + [send(cols, "y", k) for k in (2, 1, -1)]


def listing(pairs, count, far_x):
    slot = jnp.arange(pairs.shape[0], dtype=jnp.int32)
    live = slot < count
    near = live & (pairs[:, 0] // 2 != far_x)
    kind = jnp.where(near, 0, jnp.where(live, 1, 2))
    key = kind * SLOTS + slot
    place = jnp.sum(key[None, :] < key[:, None], axis=1, dtype=jnp.int32)
    entry = jnp.concatenate([pairs, slot[:, None]], 1)
    todo = jnp.sum(jnp.where(place[None, :, None] == slot[:, None, None], entry[None], 0), axis=1)
    return todo.reshape(-1).astype(jnp.int32), jnp.sum(near, dtype=jnp.int32)


def per_device(source, target, pairs, counts):
    zh, y, c, x, zl = (lax.axis_index(a) for a in AXES)
    count = counts[0, 0]
    todo, near = listing(pairs[0, 0], count, (x + 2) % 4)
    meta = jnp.stack([count, zh, y, c, x, zl, x * 4 + zl, zh * 8 + y * 2 + c, near]).astype(jnp.int32)
    *pieces, (meta, todo) = gather(*unit(source, target), (meta, todo))
    row_sums, col_sums, near_tiles, far_tiles = sums(meta, todo, *pieces)
    row_all, col_all = total(row_sums, col_sums)
    row_best, col_best, src_piece, tgt_piece = margins(
        meta, todo, row_all, col_all, near_tiles, far_tiles
    )
    return (
        row_best.reshape(1, 1, SLOTS, BLK),
        col_best.reshape(1, 1, SLOTS, BLK),
        src_piece.reshape(HALF),
        tgt_piece.reshape(HALF),
    )


def solution(mesh):
    fine = Mesh(mesh.devices.reshape(2, 4, 2, 4, 4), AXES)
    src_axes, tgt_axes = AXES, GROUP + BANK
    return jax.shard_map(
        per_device,
        mesh=fine,
        in_specs=(
            P(src_axes, None),
            P(tgt_axes, None),
            P(BANK, GROUP, None, None),
            P(BANK, GROUP),
        ),
        out_specs=(
            P(BANK, GROUP, None, None),
            P(BANK, GROUP, None, None),
            P(src_axes),
            P(tgt_axes),
        ),
        check_vma=False,
    )
```

```python
import math

import jax
import jax.numpy as jnp
from jax import lax
from jax.experimental import pallas as pl
from jax.experimental.pallas import tpu as pltpu
from jax.sharding import Mesh
from jax.sharding import PartitionSpec as P

BLK = 256
HALF = 128
SLOTS = 48
BLOCKS = 8
SHARDS = 16
TEMP_INV = 20.0
EXP2_SCALE = TEMP_INV * math.log2(math.e)
HALF_TEMP = 0.5 / TEMP_INV
NT = (((1,), (1,)), ((), ()))
AXES = ("zh", "y", "c", "x", "zl")
BANK = ("zh", "y", "c")
GROUP = ("x", "zl")


def unit_rows(rows):
    values = rows.astype(jnp.float32)
    width = values.shape[-1]
    scale = lax.rsqrt(jnp.mean(values * values, axis=-1, keepdims=True) + 1e-06)
    return (values * (scale * (1.0 / math.sqrt(width)))).astype(jnp.bfloat16)


def ring(n, step):
    return [(i, (i + step) % n) for i in range(n)]


GROUP_TILES = 8

REST = (1, 3, 2)
NEAR_PLACE = {(0, 0, 0): (0, 0, 128), (1, 0, 0): (1, 0, 128), (3, 0, 0): (2, 0, 128)}
for order, dz in enumerate(REST):
    for part, dx in ((3, 0), (4, 1), (5, 3)):
        NEAR_PLACE[(dx, dz, 0)] = (part, 128 * order, 128)
NEAR_PARTS = 6
FAR_PLACE = {
    (2, 0, 0): (0, 0, 128),
    (2, 1, 0): (1, 0, 128),
    (2, 3, 0): (1, 128, 64),
    (2, 3, 64): (2, 0, 64),
    (2, 2, 0): (2, 64, 128),
}
FAR_PARTS = 3
TGT_PLACE = {}
for order, dy in enumerate((0, 1, 3, 2)):
    TGT_PLACE[(0, dy, 0)] = (0, 128 * order)
    TGT_PLACE[(0, dy, 1)] = (1, 128 * order)
for order, dy in enumerate((0, 2, 1, 3)):
    TGT_PLACE[(1, dy, 0)] = (2 + order, 0)
    TGT_PLACE[(1, dy, 1)] = (6 + order, 0)
TGT_PARTS = 10


def load_source(meta, place, parts, src, of_x):
    for (dx, dz, offset), (part, first, rows) in place.items():
        shard = of_x(dx) * 4 + lax.rem(meta[5] - dz + 4, 4)
        dst = pl.ds(pl.multiple_of(shard * HALF + offset, 64), rows)
        src[dst, :] = parts[part][first : first + rows, :]


def load_target(meta, parts, tgt):
    zh, y, c = meta[1], meta[2], meta[3]
    for (dh, dy, dc), (part, first) in TGT_PLACE.items():
        shard = lax.rem(zh + dh, 2) * 8 + lax.rem(y - dy + 4, 4) * 2 + lax.rem(c + dc, 2)
        dst = pl.ds(pl.multiple_of(shard * HALF, HALF), HALF)
        tgt[dst, :] = parts[part][first : first + HALF, :]


def add_tiles(todo, begin, n, width, src, row_of, tgt, tiles, acc_row, acc_col):
    dead_row = acc_row.shape[0] // BLK - 1

    def group(k, carry):
        for u in range(width):
            live = k * width + u < n
            q = jnp.minimum(k * width + u, n - 1)
            i, j = row_of(todo[3 * (begin + q)]), todo[3 * (begin + q) + 1]
            left = src[pl.ds(pl.multiple_of(i * BLK, BLK), BLK), :]
            right = tgt[pl.ds(pl.multiple_of(j * BLK, BLK), BLK), :]
            scores = lax.dot_general(left, right, NT, preferred_element_type=jnp.float32)
            tiles[q] = scores
            i = jnp.where(live, i, dead_row)
            j = jnp.where(live, j, BLOCKS)
            w = jnp.exp2(scores * EXP2_SCALE)
            rows = pl.ds(pl.multiple_of(i * BLK, BLK), BLK)
            acc_row[rows, :] += w[:, :HALF] + w[:, HALF:]
            acc_col[j] += w.reshape(BLK // 8, 8, BLK).sum(0)
        return carry

    lax.fori_loop(0, (n + width - 1) // width, group, 0)


def row_totals(acc_row, count):
    return jnp.concatenate(
        [
            jnp.sum(acc_row[h * HALF : (h + 1) * HALF, :].T, axis=0, keepdims=True)
            for h in range(count)
        ],
        0,
    )


def near_kernel(meta, todo, *refs):
    parts, refs = refs[: NEAR_PARTS + TGT_PARTS], refs[NEAR_PARTS + TGT_PARTS :]
    row_out, acc_col, tiles, tgt, src, acc_row = refs
    load_source(meta, NEAR_PLACE, parts[:NEAR_PARTS], src, lambda dx: lax.rem(meta[4] - dx + 4, 4))
    load_target(meta, parts[NEAR_PARTS:], tgt)
    acc_row[...] = jnp.zeros_like(acc_row)
    acc_col[...] = jnp.zeros_like(acc_col)
    add_tiles(todo, 0, meta[8], GROUP_TILES, src, lambda i: i, tgt, tiles, acc_row, acc_col)
    row_out[...] = row_totals(acc_row, SHARDS)


def far_kernel(meta, todo, *refs):
    parts, refs = refs[:FAR_PARTS], refs[FAR_PARTS:]
    row_in, col_in, tgt, row_out, col_out, tiles, src, acc_row, acc_col = refs
    load_source(meta, FAR_PLACE, parts, src, lambda dx: 0)
    acc_row[...] = jnp.zeros_like(acc_row)
    acc_col[...] = col_in[...]
    near = meta[8]
    add_tiles(todo, near, meta[0] - near, 4, src, lambda i: lax.rem(i, 2), tgt, tiles, acc_row, acc_col)
    far_rows = row_totals(acc_row, 4)
    rows = row_in[...]
    far_x = lax.rem(meta[4] + 2, 4)
    rows = jnp.concatenate(
        [rows[4 * v : 4 * v + 4] + jnp.where(far_x == v, far_rows, 0.0) for v in range(4)], 0
    )
    row_out[...] = rows
    cols = []
    for j in range(BLOCKS):
        col = jnp.sum(acc_col[j], axis=0, keepdims=True)
        cols += [col[:, :HALF], col[:, HALF:]]
    col_out[...] = jnp.concatenate(cols, 0)


def margin_kernel(meta, todo, r0, r1, r2, r3, c0, c1, c2, c3, near_tiles, far_tiles, row_best, col_best,
                  src_piece, tgt_piece, s16, t16, s_cols, row_slots, col_slots):
    s16[...] = jnp.log((r0[...] + r1[...]) + (r2[...] + r3[...])) * HALF_TEMP
    t16[...] = jnp.log((c0[...] + c1[...]) + (c2[...] + c3[...])) * HALF_TEMP
    row_slots[...] = jnp.zeros_like(row_slots)
    col_slots[...] = jnp.zeros_like(col_slots)
    for h in range(SHARDS):
        s_cols[h * HALF : (h + 1) * HALF, :] = jnp.broadcast_to(
            s16[h : h + 1, :], (HALF, HALF)
        ).T
    src_piece[...] = s16[pl.ds(meta[6], 1), :] * (2 * TEMP_INV)
    tgt_piece[...] = t16[pl.ds(meta[7], 1), :] * (2 * TEMP_INV)

    def best_of(begin, n, width, tiles):
        def group(k, carry):
            for u in range(width):
                q = jnp.minimum(k * width + u, n - 1)
                i, j, p = (todo[3 * (begin + q) + v] for v in range(3))
                ta, tb = t16[pl.ds(2 * j, 1), :], t16[pl.ds(2 * j + 1, 1), :]
                sa, sb = s16[pl.ds(2 * i, 1), :], s16[pl.ds(2 * i + 1, 1), :]
                sc = s_cols[pl.ds(pl.multiple_of(i * BLK, BLK), BLK), :]
                scores = tiles[q]
                ua, ub = scores[:, :HALF], scores[:, HALF:]
                best = jnp.maximum(ua - ta, ub - tb)
                ra = jnp.max(best[:HALF].T, axis=0, keepdims=True)
                rb = jnp.max(best[HALF:].T, axis=0, keepdims=True)
                ca = jnp.max(ua - sc, axis=0, keepdims=True)
                cb = jnp.max(ub - sc, axis=0, keepdims=True)
                row_slots[p] = jnp.concatenate([ra - sa, rb - sb], 1) * TEMP_INV
                col_slots[p] = jnp.concatenate([ca - ta, cb - tb], 1) * TEMP_INV
            return carry

        lax.fori_loop(0, (n + width - 1) // width, group, 0)

    near = meta[8]
    best_of(0, near, GROUP_TILES, near_tiles)
    best_of(near, meta[0] - near, 4, far_tiles)
    for k in range(0, SLOTS, 8):
        row_best[k : k + 8, :] = jnp.concatenate([row_slots[k + v] for v in range(8)], 0)
        col_best[k : k + 8, :] = jnp.concatenate([col_slots[k + v] for v in range(8)], 0)


VMEM = pl.BlockSpec(memory_space=pltpu.VMEM)
SMEM = pl.BlockSpec(memory_space=pltpu.SMEM)


F32 = lambda *shape: jax.ShapeDtypeStruct(shape, jnp.float32)
PARAMS = pltpu.CompilerParams(vmem_limit_bytes=20 * 1024 * 1024)


def pinned(v):
    return pltpu.with_memory_space_constraint(v, pltpu.VMEM)


def unit_kernel(source, target, own_s, own_t, s_rows, t_rows, sems):
    copies = [
        pltpu.make_async_copy(source, s_rows, sems.at[0]),
        pltpu.make_async_copy(target, t_rows, sems.at[1]),
    ]
    for copy in copies:
        copy.start()
    copies[0].wait()
    own_s[...] = unit_rows(s_rows[...])
    copies[1].wait()
    own_t[...] = unit_rows(t_rows[...])


def unit(source, target):
    return pl.pallas_call(
        unit_kernel,
        out_shape=[jax.ShapeDtypeStruct(v.shape, v.dtype) for v in (source, target)],
        in_specs=[pl.BlockSpec(memory_space=pltpu.HBM)] * 2,
        out_specs=[VMEM] * 2,
        scratch_shapes=[pltpu.VMEM(v.shape, v.dtype) for v in (source, target)]
        + [pltpu.SemaphoreType.DMA((2,))],
        compiler_params=PARAMS,
        name="unit",
    )(*(pltpu.with_memory_space_constraint(v, pltpu.HBM) for v in (source, target)))


def sums(meta, todo, near_parts, far_parts, tgt_parts):
    width = tgt_parts[0].shape[1]
    near_store = pltpu.VMEM((SLOTS, BLK, BLK), jnp.float32)
    far_store = pltpu.VMEM((2 * BLOCKS, BLK, BLK), jnp.float32)
    col_store = pltpu.VMEM((BLOCKS + 1, 8, BLK), jnp.float32)
    slab = pltpu.VMEM((BLOCKS * BLK, width), jnp.bfloat16)
    near_rows, near_cols, near_tiles, tgt = pl.pallas_call(
        near_kernel,
        out_shape=(pltpu.VMEM((SHARDS, HALF), jnp.float32), col_store, near_store, slab),
        in_specs=[SMEM, SMEM] + [VMEM] * (NEAR_PARTS + TGT_PARTS),
        out_specs=(VMEM,) * 4,
        scratch_shapes=[slab, pltpu.VMEM(((BLOCKS + 1) * BLK, HALF), jnp.float32)],
        compiler_params=PARAMS,
        cost_estimate=pl.CostEstimate(
            flops=40 * 2 * BLK * BLK * width, bytes_accessed=12 << 20, transcendentals=40 * BLK * BLK
        ),
        name="near_sums",
    )(meta, todo, *near_parts, *tgt_parts)
    row_sums, col_sums, far_tiles = pl.pallas_call(
        far_kernel,
        out_shape=(F32(SHARDS, HALF), F32(SHARDS, HALF), far_store),
        in_specs=[SMEM, SMEM] + [VMEM] * (FAR_PARTS + 3),
        out_specs=(VMEM,) * 3,
        scratch_shapes=[
            pltpu.VMEM((2 * BLK, width), jnp.bfloat16),
            pltpu.VMEM((3 * BLK, HALF), jnp.float32),
            col_store,
        ],
        compiler_params=PARAMS,
        name="far_sums",
    )(meta, todo, *far_parts, pinned(near_rows), pinned(near_cols), pinned(tgt))
    return row_sums, col_sums, near_tiles, far_tiles


def margins(meta, todo, row_all, col_all, near_tiles, far_tiles):
    return pl.pallas_call(
        margin_kernel,
        out_shape=(F32(SLOTS, BLK), F32(SLOTS, BLK), F32(1, HALF), F32(1, HALF)),
        in_specs=[SMEM, SMEM] + [VMEM] * 10,
        out_specs=(VMEM,) * 4,
        scratch_shapes=[
            pltpu.VMEM((SHARDS, HALF), jnp.float32),
            pltpu.VMEM((SHARDS, HALF), jnp.float32),
            pltpu.VMEM((BLOCKS * BLK, HALF), jnp.float32),
            pltpu.VMEM((SLOTS, 1, BLK), jnp.float32),
            pltpu.VMEM((SLOTS, 1, BLK), jnp.float32),
        ],
        compiler_params=PARAMS,
        name="margins",
    )(meta, todo, *row_all, *col_all, pinned(near_tiles), pinned(far_tiles))


def gather(own_s, own_t, todo):
    send = lambda v, axis, step: lax.ppermute(v, axis, ring(lax.axis_size(axis), step))
    after = lambda v, done: lax.optimization_barrier((v, done))
    near = [send(own_s, "zl", k) for k in REST]
    s_own = [send(own_s, "x", k) for k in (1, -1)]
    (t_y, again), s_own = after((own_t, own_s), s_own)
    t_near = [send(t_y, "y", k) for k in (1, -1)]
    (t_zh, again), (t_near, todo) = after((t_y, again), (t_near, todo))
    across = send(t_zh, "zh", 1)
    t_own = [own_t] + t_near + [send(t_zh, "y", 2)]
    s_own.append(send(again, "x", 2))

    near, (todo, across, s_own) = after(near, (todo, across, s_own))
    rest = jnp.concatenate(near)
    up, down = send(rest, "x", 1), send(rest, "x", -1)
    t_own = jnp.concatenate(t_own)
    t_own_c = send(t_own, "c", 1)
    across, t_own_c = after(across, t_own_c)
    t_across = [across] + [send(across, "y", k) for k in (2, 1, -1)]

    t_across, (up_half, down_half) = after(t_across, (up[:192], down[192:]))
    up_far, down_far = send(up_half, "x", 1), send(down_half, "x", -1)
    t_across_c = [send(v, "c", 1) for v in t_across]
    t_parts = [t_own, t_own_c] + t_across + t_across_c
    return [own_s, s_own[0], s_own[1], rest, up, down], [s_own[2], up_far, down_far], t_parts, todo


def total(row_sums, col_sums):
    send = lambda v, axis, step: lax.ppermute(v, axis, ring(lax.axis_size(axis), step))
    cols = col_sums + send(col_sums, "c", 1)
    cols = cols + send(cols, "zh", 1)
    rows = [row_sums] + [send(row_sums, "x", k) for k in (2, 1, -1)]
    rows = (rows[0] + rows[1]) + (rows[2] + rows[3])
    return [rows] + [send(rows, "zl", k) for k in (2, 1, -1)], [cols] + [send(cols, "y", k) for k in (2, 1, -1)]


def listing(pairs, count, far_x):
    slot = jnp.arange(pairs.shape[0], dtype=jnp.int32)
    live = slot < count
    near = live & (pairs[:, 0] // 2 != far_x)
    kind = jnp.where(near, 0, jnp.where(live, 1, 2))
    key = kind * SLOTS + slot
    place = jnp.sum(key[None, :] < key[:, None], axis=1, dtype=jnp.int32)
    entry = jnp.concatenate([pairs, slot[:, None]], 1)
    todo = jnp.sum(jnp.where(place[None, :, None] == slot[:, None, None], entry[None], 0), axis=1)
    return todo.reshape(-1).astype(jnp.int32), jnp.sum(near, dtype=jnp.int32)


def per_device(source, target, pairs, counts):
    zh, y, c, x, zl = (lax.axis_index(a) for a in AXES)
    count = counts[0, 0]
    todo, near = listing(pairs[0, 0], count, (x + 2) % 4)
    meta = jnp.stack([count, zh, y, c, x, zl, x * 4 + zl, zh * 8 + y * 2 + c, near]).astype(jnp.int32)
    *pieces, (meta, todo) = gather(*unit(source, target), (meta, todo))
    row_sums, col_sums, near_tiles, far_tiles = sums(meta, todo, *pieces)
    row_all, col_all = total(row_sums, col_sums)
    row_best, col_best, src_piece, tgt_piece = margins(
        meta, todo, row_all, col_all, near_tiles, far_tiles
    )
    return (
        row_best.reshape(1, 1, SLOTS, BLK),
        col_best.reshape(1, 1, SLOTS, BLK),
        src_piece.reshape(HALF),
        tgt_piece.reshape(HALF),
    )


def solution(mesh):
    fine = Mesh(mesh.devices.reshape(2, 4, 2, 4, 4), AXES)
    src_axes, tgt_axes = AXES, GROUP + BANK
    return jax.shard_map(
        per_device,
        mesh=fine,
        in_specs=(
            P(src_axes, None),
            P(tgt_axes, None),
            P(BANK, GROUP, None, None),
            P(BANK, GROUP),
        ),
        out_specs=(
            P(BANK, GROUP, None, None),
            P(BANK, GROUP, None, None),
            P(src_axes),
            P(tgt_axes),
        ),
        check_vma=False,
    )
```
